32 devices in a mesh: board: 16 (over z, y, core), seq: 2 (over x).
Axes of the slice: x: 2, y: 2, z: 4, core: 2. Of those that a mesh axis runs over, the one named last changes fastest.
Arguments:
- board_cards: int32 [16, 6, 5], P('board'), may hold values from 0 to 51, as said below
- hand_ranks: int32 [16, 6, 1326], P('board'), may hold values from 0 to 7461
- river_count: int32 [16], P('board'), may hold values from 1 to 6, as said below
- reach_in: bfloat16 [16, 24, 1326], P('board', 'seq'), may hold values from 0 to 1
- strategy: bfloat16 [16, 6, 96, 1326], P('board', None, 'seq'), may hold values from 0.049804688 to 1
- parent_node: int32 [96], P('seq'), may hold values from 0 to 23, as said below
- pot_size: float32 [96], P('seq'), may hold values from 0.5 to 4
- flop_weight: float32 [16], P('board'), may hold values from 0.1 to 10
Outputs:
- turn_value: float32 [16, 24, 1326], P('board', 'seq')
- root_value: float32 [24, 1326], P('seq')
The draws below stay inside these ranges and needn't reach their ends.
Inputs may be any that keep to these rules, and one draw needn't show every extreme that they name: `board_cards`: the five cards of a river board are distinct; the first three are the flop group's and the same on all of its river boards. `river_count`: some flop group has 6 live river boards; slots at or past the count hold unused data. `parent_node`: each river root is the parent of exactly 4 leaves.
All inputs are finite; a program needn't handle non-finite values.
Results may differ from the reference program's by a relative error of at most 0.0003.
Values may be sent and summed in bfloat16 or wider, within the bound.
No kernel may reach another device: no remote copies, remote signals or barrier semaphores. Data moves between devices by JAX's collectives and lax.ppermute only.
A program may use at most 64 MiB of HBM per device.

```python
import math
import jax
import jax.numpy as jnp
import numpy as np
from jax import lax

DECK = 52
HANDS = 1326
RIVERS = 6
NODES = 24
LEAVES = 96
BOARDS = 16


def draw_board_cards(key, part):

    def flop_group(group_key):
        key_flop, key_river = jax.random.split(group_key)
        shuffled = jax.random.permutation(key_flop, DECK)
        flop_cards = shuffled[:3]
        remaining = shuffled[3:]

        def one_river(river_key):
            chosen = jax.random.permutation(river_key, DECK - 3)[:2]
            return jnp.concatenate([flop_cards, remaining[chosen]])
        return jax.vmap(one_river)(jax.random.split(key_river, RIVERS))
    return jax.vmap(flop_group)(jax.random.split(key, BOARDS)).astype(jnp.int32)


def draw_river_count(key, part):
    key_one, key_two, key_top = jax.random.split(jax.random.fold_in(key, 17), 3)
    factor_one = jax.random.randint(key_one, (BOARDS,), 0, RIVERS)
    factor_two = jax.random.randint(key_two, (BOARDS,), 0, RIVERS)
    counted = 1 + factor_one * factor_two // (RIVERS - 1)
    busiest = jax.random.randint(key_top, (), 0, BOARDS)
    counted = jnp.where(jnp.arange(BOARDS) == busiest, RIVERS, counted)
    return counted.astype(jnp.int32)


def draw_parent_node(key, part):
    shuffled = jax.random.permutation(jax.random.fold_in(key, 29), LEAVES)
    return (shuffled % NODES).astype(jnp.int32)


def touch_ends(drawn, key, low, largest):
    longest = drawn.shape.index(max(drawn.shape))
    spots = []
    for shift in (0, 1):
        where = [jax.random.randint(jax.random.fold_in(key, axis), (), 0, length) for axis, length in enumerate(drawn.shape)]
        where[longest] = (where[longest] + shift) % drawn.shape[longest]
        spots.append(tuple(where))
    return drawn.at[spots[0]].set(low).at[spots[1]].set(largest)


def levels(stream_key, dims, shards, low, top_value):
    def one(axis_at, parts):
        heights = jax.random.uniform(jax.random.fold_in(jax.random.fold_in(stream_key, 6), axis_at), (parts,), jnp.float32, low / len(shards), top_value / len(shards))
        return jnp.repeat(jnp.exp(heights), dims[axis_at] // parts).reshape((-1,) + (1,) * (len(dims) - axis_at - 1))

    loudness = one(*shards[0])
    for cut in shards[1:]:
        loudness = loudness * one(*cut)
    return loudness


def setup_inputs(seed: int = 0) -> dict:
    streams_of = jax.random.split(jax.random.key(seed), 9)
    return {
        "board_cards": draw_board_cards(jax.random.fold_in(streams_of[8], 71), 0),
        "hand_ranks": touch_ends(jax.random.randint(streams_of[1], (BOARDS, RIVERS, HANDS), 0, 7462), jax.random.fold_in(streams_of[1], 1), 0, 7461).astype(jnp.int32),
        "river_count": draw_river_count(jax.random.fold_in(streams_of[8], 71), 0),
        "reach_in": jnp.clip(1.0 * jax.random.uniform(streams_of[3], (BOARDS, NODES, HANDS), jnp.float32) ** levels(streams_of[3], (BOARDS, NODES, HANDS), ((0, 16), (1, 2)), -0.2, 0.2), 0.0, 1.0).astype(jnp.bfloat16),
        "strategy": jnp.clip(0.049804688 + 0.9501953 * jax.random.uniform(streams_of[4], (BOARDS, RIVERS, LEAVES, HANDS), jnp.float32) ** levels(streams_of[4], (BOARDS, RIVERS, LEAVES, HANDS), ((0, 16), (2, 2)), -0.2, 0.2), 0.049804688, 1.0).astype(jnp.bfloat16),
        "parent_node": draw_parent_node(jax.random.fold_in(streams_of[8], 71), 0),
        "pot_size": jnp.clip(jnp.exp(math.log(4.0) - 2.0794415 * jax.random.uniform(streams_of[6], (LEAVES,), jnp.float32) ** levels(streams_of[6], (LEAVES,), ((0, 2),), -0.2, 0.2)), 0.5, 4.0),
        "flop_weight": jnp.clip(jnp.exp(math.log(10.0) - 4.6051702 * jax.random.uniform(streams_of[7], (BOARDS,), jnp.float32) ** levels(streams_of[7], (BOARDS,), ((0, 16),), -0.2, 0.2)), 0.1, 10.0),
    }


lowest = -1.0e9


def hand_tables():
    card_low, card_high = np.triu_indices(DECK, 1)
    return jnp.asarray(card_low, jnp.int32), jnp.asarray(card_high, jnp.int32)


def unblocked_mask(board_row, card_low, card_high):
    card_hit = (card_low[:, None] == board_row[None, :]) | (card_high[:, None] == board_row[None, :])
    return jnp.where(jnp.any(card_hit, axis=1), 0.0, 1.0).astype(jnp.float32)


def reference(board_cards, hand_ranks, river_count, reach_in, strategy, parent_node, pot_size, flop_weight):
    card_low, card_high = hand_tables()
    shared_card = ((card_low[:, None] == card_low[None, :]) | (card_low[:, None] == card_high[None, :])
                   | (card_high[:, None] == card_low[None, :]) | (card_high[:, None] == card_high[None, :]))
    member = parent_node[:, None] == jnp.arange(NODES, dtype=jnp.int32)[None, :]

    def river_board(board_row, ranking, strat_rows, reach_rows):
        hand_live = unblocked_mask(board_row, card_low, card_high)
        lookup = reach_rows[parent_node].astype(jnp.float32)
        leaf_reach = (lookup * strat_rows.astype(jnp.float32) * hand_live[None, :]).astype(jnp.bfloat16)
        payoff = jnp.where(shared_card, 0, jnp.sign(ranking[:, None] - ranking[None, :])).astype(jnp.bfloat16)
        showdown = jnp.dot(leaf_reach, payoff.T, preferred_element_type=jnp.float32)
        leaf_value = pot_size[:, None] * showdown * hand_live[None, :] / HANDS

        def one_node(column):
            return jnp.max(jnp.where(column[:, None], leaf_value, lowest), axis=0)

        return lax.map(one_node, member.T)

    def flop_group(operands):
        board_rows, rank_rows, strat_all, reach_rows, live_count = operands

        def one_river(inner):
            river_index, board_row, ranking, strat_rows = inner
            return lax.cond(river_index < live_count,
                            lambda: river_board(board_row, ranking, strat_rows, reach_rows),
                            lambda: jnp.zeros((NODES, HANDS), jnp.float32))

        values = lax.map(one_river, (jnp.arange(RIVERS, dtype=jnp.int32), board_rows, rank_rows, strat_all))
        river_live = jnp.arange(RIVERS, dtype=jnp.int32) < live_count
        summed = jnp.sum(jnp.where(river_live[:, None, None], values, 0.0), axis=0)
        return summed / live_count.astype(jnp.float32)

    turn_value = lax.map(flop_group, (board_cards, hand_ranks, strategy, reach_in, river_count))
    root_value = jnp.sum(flop_weight[:, None, None] * turn_value / BOARDS, axis=0)
    return turn_value, root_value
```

```python
import functools

import jax
import jax.numpy as jnp
import numpy as np
from jax import lax
from jax.experimental import pallas as pl
from jax.experimental.pallas import tpu as pltpu
from jax.sharding import PartitionSpec as P

DECK = 52
LANES = 128


def round_up(value, step):
    return -(-value // step) * step


def hand_constants(hands, padded):
    low, high = np.triu_indices(DECK, 1)
    cards = np.full((2, padded), -1, np.int32)
    cards[0, :hands], cards[1, :hands] = low, high
    shared = (
        (low[:, None] == low[None, :])
        | (low[:, None] == high[None, :])
        | (high[:, None] == low[None, :])
        | (high[:, None] == high[None, :])
    )
    apart = np.zeros((padded, padded), np.float32)
    apart[:hands, :hands] = ~shared
    return cards, apart


def river_kernel(
    blocks,
    nodes,
    info_ref,
    board_ref,
    rank_ref,
    pick_ref,
    pot_ref,
    cards_ref,
    apart_ref,
    *refs,
):
    strat_refs, reach_refs, (prev_ref, out_ref, rank_row, reach_all) = (
        refs[:blocks],
        refs[blocks : 2 * blocks],
        refs[2 * blocks :],
    )
    hands = rank_ref.shape[-1]
    padded = apart_ref.shape[-1]
    leaves = pick_ref.shape[0]
    river, live_count = info_ref[0], info_ref[1]

    @pl.when(river >= live_count)
    def _():
        out_ref[...] = prev_ref[...]

    @pl.when(river < live_count)
    def _():
        live = jnp.ones((1, padded), jnp.float32)
        for slot in range(board_ref.shape[-1]):
            card = board_ref[river, slot]
            hit = (cards_ref[0:1, :] == card) | (cards_ref[1:2, :] == card)
            live = jnp.where(hit, 0.0, live)

        rank_row[...] = jnp.zeros_like(rank_row)
        rank_row[:, :hands] = rank_ref[0, pl.ds(river, 1), :].astype(jnp.float32)

        strat = jnp.concatenate([ref[...].reshape(ref.shape[-2:]) for ref in strat_refs], axis=0)
        sorted_strat = jnp.dot(pick_ref[...], strat, preferred_element_type=jnp.float32)
        reach = jnp.concatenate(
            [ref[...].reshape(ref.shape[-2:]).astype(jnp.float32) for ref in reach_refs], axis=0
        )
        lookup = jnp.concatenate([reach] * (leaves // nodes), axis=0)
        reach_all[...] = jnp.zeros_like(reach_all)
        reach_all[:, :hands] = (lookup * sorted_strat * live[:, :hands]).astype(jnp.bfloat16)

        ranks = rank_row[...]
        scale = 1.0 / (hands * live_count.astype(jnp.float32))
        for start in range(0, padded, LANES):
            here = rank_row[:, start : start + LANES]
            column = jnp.broadcast_to(here, (LANES, LANES)).T
            apart = apart_ref[start : start + LANES, :]
            pieces = []
            for at in range(0, padded, LANES):
                gap = (column - ranks[:, at : at + LANES]).astype(jnp.bfloat16)
                mask = apart[:, at : at + LANES]
                pieces.append(jnp.maximum(jnp.minimum(gap, mask), -mask))
            payoff = jnp.concatenate(pieces, axis=1)
            shown = lax.dot_general(
                payoff,
                reach_all[...],
                (((1,), (1,)), ((), ())),
                preferred_element_type=jnp.float32,
            )
            value = shown.T * pot_ref[...]
            best = value[:nodes]
            for at in range(nodes, leaves, nodes):
                best = jnp.maximum(best, value[at : at + nodes])
            width = min(LANES, hands - start)
            gain = best * (live[:, start : start + LANES] * scale)
            out_ref[:, start : start + width] = (
                prev_ref[:, start : start + width] + gain[:, :width]
            )


def body(
    board_cards, hand_ranks, river_count, reach_in, strategy, parent_node, pot_size, flop_weight
):
    seq_count = lax.axis_size("seq")
    board_count = lax.axis_size("board")
    seq_here = lax.axis_index("seq")
    rivers, local_leaves, hands = strategy.shape[1:]
    local_nodes = reach_in.shape[1]
    nodes, leaves = local_nodes * seq_count, local_leaves * seq_count
    rounds = -(-rivers // seq_count)
    padded = round_up(hands, LANES)
    cards, apart = hand_constants(hands, padded)

    def shift(array, step):
        return lax.ppermute(
            array, "seq", [(at, (at + step) % seq_count) for at in range(seq_count)]
        )

    labels = jnp.stack([parent_node.astype(jnp.float32), pot_size])
    label_blocks = [labels] + [shift(labels, step) for step in range(1, seq_count)]
    reach_blocks = [reach_in[0]] + [shift(reach_in[0], step) for step in range(1, seq_count)]

    def strategy_of(round_index, step):
        target = jnp.minimum(round_index * seq_count + (seq_here + step) % seq_count, rivers - 1)
        return lax.dynamic_index_in_dim(strategy[0], target, 0, keepdims=False)

    strategy_blocks = [
        [strategy_of(at, 0)]
        + [shift(strategy_of(at, step), step) for step in range(1, seq_count)]
        for at in range(rounds)
    ]

    labels_all = jnp.concatenate(label_blocks, axis=1)
    parent = labels_all[0].astype(jnp.int32)
    place = (seq_here - parent // local_nodes) % seq_count * local_nodes + parent % local_nodes
    earlier = np.tril(np.ones((leaves, leaves), bool), -1)
    nth = jnp.sum((place[:, None] == place[None, :]) & earlier, axis=1)
    slot = nth * nodes + place
    pick = slot[None, :] == jnp.arange(leaves)[:, None]
    pot = jnp.sum(jnp.where(pick, labels_all[1][None, :], 0.0), axis=1, keepdims=True)

    total = jnp.zeros((nodes, hands), jnp.float32)
    smem = pl.BlockSpec(memory_space=pltpu.SMEM)
    vmem = pl.BlockSpec(memory_space=pltpu.VMEM)
    for at in range(rounds):
        river = at * seq_count + seq_here
        info = jnp.stack([river, river_count[0]]).astype(jnp.int32)
        total = pl.pallas_call(
            functools.partial(river_kernel, seq_count, nodes),
            out_shape=jax.ShapeDtypeStruct((nodes, hands), jnp.float32),
            in_specs=[smem, smem] + [vmem] * (5 + 2 * seq_count + 1),
            out_specs=vmem,
            scratch_shapes=[
                pltpu.VMEM((1, padded), jnp.float32),
                pltpu.VMEM((leaves, padded), jnp.bfloat16),
            ],
            compiler_params=pltpu.CompilerParams(vmem_limit_bytes=32 * 1024 * 1024),
        )(
            info,
            board_cards[0],
            hand_ranks,
            pick.astype(jnp.bfloat16),
            pot,
            jnp.asarray(cards),
            jnp.asarray(apart, jnp.bfloat16),
            *strategy_blocks[at],
            *reach_blocks,
            total,
        )

    turn_share = total[:local_nodes]
    for step in range(1, seq_count):
        turn_share = turn_share + shift(total[step * local_nodes : (step + 1) * local_nodes], -step)

    root = flop_weight[0] * turn_share / board_count
    step = 1
    while step < board_count:
        root = root + lax.ppermute(
            root, "board", [(at, at ^ step) for at in range(board_count)]
        )
        step *= 2
    return (turn_share[None], root)


def solution(mesh):
    return jax.shard_map(
        body,
        mesh=mesh,
        in_specs=(
            P("board", None, None),
            P("board", None, None),
            P("board"),
            P("board", "seq", None),
            P("board", None, "seq", None),
            P("seq"),
            P("seq"),
            P("board"),
        ),
        out_specs=(P("board", "seq", None), P("seq", None)),
        check_vma=False,
    )
```

```python
import functools

import jax
import jax.numpy as jnp
import numpy as np
from jax import lax
from jax.experimental import pallas as pl
from jax.experimental.pallas import tpu as pltpu
from jax.sharding import PartitionSpec as P

DECK = 52
LANES = 128


def round_up(value, step):
    return -(-value // step) * step


def hand_constants(hands, padded):
    low, high = np.triu_indices(DECK, 1)
    cards = np.full((2, padded), -1, np.int32)
    cards[0, :hands], cards[1, :hands] = low, high
    shared = (
        (low[:, None] == low[None, :])
        | (low[:, None] == high[None, :])
        | (high[:, None] == low[None, :])
        | (high[:, None] == high[None, :])
    )
    apart = np.zeros((padded, padded), np.float32)
    apart[:hands, :hands] = ~shared
    return cards, apart


def copy_all(pairs, sems):
    copies = [
        pltpu.make_async_copy(source, target, sems.at[at])
        for at, (source, target) in enumerate(pairs)
    ]
    for copy in copies:
        copy.start()
    return copies


def pack_kernel(
    rounds,
    seq_count,
    strat_ref,
    reach_ref,
    parent_ref,
    pot_ref,
    *refs,
):
    outs = refs[: seq_count - 1]
    reach_tmp, parent_tmp, pot_tmp, sems = refs[seq_count - 1 :]
    rivers, leaves, hands = strat_ref.shape[1:]
    here = lax.axis_index("seq")
    pairs = [(reach_ref, reach_tmp), (parent_ref, parent_tmp), (pot_ref, pot_tmp)]
    for step in range(1, seq_count):
        owner = lax.rem(here + step, seq_count)
        for at in range(rounds):
            river = jnp.minimum(at * seq_count + owner, rivers - 1)
            pairs.append((strat_ref.at[0, river], outs[step - 1].at[pl.ds(at * leaves, leaves)]))
    copies = copy_all(pairs, sems)
    for copy in copies[:3]:
        copy.wait()
    pot = pot_tmp[...]
    high = pot.astype(jnp.bfloat16).astype(jnp.float32)
    middle = (pot - high).astype(jnp.bfloat16).astype(jnp.float32)
    low = pot - high - middle
    labels = jnp.concatenate([parent_tmp[...].astype(jnp.float32), high, middle, low], axis=0)
    extra = outs[0].shape[0] - rounds * leaves
    nodes = reach_tmp.shape[1]
    for out in outs:
        rows = [reach_tmp[0].astype(jnp.float32)]
        wide = jnp.concatenate([labels, jnp.zeros((4, hands - leaves), jnp.float32)], axis=1)
        rows.append(wide)
        if extra > nodes + 4:
            rows.append(jnp.zeros((extra - nodes - 4, hands), jnp.float32))
        out[rounds * leaves :, :] = jnp.concatenate(rows, axis=0).astype(jnp.bfloat16)
    for copy in copies[3:]:
        copy.wait()


def build_kernel(
    rounds,
    seq_count,
    rank_ref,
    board_ref,
    count_ref,
    cards_ref,
    apart_ref,
    strat_ref,
    payoff_ref,
    own_ref,
    live_ref,
    rank_tmp,
    rank_row,
    board_tmp,
    count_tmp,
    cards_tmp,
    apart_tmp,
    sems,
    apart_sems,
):
    rivers, leaves, hands = strat_ref.shape[1:]
    padded = apart_ref.shape[-1]
    here = lax.axis_index("seq")
    pairs = [
        (count_ref, count_tmp),
        (rank_ref, rank_tmp),
        (board_ref, board_tmp),
        (cards_ref, cards_tmp),
    ]
    for at in range(rounds):
        river = jnp.minimum(at * seq_count + here, rivers - 1)
        pairs.append((strat_ref.at[0, river], own_ref.at[pl.ds(at * leaves, leaves)]))
    copies = copy_all(pairs, sems)
    masks = copy_all(
        [
            (apart_ref.at[pl.ds(start, LANES)], apart_tmp.at[pl.ds(start, LANES)])
            for start in range(0, padded, LANES)
        ],
        apart_sems,
    )
    for copy in copies[:4]:
        copy.wait()
    live_count = count_tmp[0]

    rank_row[...] = jnp.zeros_like(rank_row)
    live_ref[...] = jnp.zeros_like(live_ref)
    for at in range(rounds):
        river = jnp.minimum(at * seq_count + here, rivers - 1)
        rank_row[at, :, :hands] = rank_tmp[river].astype(jnp.float32)
        live = jnp.where(at * seq_count + here < live_count, 1.0, 0.0)
        live = jnp.full((1, padded), live, jnp.float32)
        for slot in range(board_tmp.shape[0]):
            card = board_tmp[slot, 0, river]
            hit = (cards_tmp[0:1, :] == card) | (cards_tmp[1:2, :] == card)
            live = jnp.where(hit, 0.0, live)
        live_ref[at : at + 1, :] = live
    scale = 1.0 / (hands * jnp.full((1, padded), live_count.astype(jnp.float32)))
    live_ref[rounds : rounds + 1, :] = scale
    live_rounds = (live_count - here + seq_count - 1) // seq_count
    live_ref[rounds + 1 : rounds + 2, :] = jnp.full(
        (1, padded), live_rounds.astype(jnp.float32)
    )

    for start, mask_copy in zip(range(0, padded, LANES), masks):
        mask_copy.wait()

        def one_river(at, _):
            column = jnp.broadcast_to(rank_row[at, :, start : start + LANES], (LANES, LANES)).T
            for lane in range(0, padded, LANES):
                gap = (rank_row[at, :, lane : lane + LANES] - column).astype(jnp.bfloat16)
                mask = apart_tmp[start : start + LANES, lane : lane + LANES]
                payoff_ref[at, start : start + LANES, lane : lane + LANES] = jnp.maximum(
                    jnp.minimum(gap, mask), -mask
                )
            return 0

        lax.fori_loop(0, live_rounds, one_river, 0)
    for copy in copies[4:]:
        copy.wait()


def value_kernel(rounds, seq_count, nodes, leaves, *refs):
    payoff_ref, own_ref, live_ref, sent_ref = refs[:4]
    came = refs[4 : 4 + seq_count - 1]
    out_ref, reach_all = refs[4 + seq_count - 1 :]
    hands = own_ref.shape[-1]
    padded = payoff_ref.shape[-1]
    local_leaves, local_nodes = leaves // seq_count, nodes // seq_count
    here = lax.axis_index("seq")
    packs = (sent_ref,) + tuple(came)
    base = rounds * local_leaves

    reach, places, pots = [], [], []
    for pack in packs:
        small = pack[base:, :].astype(jnp.float32)
        reach.append(small[:local_nodes])
        labels = small[local_nodes : local_nodes + 4, :LANES]
        parent = labels[0:1]
        place = parent
        for owner in range(seq_count):
            inside = (parent >= owner * local_nodes) & (parent < (owner + 1) * local_nodes)
            move = (lax.rem(here - owner + seq_count, seq_count) - owner) * local_nodes
            place = jnp.where(inside, parent + move.astype(jnp.float32), place)
        lane = lax.broadcasted_iota(jnp.int32, (1, LANES), 1)
        places.append(jnp.where(lane < local_leaves, place, -1.0))
        pots.append(labels[1:2] + labels[2:3] + labels[3:4])

    sub = lax.broadcasted_iota(jnp.int32, (LANES, LANES), 0)
    lane = lax.broadcasted_iota(jnp.int32, (LANES, LANES), 1)
    columns = [jnp.broadcast_to(place, (LANES, LANES)).T for place in places]
    picks = []
    pot_sorted = jnp.zeros((leaves, 1), jnp.float32)
    target = lax.broadcasted_iota(jnp.int32, (leaves, LANES), 0).astype(jnp.float32)
    for at in range(seq_count):
        nth = jnp.sum(
            jnp.where((columns[at] == places[at]) & (sub < lane), 1.0, 0.0), axis=0, keepdims=True
        )
        for before in range(at):
            nth = nth + jnp.sum(
                jnp.where(columns[before] == places[at], 1.0, 0.0), axis=0, keepdims=True
            )
        slot = jnp.where(places[at] >= 0.0, nth * nodes + places[at], -1.0)
        pick = jnp.where(target == slot, 1.0, 0.0)
        pot_sorted = pot_sorted + jnp.sum(pick * pots[at], axis=1, keepdims=True)
        picks.append(pick.astype(jnp.bfloat16)[:, :local_leaves])
    lookup = jnp.concatenate(reach * (leaves // nodes), axis=0)

    reach_all[...] = jnp.zeros_like(reach_all)
    out_ref[...] = jnp.zeros_like(out_ref)
    live_rounds = jnp.max(live_ref[rounds + 1 : rounds + 2, :LANES])
    for at in range(rounds):

        @pl.when(live_rounds > at)
        def _():
            rows = slice(at * local_leaves, (at + 1) * local_leaves)
            live = live_ref[at : at + 1, :]
            strat = jnp.dot(picks[0], own_ref[rows, :], preferred_element_type=jnp.float32)
            for pick, pack in zip(picks[1:], came):
                strat = strat + jnp.dot(pick, pack[rows, :], preferred_element_type=jnp.float32)
            reach_all[:, :hands] = (lookup * strat * live[:, :hands]).astype(jnp.bfloat16)
            shown = jnp.dot(reach_all[...], payoff_ref[at], preferred_element_type=jnp.float32)
            value = shown * pot_sorted
            best = value[:nodes]
            for row in range(nodes, leaves, nodes):
                best = jnp.maximum(best, value[row : row + nodes])
            gain = best * (live * live_ref[rounds : rounds + 1, :])
            out_ref[...] += gain[:, :hands]


def body(
    board_cards, hand_ranks, river_count, reach_in, strategy, parent_node, pot_size, flop_weight
):
    seq_count = lax.axis_size("seq")
    board_count = lax.axis_size("board")
    rivers, local_leaves, hands = strategy.shape[1:]
    local_nodes = reach_in.shape[1]
    nodes, leaves = local_nodes * seq_count, local_leaves * seq_count
    rounds = -(-rivers // seq_count)
    padded = round_up(hands, LANES)
    cards, apart = hand_constants(hands, padded)
    anywhere = pl.BlockSpec(memory_space=pl.ANY)
    vmem = pl.BlockSpec(memory_space=pltpu.VMEM)
    params = pltpu.CompilerParams(vmem_limit_bytes=30 * 1024 * 1024)

    def shift(array, step):
        return lax.ppermute(
            array, "seq", [(at, (at + step) % seq_count) for at in range(seq_count)]
        )

    pack_rows = rounds * local_leaves + round_up(local_nodes + 4, 16)
    packs = pl.pallas_call(
        functools.partial(pack_kernel, rounds, seq_count),
        out_shape=[jax.ShapeDtypeStruct((pack_rows, hands), jnp.bfloat16)] * (seq_count - 1),
        in_specs=[anywhere] * 4,
        out_specs=[vmem] * (seq_count - 1),
        scratch_shapes=[
            pltpu.VMEM(reach_in.shape, jnp.bfloat16),
            pltpu.VMEM((1, local_leaves), jnp.int32),
            pltpu.VMEM((1, local_leaves), jnp.float32),
            pltpu.SemaphoreType.DMA((3 + rounds * (seq_count - 1),)),
        ],
        compiler_params=params,
        name="pack",
    )(strategy, reach_in, parent_node[None], pot_size[None])
    came = [shift(pack, step) for step, pack in enumerate(packs, 1)]

    payoff, own, live = pl.pallas_call(
        functools.partial(build_kernel, rounds, seq_count),
        out_shape=[
            jax.ShapeDtypeStruct((rounds, padded, padded), jnp.bfloat16),
            jax.ShapeDtypeStruct((rounds * local_leaves, hands), jnp.bfloat16),
            jax.ShapeDtypeStruct((round_up(rounds + 2, 8), padded), jnp.float32),
        ],
        in_specs=[anywhere] * 6,
        out_specs=[vmem] * 3,
        scratch_shapes=[
            pltpu.VMEM((rivers, 1, hands), jnp.int32),
            pltpu.VMEM((rounds, 1, padded), jnp.float32),
            pltpu.SMEM((board_cards.shape[2], 1, rivers), jnp.int32),
            pltpu.SMEM((1,), jnp.int32),
            pltpu.VMEM((2, padded), jnp.int32),
            pltpu.VMEM((padded, padded), jnp.bfloat16),
            pltpu.SemaphoreType.DMA((4 + rounds,)),
            pltpu.SemaphoreType.DMA((padded // LANES,)),
        ],
        compiler_params=params,
        cost_estimate=pl.CostEstimate(
            flops=10 * rounds * padded * padded, bytes_accessed=4 * padded * padded, transcendentals=0
        ),
        name="build",
    )(
        hand_ranks.transpose(1, 0, 2),
        board_cards.transpose(2, 0, 1),
        river_count,
        jnp.asarray(cards),
        jnp.asarray(apart, jnp.bfloat16),
        strategy,
    )

    total = pl.pallas_call(
        functools.partial(value_kernel, rounds, seq_count, nodes, leaves),
        out_shape=jax.ShapeDtypeStruct((nodes, hands), jnp.float32),
        in_specs=[vmem] * (4 + seq_count - 1),
        out_specs=vmem,
        scratch_shapes=[pltpu.VMEM((leaves, padded), jnp.bfloat16)],
        compiler_params=params,
        name="value",
    )(payoff, own, live, packs[0], *came)

    turn_share = total[:local_nodes]
    for step in range(1, seq_count):
        turn_share = turn_share + shift(total[step * local_nodes : (step + 1) * local_nodes], -step)

    root = flop_weight[0] * turn_share / board_count
    step = 1
    while step < board_count:
        root = root + lax.ppermute(
            root, "board", [(at, at ^ step) for at in range(board_count)]
        )
        step *= 2
    return (turn_share[None], root)


def solution(mesh):
    return jax.shard_map(
        body,
        mesh=mesh,
        in_specs=(
            P("board", None, None),
            P("board", None, None),
            P("board"),
            P("board", "seq", None),
            P("board", None, "seq", None),
            P("seq"),
            P("seq"),
            P("board"),
        ),
        out_specs=(P("board", "seq", None), P("seq", None)),
        check_vma=False,
    )
```

```python
import functools

import jax
import jax.numpy as jnp
from jax import lax
from jax.experimental import pallas as pl
from jax.experimental.pallas import tpu as pltpu
from jax.sharding import PartitionSpec as P

DECK = 52
LANES = 128
MIB = 1024 * 1024


def round_up(value, step):
    return -(-value // step) * step


def hand_cards(padded):
    hand = lax.broadcasted_iota(jnp.int32, (1, padded), 1)
    low = jnp.zeros((1, padded), jnp.int32)
    start = jnp.zeros((1, padded), jnp.int32)
    first = 0
    for card in range(DECK - 1):
        if card:
            low = jnp.where(hand >= first, card, low)
            start = jnp.where(hand >= first, first, start)
        first += DECK - 1 - card
    high = hand - start + low + 1
    real = hand < first
    return jnp.where(real, low, -1), jnp.where(real, high, -1)


def pad_rows(rows):
    return 1 << max(rows - 1, 0).bit_length()


def tile_count(rows, hands):
    full, rest = divmod(rows, 8)
    whole, tail = divmod(hands, LANES)
    count = full * whole
    if rest:
        count += -(-whole // (8 // pad_rows(rest)))
    groups = full + (rest > 0)
    if tail:
        count += -(-groups // 2) if tail <= LANES // 2 else groups
    return count


def pack_tiles(value, rows, hands):
    full, rest = divmod(rows, 8)
    whole, tail = divmod(hands, LANES)
    tiles = [
        value[8 * group : 8 * group + 8, LANES * at : LANES * (at + 1)]
        for group in range(full)
        for at in range(whole)
    ]
    if rest:
        part = pad_rows(rest)
        each = 8 // part
        for start in range(0, whole, each):
            pieces = [
                value[8 * full : 8 * full + part, LANES * at : LANES * (at + 1)]
                for at in range(start, min(start + each, whole))
            ]
            if len(pieces) < each:
                pieces.append(jnp.zeros((8 - part * len(pieces), LANES), value.dtype))
            tiles.append(jnp.concatenate(pieces, axis=0) if len(pieces) > 1 else pieces[0])
    if tail:
        groups = full + (rest > 0)
        tails = [value[8 * group : 8 * group + 8, LANES * whole :] for group in range(groups)]
        if tail <= LANES // 2:
            for at in range(0, groups, 2):
                tile = tails[at]
                if at + 1 < groups:
                    tile = tile + pltpu.roll(tails[at + 1], LANES // 2, 1)
                tiles.append(tile)
        else:
            tiles.extend(tails)
    return tiles


def unpack_tiles(tiles, rows, hands):
    full, rest = divmod(rows, 8)
    whole, tail = divmod(hands, LANES)
    groups = [[tiles[group * whole + at] for at in range(whole)] for group in range(full)]
    used = full * whole
    if rest:
        part = pad_rows(rest)
        each = 8 // part
        last = []
        for at in range(whole):
            tile = tiles[used + at // each]
            begin = part * (at % each)
            last.append(pltpu.roll(tile, (8 - begin) % 8, 0) if begin else tile)
        used += -(-whole // each)
        groups.append(last)
    if tail:
        for at, group in enumerate(groups):
            if tail <= LANES // 2:
                tile = tiles[used + at // 2]
                if at % 2:
                    tile = pltpu.roll(tile, LANES // 2, 1)
            else:
                tile = tiles[used + at]
            group.append(tile[:, :tail])
    return [jnp.concatenate(group, axis=1) for group in groups]


def copy_all(pairs, sems):
    copies = [
        pltpu.make_async_copy(source, target, sems.at[at])
        for at, (source, target) in enumerate(pairs)
    ]
    for copy in copies:
        copy.start()
    return copies


def pack_kernel(
    rounds,
    seq_count,
    strat_ref,
    reach_ref,
    parent_ref,
    pot_ref,
    *refs,
):
    outs, small_ref = refs[: seq_count - 1], refs[seq_count - 1]
    reach_tmp, parent_tmp, pot_tmp, small, sems, small_sems = refs[seq_count:]
    rivers, leaves, hands = strat_ref.shape[1:]
    here = lax.axis_index("seq")
    pairs = [(reach_ref, reach_tmp), (parent_ref, parent_tmp), (pot_ref, pot_tmp)]
    for step in range(1, seq_count):
        owner = lax.rem(here + step, seq_count)
        for at in range(rounds):
            river = jnp.minimum(at * seq_count + owner, rivers - 1)
            pairs.append((strat_ref.at[0, river], outs[step - 1].at[pl.ds(at * leaves, leaves)]))
    copies = copy_all(pairs, sems)
    for copy in copies[:3]:
        copy.wait()
    pot = pot_tmp[...]
    high = pot.astype(jnp.bfloat16).astype(jnp.float32)
    middle = (pot - high).astype(jnp.bfloat16).astype(jnp.float32)
    low = pot - high - middle
    labels = jnp.concatenate([parent_tmp[...].astype(jnp.float32), high, middle, low], axis=0)
    extra, nodes = small.shape[0], reach_tmp.shape[1]
    wide = jnp.concatenate([labels, jnp.zeros((4, hands - leaves), jnp.float32)], axis=1)
    rows = [reach_tmp[0].astype(jnp.float32), wide]
    if extra > nodes + 4:
        rows.append(jnp.zeros((extra - nodes - 4, hands), jnp.float32))
    small[...] = jnp.concatenate(rows, axis=0).astype(jnp.bfloat16)
    copies += copy_all(
        [(small, small_ref)] + [(small, out.at[pl.ds(rounds * leaves, extra)]) for out in outs],
        small_sems,
    )
    for copy in copies[3:]:
        copy.wait()


def build_kernel(
    rounds,
    seq_count,
    rank_ref,
    board_ref,
    count_ref,
    strat_ref,
    weight_ref,
    small_ref,
    payoff_ref,
    own_ref,
    live_ref,
    rank_tmp,
    rank_row,
    board_tmp,
    count_tmp,
    weight_tmp,
    holds,
    apart,
    sems,
):
    rivers, leaves, hands = strat_ref.shape[1:]
    padded = payoff_ref.shape[-1]
    here = lax.axis_index("seq")
    pairs = [
        (count_ref, count_tmp),
        (rank_ref, rank_tmp),
        (board_ref, board_tmp),
        (weight_ref, weight_tmp),
        (small_ref, own_ref.at[pl.ds(rounds * leaves, small_ref.shape[0])]),
    ]
    for at in range(rounds):
        river = jnp.minimum(at * seq_count + here, rivers - 1)
        pairs.append((strat_ref.at[0, river], own_ref.at[pl.ds(at * leaves, leaves)]))
    copies = copy_all(pairs, sems)
    low, high = hand_cards(padded)
    card = lax.broadcasted_iota(jnp.int32, (holds.shape[0], padded), 0)
    held = jnp.where((card == low) | (card == high), 1.0, 0.0)
    holds[...] = held.astype(jnp.bfloat16)
    for copy in copies[:4]:
        copy.wait()
    live_count = count_tmp[0]

    rank_row[...] = jnp.zeros_like(rank_row)
    live_ref[...] = jnp.zeros_like(live_ref)
    for at in range(rounds):
        river = jnp.minimum(at * seq_count + here, rivers - 1)
        rank_row[at, :, :hands] = rank_tmp[river].astype(jnp.float32)
        live = jnp.where(at * seq_count + here < live_count, 1.0, 0.0)
        live = jnp.where(low >= 0, live, 0.0)
        for slot in range(board_tmp.shape[0]):
            card = board_tmp[slot, 0, river]
            hit = (low == card) | (high == card)
            live = jnp.where(hit, 0.0, live)
        live_ref[at : at + 1, :] = live
    scale = 1.0 / (hands * jnp.full((1, padded), live_count.astype(jnp.float32)))
    live_ref[rounds : rounds + 1, :] = scale
    live_rounds = (live_count - here + seq_count - 1) // seq_count
    live_ref[rounds + 1 : rounds + 2, :] = jnp.full(
        (1, padded), live_rounds.astype(jnp.float32)
    )
    live_ref[rounds + 2 : rounds + 3, :] = jnp.full(
        (1, padded), weight_tmp[0] / lax.axis_size("board")
    )

    for start in range(0, padded, LANES):
        shared = lax.dot_general(
            holds[:, start : start + LANES],
            holds[...],
            (((0,), (0,)), ((), ())),
            preferred_element_type=jnp.float32,
        )
        apart[...] = jnp.maximum(1.0 - shared, 0.0).astype(jnp.bfloat16)

        def one_river(at, _):
            column = jnp.broadcast_to(rank_row[at, :, start : start + LANES], (LANES, LANES)).T
            for lane in range(0, padded, LANES):
                gap = (rank_row[at, :, lane : lane + LANES] - column).astype(jnp.bfloat16)
                mask = apart[:, lane : lane + LANES]
                payoff_ref[at, start : start + LANES, lane : lane + LANES] = jnp.maximum(
                    jnp.minimum(gap, mask), -mask
                )
            return 0

        lax.fori_loop(0, live_rounds, one_river, 0)
    for copy in copies[4:]:
        copy.wait()


def value_kernel(rounds, seq_count, nodes, leaves, *refs):
    payoff_ref, own_ref, live_ref = refs[:3]
    came = refs[3 : 3 + seq_count - 1]
    share_ref, root_ref, total, reach_all = refs[3 + seq_count - 1 :]
    hands = own_ref.shape[-1]
    padded = payoff_ref.shape[-1]
    local_leaves, local_nodes = leaves // seq_count, nodes // seq_count
    here = lax.axis_index("seq")
    packs = (own_ref,) + tuple(came)
    base = rounds * local_leaves

    reach, places, pots = [], [], []
    for pack in packs:
        small = pack[base:, :].astype(jnp.float32)
        reach.append(small[:local_nodes])
        labels = small[local_nodes : local_nodes + 4, :LANES]
        parent = labels[0:1]
        place = parent
        for owner in range(seq_count):
            inside = (parent >= owner * local_nodes) & (parent < (owner + 1) * local_nodes)
            move = (lax.rem(here - owner + seq_count, seq_count) - owner) * local_nodes
            place = jnp.where(inside, parent + move.astype(jnp.float32), place)
        lane = lax.broadcasted_iota(jnp.int32, (1, LANES), 1)
        places.append(jnp.where(lane < local_leaves, place, -1.0))
        pots.append(labels[1:2] + labels[2:3] + labels[3:4])

    sub = lax.broadcasted_iota(jnp.int32, (LANES, LANES), 0)
    lane = lax.broadcasted_iota(jnp.int32, (LANES, LANES), 1)
    columns = [jnp.broadcast_to(place, (LANES, LANES)).T for place in places]
    picks = []
    pot_sorted = jnp.zeros((leaves, 1), jnp.float32)
    target = lax.broadcasted_iota(jnp.int32, (leaves, LANES), 0).astype(jnp.float32)
    for at in range(seq_count):
        nth = jnp.sum(
            jnp.where((columns[at] == places[at]) & (sub < lane), 1.0, 0.0), axis=0, keepdims=True
        )
        for before in range(at):
            nth = nth + jnp.sum(
                jnp.where(columns[before] == places[at], 1.0, 0.0), axis=0, keepdims=True
            )
        slot = jnp.where(places[at] >= 0.0, nth * nodes + places[at], -1.0)
        pick = jnp.where(target == slot, 1.0, 0.0)
        pot_sorted = pot_sorted + jnp.sum(pick * pots[at], axis=1, keepdims=True)
        picks.append(pick.astype(jnp.bfloat16)[:, :local_leaves])
    lookup = jnp.concatenate(reach * (leaves // nodes), axis=0)

    reach_all[...] = jnp.zeros_like(reach_all)
    total[...] = jnp.zeros_like(total)
    live_rounds = jnp.max(live_ref[rounds + 1 : rounds + 2, :LANES])
    for at in range(rounds):

        @pl.when(live_rounds > at)
        def _():
            rows = slice(at * local_leaves, (at + 1) * local_leaves)
            live = live_ref[at : at + 1, :]
            strat = jnp.dot(picks[0], own_ref[rows, :], preferred_element_type=jnp.float32)
            for pick, pack in zip(picks[1:], came):
                strat = strat + jnp.dot(pick, pack[rows, :], preferred_element_type=jnp.float32)
            reach_all[:, :hands] = (lookup * strat * live[:, :hands]).astype(jnp.bfloat16)
            shown = jnp.dot(reach_all[...], payoff_ref[at], preferred_element_type=jnp.float32)
            value = shown * pot_sorted
            best = value[:nodes]
            for row in range(nodes, leaves, nodes):
                best = jnp.maximum(best, value[row : row + nodes])
            gain = best * (live * live_ref[rounds : rounds + 1, :])
            total[...] += gain

    weight = live_ref[rounds + 2 : rounds + 3, :LANES]
    count = tile_count(local_nodes, hands)
    boards, _, each = root_ref.shape[:3]
    if boards * each > count:
        root_ref[...] = jnp.zeros_like(root_ref)
    short = round_up(local_nodes, 8) - local_nodes
    for step in range(seq_count):
        rows = total[step * local_nodes : (step + 1) * local_nodes, :]
        if short:
            rows = jnp.concatenate([rows, jnp.zeros((short, padded), jnp.float32)], axis=0)
        owner = lax.rem(here - step + seq_count, seq_count)
        for at, tile in enumerate(pack_tiles(rows, local_nodes, hands)):
            share_ref[step, at] = tile
            root_ref[at // each, owner, at % each] = tile * weight


def sum_kernel(came_ref, out_ref):
    total = jnp.sum(came_ref[...], axis=0)
    for at in range(out_ref.shape[0]):
        out_ref[at] = total


def share_kernel(rows, hands, *refs):
    blocks, out_ref, tmp, sem = refs[:-3], refs[-3], refs[-2], refs[-1]
    tiles = []
    for at in range(tile_count(rows, hands)):
        tile = blocks[0][0, at]
        for block in blocks[1:]:
            tile = tile + block[at]
        tiles.append(tile)
    for at, group in enumerate(unpack_tiles(tiles, rows, hands)):
        for row in range(8 * at, min(8 * at + 8, rows)):
            tmp[row] = group[row - 8 * at : row - 8 * at + 1]
    copy = pltpu.make_async_copy(tmp, out_ref, sem)
    copy.start()
    copy.wait()


def root_kernel(rows, hands, tiles_ref, out_ref, tmp, sem):
    tiles = [tiles_ref[at] for at in range(tile_count(rows, hands))]
    for at, group in enumerate(unpack_tiles(tiles, rows, hands)):
        height = min(8, rows - 8 * at)
        tmp[8 * at : 8 * at + height, :] = group[:height]
    copy = pltpu.make_async_copy(tmp, out_ref, sem)
    copy.start()
    copy.wait()


def body(
    board_cards, hand_ranks, river_count, reach_in, strategy, parent_node, pot_size, flop_weight
):
    seq_count = lax.axis_size("seq")
    board_count = lax.axis_size("board")
    rivers, local_leaves, hands = strategy.shape[1:]
    local_nodes = reach_in.shape[1]
    nodes, leaves = local_nodes * seq_count, local_leaves * seq_count
    rounds = -(-rivers // seq_count)
    padded = round_up(hands, LANES)
    anywhere = pl.BlockSpec(memory_space=pltpu.HBM)
    vmem = pl.BlockSpec(memory_space=pltpu.VMEM)
    params = pltpu.CompilerParams(vmem_limit_bytes=16 * MIB)

    def shift(array, step):
        return lax.ppermute(
            array, "seq", [(at, (at + step) % seq_count) for at in range(seq_count)]
        )

    small_rows = round_up(local_nodes + 4, 16)
    pack_rows = rounds * local_leaves + small_rows
    *packs, small = pl.pallas_call(
        functools.partial(pack_kernel, rounds, seq_count),
        out_shape=[jax.ShapeDtypeStruct((pack_rows, hands), jnp.bfloat16)] * (seq_count - 1)
        + [jax.ShapeDtypeStruct((small_rows, hands), jnp.bfloat16)],
        in_specs=[anywhere] * 4,
        out_specs=[anywhere] * seq_count,
        scratch_shapes=[
            pltpu.VMEM(reach_in.shape, jnp.bfloat16),
            pltpu.VMEM((1, local_leaves), jnp.int32),
            pltpu.VMEM((1, local_leaves), jnp.float32),
            pltpu.VMEM((small_rows, hands), jnp.bfloat16),
            pltpu.SemaphoreType.DMA((3 + rounds * (seq_count - 1),)),
            pltpu.SemaphoreType.DMA((seq_count,)),
        ],
        compiler_params=pltpu.CompilerParams(vmem_limit_bytes=60 * MIB),
        name="pack",
    )(strategy, reach_in, parent_node[None], pot_size[None])
    came = [shift(pack, step) for step, pack in enumerate(packs, 1)]

    payoff, own, live = pl.pallas_call(
        functools.partial(build_kernel, rounds, seq_count),
        out_shape=[
            jax.ShapeDtypeStruct((rounds, padded, padded), jnp.bfloat16),
            jax.ShapeDtypeStruct((pack_rows, hands), jnp.bfloat16),
            jax.ShapeDtypeStruct((round_up(rounds + 3, 8), padded), jnp.float32),
        ],
        in_specs=[anywhere] * 6,
        out_specs=[vmem] * 3,
        scratch_shapes=[
            pltpu.VMEM((rivers, 1, hands), jnp.int32),
            pltpu.VMEM((rounds, 1, padded), jnp.float32),
            pltpu.SMEM((board_cards.shape[2], 1, rivers), jnp.int32),
            pltpu.SMEM((1,), jnp.int32),
            pltpu.SMEM((1,), jnp.float32),
            pltpu.VMEM((round_up(DECK, 16), padded), jnp.bfloat16),
            pltpu.VMEM((LANES, padded), jnp.bfloat16),
            pltpu.SemaphoreType.DMA((5 + rounds,)),
        ],
        compiler_params=pltpu.CompilerParams(vmem_limit_bytes=30 * MIB),
        cost_estimate=pl.CostEstimate(
            flops=10 * rounds * padded * padded, bytes_accessed=4 * padded * padded, transcendentals=0
        ),
        name="build",
    )(
        hand_ranks.transpose(1, 0, 2),
        board_cards.transpose(2, 0, 1),
        river_count,
        strategy,
        flop_weight,
        small,
    )

    count = tile_count(local_nodes, hands)
    each = -(-count // board_count)
    share, root = pl.pallas_call(
        functools.partial(value_kernel, rounds, seq_count, nodes, leaves),
        out_shape=[
            jax.ShapeDtypeStruct((seq_count, count, 8, LANES), jnp.float32),
            jax.ShapeDtypeStruct((board_count, seq_count, each, 8, LANES), jnp.float32),
        ],
        in_specs=[vmem] * (3 + seq_count - 1),
        out_specs=[vmem] * 2,
        scratch_shapes=[
            pltpu.VMEM((nodes, padded), jnp.float32),
            pltpu.VMEM((leaves, padded), jnp.bfloat16),
        ],
        compiler_params=params,
        name="value",
    )(payoff, own, live, *came)

    root = lax.all_to_all(
        root.reshape(board_count * seq_count, each * 8, LANES),
        ("board", "seq"),
        split_axis=0,
        concat_axis=0,
        tiled=True,
    )
    shares = [share] + [shift(share[step], -step) for step in range(1, seq_count)]
    root = pl.pallas_call(
        sum_kernel,
        out_shape=jax.ShapeDtypeStruct((board_count, each * 8, LANES), jnp.float32),
        in_specs=[vmem],
        out_specs=vmem,
        compiler_params=params,
        name="sum",
    )(root)
    root = lax.all_to_all(root, "board", split_axis=0, concat_axis=0, tiled=True)

    turn_value = pl.pallas_call(
        functools.partial(share_kernel, local_nodes, hands),
        out_shape=jax.ShapeDtypeStruct((local_nodes, 1, hands), jnp.float32),
        in_specs=[vmem] * seq_count,
        out_specs=anywhere,
        scratch_shapes=[
            pltpu.VMEM((local_nodes, 1, hands), jnp.float32),
            pltpu.SemaphoreType.DMA,
        ],
        compiler_params=params,
        name="share",
    )(*shares)
    root_value = pl.pallas_call(
        functools.partial(root_kernel, local_nodes, hands),
        out_shape=jax.ShapeDtypeStruct((local_nodes, hands), jnp.float32),
        in_specs=[vmem],
        out_specs=anywhere,
        scratch_shapes=[pltpu.VMEM((local_nodes, hands), jnp.float32), pltpu.SemaphoreType.DMA],
        compiler_params=params,
        name="root",
    )(root.reshape(board_count * each, 8, LANES))
    return (turn_value.transpose(1, 0, 2), root_value)


def solution(mesh):
    return jax.shard_map(
        body,
        mesh=mesh,
        in_specs=(
            P("board", None, None),
            P("board", None, None),
            P("board"),
            P("board", "seq", None),
            P("board", None, "seq", None),
            P("seq"),
            P("seq"),
            P("board"),
        ),
        out_specs=(P("board", "seq", None), P("seq", None)),
        check_vma=False,
    )
```

```python
import functools

import jax
import jax.numpy as jnp
from jax import lax
from jax.experimental import pallas as pl
from jax.experimental.pallas import tpu as pltpu
from jax.sharding import PartitionSpec as P

DECK = 52
LANES = 128
MIB = 1024 * 1024


def round_up(value, step):
    return -(-value // step) * step


def hand_cards(padded):
    hand = lax.broadcasted_iota(jnp.int32, (1, padded), 1)
    low = jnp.zeros((1, padded), jnp.int32)
    start = jnp.zeros((1, padded), jnp.int32)
    first = 0
    for card in range(DECK - 1):
        if card:
            low = jnp.where(hand >= first, card, low)
            start = jnp.where(hand >= first, first, start)
        first += DECK - 1 - card
    high = hand - start + low + 1
    real = hand < first
    return jnp.where(real, low, -1), jnp.where(real, high, -1)


def pad_rows(rows):
    return 1 << max(rows - 1, 0).bit_length()


def tile_count(rows, hands):
    full, rest = divmod(rows, 8)
    whole, tail = divmod(hands, LANES)
    count = full * whole
    if rest:
        count += -(-whole // (8 // pad_rows(rest)))
    groups = full + (rest > 0)
    if tail:
        count += -(-groups // 2) if tail <= LANES // 2 else groups
    return count


def pack_tiles(value, rows, hands):
    full, rest = divmod(rows, 8)
    whole, tail = divmod(hands, LANES)
    tiles = [
        value[8 * group : 8 * group + 8, LANES * at : LANES * (at + 1)]
        for group in range(full)
        for at in range(whole)
    ]
    if rest:
        part = pad_rows(rest)
        each = 8 // part
        for start in range(0, whole, each):
            pieces = [
                value[8 * full : 8 * full + part, LANES * at : LANES * (at + 1)]
                for at in range(start, min(start + each, whole))
            ]
            if len(pieces) < each:
                pieces.append(jnp.zeros((8 - part * len(pieces), LANES), value.dtype))
            tiles.append(jnp.concatenate(pieces, axis=0) if len(pieces) > 1 else pieces[0])
    if tail:
        groups = full + (rest > 0)
        tails = [value[8 * group : 8 * group + 8, LANES * whole :] for group in range(groups)]
        if tail <= LANES // 2:
            for at in range(0, groups, 2):
                tile = tails[at]
                if at + 1 < groups:
                    tile = tile + pltpu.roll(tails[at + 1], LANES // 2, 1)
                tiles.append(tile)
        else:
            tiles.extend(tails)
    return tiles


def unpack_tiles(tiles, rows, hands):
    full, rest = divmod(rows, 8)
    whole, tail = divmod(hands, LANES)
    groups = [[tiles[group * whole + at] for at in range(whole)] for group in range(full)]
    used = full * whole
    if rest:
        part = pad_rows(rest)
        each = 8 // part
        last = []
        for at in range(whole):
            tile = tiles[used + at // each]
            begin = part * (at % each)
            last.append(pltpu.roll(tile, (8 - begin) % 8, 0) if begin else tile)
        used += -(-whole // each)
        groups.append(last)
    if tail:
        for at, group in enumerate(groups):
            if tail <= LANES // 2:
                tile = tiles[used + at // 2]
                if at % 2:
                    tile = pltpu.roll(tile, LANES // 2, 1)
            else:
                tile = tiles[used + at]
            group.append(tile[:, :tail])
    return [jnp.concatenate(group, axis=1) for group in groups]


def copy_all(pairs, sems):
    copies = [
        pltpu.make_async_copy(source, target, sems.at[at])
        for at, (source, target) in enumerate(pairs)
    ]
    for copy in copies:
        copy.start()
    return copies


def pack_kernel(
    rounds,
    seq_count,
    strat_ref,
    reach_ref,
    parent_ref,
    pot_ref,
    rank_ref,
    board_ref,
    *refs,
):
    packs, info_ref = refs[:seq_count], refs[seq_count]
    strat_tmp, reach_tmp, parent_tmp, pot_tmp, rank_tmp, board_tmp, small, info = refs[
        seq_count + 1 : -2
    ]
    in_sems, out_sems = refs[-2:]
    rivers, leaves, hands = strat_ref.shape[1:]
    padded = info.shape[-1]
    here = lax.axis_index("seq")
    loads = [
        (reach_ref, reach_tmp),
        (parent_ref, parent_tmp),
        (pot_ref, pot_tmp),
        (rank_ref, rank_tmp),
        (board_ref, board_tmp),
    ]
    first = len(loads)
    stores = []
    order = [step % seq_count for step in range(1, seq_count + 1)]
    for step in order:
        owner = lax.rem(here + step, seq_count)
        for at in range(rounds):
            river = jnp.minimum(at * seq_count + owner, rivers - 1)
            held = strat_tmp.at[step, pl.ds(at * leaves, leaves)]
            loads.append((strat_ref.at[0, river], held))
            stores.append((held, packs[step].at[pl.ds(at * leaves, leaves)]))
    loads = copy_all(loads, in_sems)

    low, high = hand_cards(padded)
    for copy in loads[:3]:
        copy.wait()
    pot = pot_tmp[...]
    top = pot.astype(jnp.bfloat16).astype(jnp.float32)
    middle = (pot - top).astype(jnp.bfloat16).astype(jnp.float32)
    labels = jnp.concatenate(
        [parent_tmp[...].astype(jnp.float32), top, middle, pot - top - middle], axis=0
    )
    extra, nodes = small.shape[0], reach_tmp.shape[1]
    wide = jnp.concatenate([labels, jnp.zeros((4, hands - leaves), jnp.float32)], axis=1)
    rows = [reach_tmp[0].astype(jnp.float32), wide]
    if extra > nodes + 4:
        rows.append(jnp.zeros((extra - nodes - 4, hands), jnp.float32))
    small[...] = jnp.concatenate(rows, axis=0).astype(jnp.bfloat16)
    stores += [(small, pack.at[pl.ds(rounds * leaves, extra)]) for pack in packs]
    stores += [(info, info_ref)]
    stores = [
        pltpu.make_async_copy(source, target, out_sems.at[at])
        for at, (source, target) in enumerate(stores)
    ]
    for copy in stores[-1 - seq_count : -1]:
        copy.start()
    for at in range((seq_count - 1) * rounds):
        loads[first + at].wait()
        stores[at].start()

    for copy in loads[3:first]:
        copy.wait()
    info[...] = jnp.zeros_like(info)
    for at in range(rounds):
        river = jnp.minimum(at * seq_count + here, rivers - 1)
        info[at : at + 1, :hands] = rank_tmp[river].astype(jnp.float32)
        live = jnp.where(low >= 0, 1.0, 0.0)
        for slot in range(board_tmp.shape[0]):
            card = board_tmp[slot, 0, river]
            live = jnp.where((low == card) | (high == card), 0.0, live)
        info[rounds + at : rounds + at + 1, :] = live
    stores[-1].start()
    for at in range((seq_count - 1) * rounds, seq_count * rounds):
        loads[first + at].wait()
        stores[at].start()
    for copy in stores:
        copy.wait()


def build_kernel(
    rounds,
    seq_count,
    count_ref,
    weight_ref,
    info_ref,
    pack_ref,
    payoff_ref,
    own_ref,
    live_ref,
    holds,
    apart,
    sem,
):
    padded = payoff_ref.shape[-1]
    hands = pack_ref.shape[-1]
    here = lax.axis_index("seq")
    handed = pltpu.make_async_copy(pack_ref, own_ref, sem)
    handed.start()
    live_count = count_ref[0]
    live_rounds = lax.div(live_count - here + seq_count - 1, seq_count)
    live_ref[...] = jnp.zeros_like(live_ref)
    live_ref[:rounds, :] = info_ref[rounds : 2 * rounds, :]
    live_ref[rounds : rounds + 1, :] = 1.0 / (
        hands * jnp.full((1, padded), live_count.astype(jnp.float32))
    )
    live_ref[rounds + 1 : rounds + 2, :] = jnp.full(
        (1, padded), live_rounds.astype(jnp.float32)
    )
    live_ref[rounds + 2 : rounds + 3, :] = jnp.full(
        (1, padded), weight_ref[0] / lax.axis_size("board")
    )

    low, high = hand_cards(padded)
    card = lax.broadcasted_iota(jnp.int32, (holds.shape[0], padded), 0)
    holds[...] = jnp.where((card == low) | (card == high), 1.0, 0.0).astype(jnp.bfloat16)

    def mask_rows(start):
        shared = lax.dot_general(
            holds[:, start : start + LANES],
            holds[...],
            (((0,), (0,)), ((), ())),
            preferred_element_type=jnp.float32,
        )
        apart[start : start + LANES, :] = jnp.maximum(1.0 - shared, 0.0).astype(jnp.bfloat16)

    mask_rows(0)
    for start in range(0, padded, LANES):
        if start + LANES < padded:
            mask_rows(start + LANES)
        rows = slice(start, start + LANES)
        columns = [
            jnp.broadcast_to(info_ref[at : at + 1, rows], (LANES, LANES)).T
            for at in range(rounds)
        ]
        for lane in range(0, padded, LANES):
            here_lanes = slice(lane, lane + LANES)
            mask = apart[rows, here_lanes]
            for at in range(rounds):
                gap = (info_ref[at : at + 1, here_lanes] - columns[at]).astype(jnp.bfloat16)
                payoff_ref[at, rows, here_lanes] = jnp.maximum(jnp.minimum(gap, mask), -mask)
    handed.wait()


def value_kernel(rounds, seq_count, nodes, leaves, *refs):
    payoff_ref, own_ref, live_ref = refs[:3]
    came = refs[3 : 3 + seq_count - 1]
    outs, (total, reach_all) = refs[3 + seq_count - 1 : -2], refs[-2:]
    hands = own_ref.shape[-1]
    padded = payoff_ref.shape[-1]
    local_leaves, local_nodes = leaves // seq_count, nodes // seq_count
    here = lax.axis_index("seq")
    packs = (own_ref,) + tuple(came)
    base = rounds * local_leaves

    reach, places, pots = [], [], []
    for pack in packs:
        small = pack[base:, :].astype(jnp.float32)
        reach.append(small[:local_nodes])
        labels = small[local_nodes : local_nodes + 4, :LANES]
        parent = labels[0:1]
        place = parent
        for owner in range(seq_count):
            inside = (parent >= owner * local_nodes) & (parent < (owner + 1) * local_nodes)
            move = (lax.rem(here - owner + seq_count, seq_count) - owner) * local_nodes
            place = jnp.where(inside, parent + move.astype(jnp.float32), place)
        lane = lax.broadcasted_iota(jnp.int32, (1, LANES), 1)
        places.append(jnp.where(lane < local_leaves, place, -1.0))
        pots.append(labels[1:2] + labels[2:3] + labels[3:4])

    sub = lax.broadcasted_iota(jnp.int32, (LANES, LANES), 0)
    lane = lax.broadcasted_iota(jnp.int32, (LANES, LANES), 1)
    columns = [jnp.broadcast_to(place, (LANES, LANES)).T for place in places]
    picks = []
    pot_sorted = jnp.zeros((leaves, 1), jnp.float32)
    target = lax.broadcasted_iota(jnp.int32, (leaves, LANES), 0).astype(jnp.float32)
    for at in range(seq_count):
        nth = jnp.sum(
            jnp.where((columns[at] == places[at]) & (sub < lane), 1.0, 0.0), axis=0, keepdims=True
        )
        for before in range(at):
            nth = nth + jnp.sum(
                jnp.where(columns[before] == places[at], 1.0, 0.0), axis=0, keepdims=True
            )
        slot = jnp.where(places[at] >= 0.0, nth * nodes + places[at], -1.0)
        pick = jnp.where(target == slot, 1.0, 0.0)
        pot_sorted = pot_sorted + jnp.sum(pick * pots[at], axis=1, keepdims=True)
        picks.append(pick.astype(jnp.bfloat16)[:, :local_leaves])
    lookup = jnp.concatenate(reach * (leaves // nodes), axis=0)

    reach_all[...] = jnp.zeros_like(reach_all)
    total[...] = jnp.zeros_like(total)
    live_rounds = jnp.max(live_ref[rounds + 1 : rounds + 2, :LANES])
    for at in range(rounds):

        @pl.when(live_rounds > at)
        def _():
            rows = slice(at * local_leaves, (at + 1) * local_leaves)
            live = live_ref[at : at + 1, :]
            strat = jnp.dot(picks[0], own_ref[rows, :], preferred_element_type=jnp.float32)
            for pick, pack in zip(picks[1:], came):
                strat = strat + jnp.dot(pick, pack[rows, :], preferred_element_type=jnp.float32)
            reach_all[:, :hands] = (lookup * strat * live[:, :hands]).astype(jnp.bfloat16)
            shown = jnp.dot(reach_all[...], payoff_ref[at], preferred_element_type=jnp.float32)
            value = shown * pot_sorted
            best = value[:nodes]
            for row in range(nodes, leaves, nodes):
                best = jnp.maximum(best, value[row : row + nodes])
            gain = best * (live * live_ref[rounds : rounds + 1, :])
            total[...] += gain

    outs[-1][...] = jnp.broadcast_to(live_ref[rounds + 2 : rounds + 3, :LANES], (8, LANES))
    short = round_up(local_nodes, 8) - local_nodes
    for step in range(seq_count):
        rows = total[step * local_nodes : (step + 1) * local_nodes, :]
        if short:
            rows = jnp.concatenate([rows, jnp.zeros((short, padded), jnp.float32)], axis=0)
        for at, tile in enumerate(pack_tiles(rows, local_nodes, hands)):
            outs[step][at] = tile


def share_kernel(rows, hands, tiles_ref, out_ref, tmp, sem):
    tiles = [tiles_ref[at] for at in range(tile_count(rows, hands))]
    for at, group in enumerate(unpack_tiles(tiles, rows, hands)):
        for row in range(8 * at, min(8 * at + 8, rows)):
            tmp[row] = group[row - 8 * at : row - 8 * at + 1]
    copy = pltpu.make_async_copy(tmp, out_ref, sem)
    copy.start()
    copy.wait()


def root_kernel(rows, hands, mine_ref, came_ref, out_ref, tmp, sem):
    tiles = [mine_ref[at] + came_ref[at] for at in range(tile_count(rows, hands))]
    for at, group in enumerate(unpack_tiles(tiles, rows, hands)):
        height = min(8, rows - 8 * at)
        tmp[8 * at : 8 * at + height, :] = group[:height]
    copy = pltpu.make_async_copy(tmp, out_ref, sem)
    copy.start()
    copy.wait()


def body(
    board_cards, hand_ranks, river_count, reach_in, strategy, parent_node, pot_size, flop_weight
):
    seq_count = lax.axis_size("seq")
    board_count = lax.axis_size("board")
    rivers, local_leaves, hands = strategy.shape[1:]
    local_nodes = reach_in.shape[1]
    nodes, leaves = local_nodes * seq_count, local_leaves * seq_count
    rounds = -(-rivers // seq_count)
    padded = round_up(hands, LANES)
    anywhere = pl.BlockSpec(memory_space=pltpu.HBM)
    vmem = pl.BlockSpec(memory_space=pltpu.VMEM)
    params = pltpu.CompilerParams(vmem_limit_bytes=16 * MIB)

    def shift(array, step):
        return lax.ppermute(
            array, "seq", [(at, (at + step) % seq_count) for at in range(seq_count)]
        )

    small_rows = round_up(local_nodes + 4, 16)
    pack_rows = rounds * local_leaves + small_rows
    info_rows = round_up(2 * rounds, 8)
    own_pack, *packs, info = pl.pallas_call(
        functools.partial(pack_kernel, rounds, seq_count),
        out_shape=[jax.ShapeDtypeStruct((pack_rows, hands), jnp.bfloat16)] * seq_count
        + [jax.ShapeDtypeStruct((info_rows, padded), jnp.float32)],
        in_specs=[anywhere] * 6,
        out_specs=[anywhere] * (seq_count + 1),
        scratch_shapes=[
            pltpu.VMEM((seq_count, rounds * local_leaves, hands), jnp.bfloat16),
            pltpu.VMEM(reach_in.shape, jnp.bfloat16),
            pltpu.VMEM((1, local_leaves), jnp.int32),
            pltpu.VMEM((1, local_leaves), jnp.float32),
            pltpu.VMEM((rivers, 1, hands), jnp.int32),
            pltpu.SMEM((board_cards.shape[2], 1, rivers), jnp.int32),
            pltpu.VMEM((small_rows, hands), jnp.bfloat16),
            pltpu.VMEM((info_rows, padded), jnp.float32),
            pltpu.SemaphoreType.DMA((5 + rounds * seq_count,)),
            pltpu.SemaphoreType.DMA((1 + (1 + rounds) * seq_count,)),
        ],
        compiler_params=pltpu.CompilerParams(vmem_limit_bytes=60 * MIB),
        name="pack",
    )(
        strategy,
        reach_in,
        parent_node[None],
        pot_size[None],
        hand_ranks.transpose(1, 0, 2),
        board_cards.transpose(2, 0, 1),
    )
    came = [shift(pack, step) for step, pack in enumerate(packs, 1)]

    smem = pl.BlockSpec(memory_space=pltpu.SMEM)
    payoff, own, live = pl.pallas_call(
        functools.partial(build_kernel, rounds, seq_count),
        out_shape=[
            jax.ShapeDtypeStruct((rounds, padded, padded), jnp.bfloat16),
            jax.ShapeDtypeStruct((pack_rows, hands), jnp.bfloat16),
            jax.ShapeDtypeStruct((round_up(rounds + 3, 8), padded), jnp.float32),
        ],
        in_specs=[smem, smem, vmem, vmem],
        out_specs=[vmem] * 3,
        scratch_shapes=[
            pltpu.VMEM((round_up(DECK, 16), padded), jnp.bfloat16),
            pltpu.VMEM((padded, padded), jnp.bfloat16),
            pltpu.SemaphoreType.DMA,
        ],
        compiler_params=pltpu.CompilerParams(vmem_limit_bytes=30 * MIB),
        cost_estimate=pl.CostEstimate(
            flops=10 * rounds * padded * padded, bytes_accessed=4 * padded * padded, transcendentals=0
        ),
        name="build",
    )(river_count, flop_weight, info, own_pack)

    count = tile_count(local_nodes, hands)
    *shares, weight = pl.pallas_call(
        functools.partial(value_kernel, rounds, seq_count, nodes, leaves),
        out_shape=[jax.ShapeDtypeStruct((count, 8, LANES), jnp.float32)] * seq_count
        + [jax.ShapeDtypeStruct((8, LANES), jnp.float32)],
        in_specs=[vmem] * (3 + seq_count - 1),
        out_specs=[vmem] * (seq_count + 1),
        scratch_shapes=[
            pltpu.VMEM((nodes, padded), jnp.float32),
            pltpu.VMEM((leaves, padded), jnp.bfloat16),
        ],
        compiler_params=params,
        name="value",
    )(payoff, own, live, *came)

    share = shares[0]
    for step in range(1, seq_count):
        share = share + shift(shares[step], -step)
    root = share * weight[None]
    step = 1
    while True:
        came = lax.ppermute(root, "board", [(at, at ^ step) for at in range(board_count)])
        step *= 2
        if step >= board_count:
            break
        root = root + came

    turn_value = pl.pallas_call(
        functools.partial(share_kernel, local_nodes, hands),
        out_shape=jax.ShapeDtypeStruct((local_nodes, 1, hands), jnp.float32),
        in_specs=[vmem],
        out_specs=anywhere,
        scratch_shapes=[
            pltpu.VMEM((local_nodes, 1, hands), jnp.float32),
            pltpu.SemaphoreType.DMA,
        ],
        compiler_params=params,
        name="share",
    )(share)
    root_value = pl.pallas_call(
        functools.partial(root_kernel, local_nodes, hands),
        out_shape=jax.ShapeDtypeStruct((local_nodes, hands), jnp.float32),
        in_specs=[vmem] * 2,
        out_specs=anywhere,
        scratch_shapes=[pltpu.VMEM((local_nodes, hands), jnp.float32), pltpu.SemaphoreType.DMA],
        compiler_params=params,
        name="root",
    )(root, came)
    return (turn_value.transpose(1, 0, 2), root_value)


def solution(mesh):
    return jax.shard_map(
        body,
        mesh=mesh,
        in_specs=(
            P("board", None, None),
            P("board", None, None),
            P("board"),
            P("board", "seq", None),
            P("board", None, "seq", None),
            P("seq"),
            P("seq"),
            P("board"),
        ),
        out_specs=(P("board", "seq", None), P("seq", None)),
        check_vma=False,
    )
```

```python
import functools

import jax
import jax.numpy as jnp
from jax import lax
from jax.experimental import pallas as pl
from jax.experimental.pallas import tpu as pltpu
from jax.sharding import PartitionSpec as P

DECK = 52
LANES = 128
MIB = 1024 * 1024


def round_up(value, step):
    return -(-value // step) * step


def hand_cards(padded):
    hand = lax.broadcasted_iota(jnp.int32, (1, padded), 1)
    low = jnp.zeros((1, padded), jnp.int32)
    start = jnp.zeros((1, padded), jnp.int32)
    first = 0
    for card in range(DECK - 1):
        if card:
            low = jnp.where(hand >= first, card, low)
            start = jnp.where(hand >= first, first, start)
        first += DECK - 1 - card
    high = hand - start + low + 1
    real = hand < first
    return jnp.where(real, low, -1), jnp.where(real, high, -1)


def pad_rows(rows):
    return 1 << max(rows - 1, 0).bit_length()


def tile_count(rows, hands):
    full, rest = divmod(rows, 8)
    whole, tail = divmod(hands, LANES)
    count = full * whole
    if rest:
        count += -(-whole // (8 // pad_rows(rest)))
    groups = full + (rest > 0)
    if tail:
        count += -(-groups // 2) if tail <= LANES // 2 else groups
    return count


def pack_tiles(value, rows, hands):
    full, rest = divmod(rows, 8)
    whole, tail = divmod(hands, LANES)
    tiles = [
        value[8 * group : 8 * group + 8, LANES * at : LANES * (at + 1)]
        for group in range(full)
        for at in range(whole)
    ]
    if rest:
        part = pad_rows(rest)
        each = 8 // part
        for start in range(0, whole, each):
            pieces = [
                value[8 * full : 8 * full + part, LANES * at : LANES * (at + 1)]
                for at in range(start, min(start + each, whole))
            ]
            if len(pieces) < each:
                pieces.append(jnp.zeros((8 - part * len(pieces), LANES), value.dtype))
            tiles.append(jnp.concatenate(pieces, axis=0) if len(pieces) > 1 else pieces[0])
    if tail:
        groups = full + (rest > 0)
        tails = [value[8 * group : 8 * group + 8, LANES * whole :] for group in range(groups)]
        if tail <= LANES // 2:
            for at in range(0, groups, 2):
                tile = tails[at]
                if at + 1 < groups:
                    tile = tile + pltpu.roll(tails[at + 1], LANES // 2, 1)
                tiles.append(tile)
        else:
            tiles.extend(tails)
    return tiles


def unpack_tiles(tiles, rows, hands):
    full, rest = divmod(rows, 8)
    whole, tail = divmod(hands, LANES)
    groups = [[tiles[group * whole + at] for at in range(whole)] for group in range(full)]
    used = full * whole
    if rest:
        part = pad_rows(rest)
        each = 8 // part
        last = []
        for at in range(whole):
            tile = tiles[used + at // each]
            begin = part * (at % each)
            last.append(pltpu.roll(tile, (8 - begin) % 8, 0) if begin else tile)
        used += -(-whole // each)
        groups.append(last)
    if tail:
        for at, group in enumerate(groups):
            if tail <= LANES // 2:
                tile = tiles[used + at // 2]
                if at % 2:
                    tile = pltpu.roll(tile, LANES // 2, 1)
            else:
                tile = tiles[used + at]
            group.append(tile[:, :tail])
    return [jnp.concatenate(group, axis=1) for group in groups]


def copy_all(pairs, sems):
    copies = [
        pltpu.make_async_copy(source, target, sems.at[at])
        for at, (source, target) in enumerate(pairs)
    ]
    for copy in copies:
        copy.start()
    return copies


def pack_kernel(
    rounds,
    seq_count,
    reach_ref,
    parent_ref,
    pot_ref,
    rank_ref,
    board_ref,
    count_ref,
    weight_ref,
    small_ref,
    info_ref,
    reach_tmp,
    parent_tmp,
    pot_tmp,
    rank_tmp,
    board_tmp,
    count_tmp,
    weight_tmp,
    small,
    info,
    sems,
    out_sems,
):
    hands, padded = small.shape[-1], info.shape[-1]
    nodes, leaves = reach_tmp.shape[1], parent_tmp.shape[-1]
    rivers = rank_tmp.shape[0]
    here = lax.axis_index("seq")
    loads = copy_all(
        [
            (reach_ref, reach_tmp),
            (parent_ref, parent_tmp),
            (pot_ref, pot_tmp),
            (rank_ref, rank_tmp),
            (board_ref, board_tmp),
            (count_ref, count_tmp),
            (weight_ref, weight_tmp),
        ],
        sems,
    )
    low, high = hand_cards(padded)
    info[...] = jnp.zeros_like(info)
    for copy in loads[:3]:
        copy.wait()
    pot = pot_tmp[...]
    parent = parent_tmp[...].astype(jnp.float32)
    reach = reach_tmp[0].astype(jnp.float32)
    top = pot.astype(jnp.bfloat16).astype(jnp.float32)
    middle = (pot - top).astype(jnp.bfloat16).astype(jnp.float32)
    labels = jnp.concatenate([parent, top, middle, pot - top - middle], axis=0)
    rows = [reach, jnp.concatenate([labels, jnp.zeros((4, hands - leaves), jnp.float32)], axis=1)]
    extra = small.shape[0]
    if extra > nodes + 4:
        rows.append(jnp.zeros((extra - nodes - 4, hands), jnp.float32))
    small[...] = jnp.concatenate(rows, axis=0).astype(jnp.bfloat16)
    sent = pltpu.make_async_copy(small, small_ref, out_sems.at[0])
    sent.start()

    for copy in loads[3:]:
        copy.wait()
    live_count = count_tmp[0]
    base = 2 * rounds
    for at in range(rounds):
        river = jnp.minimum(at * seq_count + here, rivers - 1)
        info[at : at + 1, :hands] = rank_tmp[river].astype(jnp.float32)
        live = jnp.where(low >= 0, 1.0, 0.0)
        for slot in range(board_tmp.shape[0]):
            card = board_tmp[slot, 0, river]
            live = jnp.where((low == card) | (high == card), 0.0, live)
        info[rounds + at : rounds + at + 1, :] = live
    info[base : base + 1, :] = 1.0 / (hands * jnp.full((1, padded), live_count.astype(jnp.float32)))
    live_rounds = lax.div(live_count - here + seq_count - 1, seq_count)
    info[base + 1 : base + 2, :] = jnp.full((1, padded), live_rounds.astype(jnp.float32))
    info[base + 2 : base + 3, :] = jnp.full((1, padded), weight_tmp[0] / lax.axis_size("board"))
    info[base + 3 : base + 4, :leaves] = parent
    info[base + 4 : base + 5, :leaves] = pot
    info[base + 5 : base + 5 + nodes, :hands] = reach
    kept = pltpu.make_async_copy(info, info_ref, out_sems.at[1])
    kept.start()
    sent.wait()
    kept.wait()


def build_kernel(rounds, info_ref, payoff_ref, kept_ref, holds, apart):
    padded = payoff_ref.shape[-1]
    kept_ref[...] = info_ref[...]

    low, high = hand_cards(padded)
    card = lax.broadcasted_iota(jnp.int32, (holds.shape[0], padded), 0)
    holds[...] = jnp.where((card == low) | (card == high), 1.0, 0.0).astype(jnp.bfloat16)

    def mask_rows(start):
        shared = lax.dot_general(
            holds[:, start : start + LANES],
            holds[...],
            (((0,), (0,)), ((), ())),
            preferred_element_type=jnp.float32,
        )
        apart[start : start + LANES, :] = jnp.maximum(1.0 - shared, 0.0).astype(jnp.bfloat16)

    mask_rows(0)
    for start in range(0, padded, LANES):
        if start + LANES < padded:
            mask_rows(start + LANES)
        rows = slice(start, start + LANES)
        columns = [
            jnp.broadcast_to(info_ref[at : at + 1, rows], (LANES, LANES)).T
            for at in range(rounds)
        ]
        for lane in range(0, padded, LANES):
            here_lanes = slice(lane, lane + LANES)
            mask = apart[rows, here_lanes]
            for at in range(rounds):
                gap = (columns[at] - info_ref[at : at + 1, here_lanes]).astype(jnp.bfloat16)
                payoff_ref[at, rows, here_lanes] = jnp.maximum(jnp.minimum(gap, mask), -mask)


def value_kernel(rounds, seq_count, nodes, leaves, *refs):
    payoff_ref, info_ref, own_ref = refs[:3]
    came = refs[3 : 2 + seq_count]
    smalls = refs[2 + seq_count : 1 + 2 * seq_count]
    outs, (total, reach_all) = refs[1 + 2 * seq_count : -2], refs[-2:]
    hands = own_ref.shape[-1]
    padded = payoff_ref.shape[-1]
    local_leaves, local_nodes = leaves // seq_count, nodes // seq_count
    here = lax.axis_index("seq")
    base = 2 * rounds

    reach, places, pots = [], [], []
    for at in range(seq_count):
        if at == 0:
            reach.append(info_ref[base + 5 : base + 5 + local_nodes, :hands])
            parent = info_ref[base + 3 : base + 4, :LANES]
            pots.append(info_ref[base + 4 : base + 5, :LANES])
        else:
            small = smalls[at - 1][...].astype(jnp.float32)
            reach.append(small[:local_nodes])
            labels = small[local_nodes : local_nodes + 4, :LANES]
            parent = labels[0:1]
            pots.append(labels[1:2] + labels[2:3] + labels[3:4])
        place = parent
        for owner in range(seq_count):
            inside = (parent >= owner * local_nodes) & (parent < (owner + 1) * local_nodes)
            move = (lax.rem(here - owner + seq_count, seq_count) - owner) * local_nodes
            place = jnp.where(inside, parent + move.astype(jnp.float32), place)
        lane = lax.broadcasted_iota(jnp.int32, (1, LANES), 1)
        places.append(jnp.where(lane < local_leaves, place, -1.0))

    sub = lax.broadcasted_iota(jnp.int32, (LANES, LANES), 0)
    lane = lax.broadcasted_iota(jnp.int32, (LANES, LANES), 1)
    columns = [jnp.broadcast_to(place, (LANES, LANES)).T for place in places]
    picks = []
    pot_sorted = jnp.zeros((leaves, 1), jnp.float32)
    target = lax.broadcasted_iota(jnp.int32, (leaves, LANES), 0).astype(jnp.float32)
    for at in range(seq_count):
        nth = jnp.sum(
            jnp.where((columns[at] == places[at]) & (sub < lane), 1.0, 0.0), axis=0, keepdims=True
        )
        for before in range(at):
            nth = nth + jnp.sum(
                jnp.where(columns[before] == places[at], 1.0, 0.0), axis=0, keepdims=True
            )
        slot = jnp.where(places[at] >= 0.0, nth * nodes + places[at], -1.0)
        pick = jnp.where(target == slot, 1.0, 0.0)
        pot_sorted = pot_sorted + jnp.sum(pick * pots[at], axis=1, keepdims=True)
        picks.append(pick.astype(jnp.bfloat16)[:, :local_leaves])
    lookup = jnp.concatenate(reach * (leaves // nodes), axis=0)

    reach_all[...] = jnp.zeros_like(reach_all)
    total[...] = jnp.zeros_like(total)
    live_rounds = jnp.max(info_ref[base + 1 : base + 2, :LANES])
    for at in range(rounds):

        @pl.when(live_rounds > at)
        def _():
            rows = slice(at * local_leaves, (at + 1) * local_leaves)
            live = info_ref[rounds + at : rounds + at + 1, :]
            strat = jnp.dot(picks[0], own_ref[rows, :], preferred_element_type=jnp.float32)
            for pick, pack in zip(picks[1:], came):
                strat = strat + jnp.dot(pick, pack[rows, :], preferred_element_type=jnp.float32)
            reach_all[:, :hands] = (lookup * strat * live[:, :hands]).astype(jnp.bfloat16)
            shown = lax.dot_general(
                payoff_ref[at],
                reach_all[...],
                (((1,), (1,)), ((), ())),
                preferred_element_type=jnp.float32,
            )
            value = shown.T * pot_sorted
            best = value[:nodes]
            for row in range(nodes, leaves, nodes):
                best = jnp.maximum(best, value[row : row + nodes])
            gain = best * (live * info_ref[base : base + 1, :])
            total[...] += gain

    outs[-1][...] = jnp.broadcast_to(info_ref[base + 2 : base + 3, :LANES], (8, LANES))
    short = round_up(local_nodes, 8) - local_nodes
    for step in range(seq_count):
        rows = total[step * local_nodes : (step + 1) * local_nodes, :]
        if short:
            rows = jnp.concatenate([rows, jnp.zeros((short, padded), jnp.float32)], axis=0)
        for at, tile in enumerate(pack_tiles(rows, local_nodes, hands)):
            outs[step][at] = tile


def share_kernel(rows, hands, tiles_ref, out_ref, tmp, sem):
    tiles = [tiles_ref[at] for at in range(tile_count(rows, hands))]
    for at, group in enumerate(unpack_tiles(tiles, rows, hands)):
        for row in range(8 * at, min(8 * at + 8, rows)):
            tmp[row] = group[row - 8 * at : row - 8 * at + 1]
    copy = pltpu.make_async_copy(tmp, out_ref, sem)
    copy.start()
    copy.wait()


def root_kernel(rows, hands, mine_ref, other_ref, out_ref, tmp, sem):
    first = lax.rem(lax.axis_index("board"), 2) == 0
    lower = jnp.where(first, mine_ref[...], other_ref[...])
    upper = jnp.where(first, other_ref[...], mine_ref[...])
    half = mine_ref.shape[0]
    count = tile_count(rows, hands)
    tiles = [lower[at] for at in range(half)] + [upper[at] for at in range(count - half)]
    for at, group in enumerate(unpack_tiles(tiles, rows, hands)):
        height = min(8, rows - 8 * at)
        tmp[8 * at : 8 * at + height, :] = group[:height]
    copy = pltpu.make_async_copy(tmp, out_ref, sem)
    copy.start()
    copy.wait()


def body(
    board_cards, hand_ranks, river_count, reach_in, strategy, parent_node, pot_size, flop_weight
):
    seq_count = lax.axis_size("seq")
    seq_here = lax.axis_index("seq")
    board_count = lax.axis_size("board")
    rivers, local_leaves, hands = strategy.shape[1:]
    local_nodes = reach_in.shape[1]
    nodes, leaves = local_nodes * seq_count, local_leaves * seq_count
    rounds = -(-rivers // seq_count)
    padded = round_up(hands, LANES)
    anywhere = pl.BlockSpec(memory_space=pltpu.HBM)
    vmem = pl.BlockSpec(memory_space=pltpu.VMEM)
    params = pltpu.CompilerParams(vmem_limit_bytes=16 * MIB)

    def shift(array, step):
        return lax.ppermute(
            array, "seq", [(at, (at + step) % seq_count) for at in range(seq_count)]
        )

    def strategy_for(step):
        owner = (seq_here + step) % seq_count
        if rivers % seq_count == 0:
            split = strategy.reshape(rounds, seq_count, local_leaves, hands)
            rows = lax.dynamic_slice_in_dim(split, owner, 1, axis=1)
        else:
            picked = [
                lax.dynamic_slice_in_dim(
                    strategy[0], jnp.minimum(at * seq_count + owner, rivers - 1), 1, axis=0
                )
                for at in range(rounds)
            ]
            rows = jnp.concatenate(picked, axis=0)
        return rows.reshape(rounds * local_leaves, hands)

    own = strategy_for(0)
    came = [shift(strategy_for(step), step) for step in range(1, seq_count)]

    small_rows = round_up(local_nodes + 4, 16)
    info_rows = round_up(2 * rounds + 5 + local_nodes, 8)
    small, info = pl.pallas_call(
        functools.partial(pack_kernel, rounds, seq_count),
        out_shape=[
            jax.ShapeDtypeStruct((small_rows, hands), jnp.bfloat16),
            jax.ShapeDtypeStruct((info_rows, padded), jnp.float32),
        ],
        in_specs=[anywhere] * 7,
        out_specs=[anywhere] * 2,
        scratch_shapes=[
            pltpu.VMEM(reach_in.shape, jnp.bfloat16),
            pltpu.VMEM((1, local_leaves), jnp.int32),
            pltpu.VMEM((1, local_leaves), jnp.float32),
            pltpu.VMEM((rivers, 1, hands), jnp.int32),
            pltpu.SMEM((board_cards.shape[2], 1, rivers), jnp.int32),
            pltpu.SMEM((1,), jnp.int32),
            pltpu.SMEM((1,), jnp.float32),
            pltpu.VMEM((small_rows, hands), jnp.bfloat16),
            pltpu.VMEM((info_rows, padded), jnp.float32),
            pltpu.SemaphoreType.DMA((7,)),
            pltpu.SemaphoreType.DMA((2,)),
        ],
        compiler_params=pltpu.CompilerParams(vmem_limit_bytes=60 * MIB),
        name="pack",
    )(
        reach_in,
        parent_node[None],
        pot_size[None],
        hand_ranks.transpose(1, 0, 2),
        board_cards.transpose(2, 0, 1),
        river_count,
        flop_weight,
    )
    smalls = [shift(small, step) for step in range(1, seq_count)]

    payoff, info = pl.pallas_call(
        functools.partial(build_kernel, rounds),
        out_shape=[
            jax.ShapeDtypeStruct((rounds, padded, padded), jnp.bfloat16),
            jax.ShapeDtypeStruct((info_rows, padded), jnp.float32),
        ],
        in_specs=[vmem],
        out_specs=[vmem] * 2,
        scratch_shapes=[
            pltpu.VMEM((round_up(DECK, 16), padded), jnp.bfloat16),
            pltpu.VMEM((padded, padded), jnp.bfloat16),
        ],
        compiler_params=pltpu.CompilerParams(vmem_limit_bytes=30 * MIB),
        cost_estimate=pl.CostEstimate(
            flops=10 * rounds * padded * padded, bytes_accessed=4 * padded * padded, transcendentals=0
        ),
        name="build",
    )(info)

    count = tile_count(local_nodes, hands)
    *shares, weight = pl.pallas_call(
        functools.partial(value_kernel, rounds, seq_count, nodes, leaves),
        out_shape=[jax.ShapeDtypeStruct((count, 8, LANES), jnp.float32)] * seq_count
        + [jax.ShapeDtypeStruct((8, LANES), jnp.float32)],
        in_specs=[vmem] * (1 + 2 * seq_count),
        out_specs=[vmem] * (seq_count + 1),
        scratch_shapes=[
            pltpu.VMEM((nodes, padded), jnp.float32),
            pltpu.VMEM((leaves, padded), jnp.bfloat16),
        ],
        compiler_params=params,
        name="value",
    )(payoff, info, own, *came, *smalls)

    share = shares[0]
    for step in range(1, seq_count):
        share = share + shift(shares[step], -step)
    def swap(array, step):
        return lax.ppermute(array, "board", [(at, at ^ step) for at in range(board_count)])

    half = -(-count // 2)
    parity = lax.axis_index("board") % 2
    root = share * weight[None]
    if count % 2:
        root = jnp.concatenate([root, jnp.zeros((1, 8, LANES), jnp.float32)], axis=0)
    root = root.reshape(2, half, 8, LANES)
    mine = lax.dynamic_index_in_dim(root, parity, 0, keepdims=False)
    mine = mine + swap(lax.dynamic_index_in_dim(root, 1 - parity, 0, keepdims=False), 1)
    step = 2
    while step < board_count:
        mine = mine + swap(mine, step)
        step *= 2
    other = swap(mine, 1)

    turn_value = pl.pallas_call(
        functools.partial(share_kernel, local_nodes, hands),
        out_shape=jax.ShapeDtypeStruct((local_nodes, 1, hands), jnp.float32),
        in_specs=[vmem],
        out_specs=anywhere,
        scratch_shapes=[
            pltpu.VMEM((local_nodes, 1, hands), jnp.float32),
            pltpu.SemaphoreType.DMA,
        ],
        compiler_params=params,
        name="share",
    )(share)
    root_value = pl.pallas_call(
        functools.partial(root_kernel, local_nodes, hands),
        out_shape=jax.ShapeDtypeStruct((local_nodes, hands), jnp.float32),
        in_specs=[vmem] * 2,
        out_specs=anywhere,
        scratch_shapes=[pltpu.VMEM((local_nodes, hands), jnp.float32), pltpu.SemaphoreType.DMA],
        compiler_params=params,
        name="root",
    )(mine, other)
    return (turn_value.transpose(1, 0, 2), root_value)


def solution(mesh):
    return jax.shard_map(
        body,
        mesh=mesh,
        in_specs=(
            P("board", None, None),
            P("board", None, None),
            P("board"),
            P("board", "seq", None),
            P("board", None, "seq", None),
            P("seq"),
            P("seq"),
            P("board"),
        ),
        out_specs=(P("board", "seq", None), P("seq", None)),
        check_vma=False,
    )
```

```python
import functools

import jax
import jax.numpy as jnp
from jax import lax
from jax.experimental import pallas as pl
from jax.experimental.pallas import tpu as pltpu
from jax.sharding import PartitionSpec as P

DECK = 52
LANES = 128
MIB = 1024 * 1024


def round_up(value, step):
    return -(-value // step) * step


def hand_cards(padded):
    hand = lax.broadcasted_iota(jnp.int32, (1, padded), 1)
    low = jnp.zeros((1, padded), jnp.int32)
    start = jnp.zeros((1, padded), jnp.int32)
    first = 0
    for card in range(DECK - 1):
        if card:
            low = jnp.where(hand >= first, card, low)
            start = jnp.where(hand >= first, first, start)
        first += DECK - 1 - card
    high = hand - start + low + 1
    real = hand < first
    return jnp.where(real, low, -1), jnp.where(real, high, -1)


def pad_rows(rows):
    return 1 << max(rows - 1, 0).bit_length()


def tile_count(rows, hands):
    full, rest = divmod(rows, 8)
    whole, tail = divmod(hands, LANES)
    count = full * whole
    if rest:
        count += -(-whole // (8 // pad_rows(rest)))
    groups = full + (rest > 0)
    if tail:
        count += -(-groups // 2) if tail <= LANES // 2 else groups
    return count


def pack_tiles(value, rows, hands):
    full, rest = divmod(rows, 8)
    whole, tail = divmod(hands, LANES)
    tiles = [
        value[8 * group : 8 * group + 8, LANES * at : LANES * (at + 1)]
        for group in range(full)
        for at in range(whole)
    ]
    if rest:
        part = pad_rows(rest)
        each = 8 // part
        for start in range(0, whole, each):
            pieces = [
                value[8 * full : 8 * full + part, LANES * at : LANES * (at + 1)]
                for at in range(start, min(start + each, whole))
            ]
            if len(pieces) < each:
                pieces.append(jnp.zeros((8 - part * len(pieces), LANES), value.dtype))
            tiles.append(jnp.concatenate(pieces, axis=0) if len(pieces) > 1 else pieces[0])
    if tail:
        groups = full + (rest > 0)
        tails = [value[8 * group : 8 * group + 8, LANES * whole :] for group in range(groups)]
        if tail <= LANES // 2:
            for at in range(0, groups, 2):
                tile = tails[at]
                if at + 1 < groups:
                    tile = tile + pltpu.roll(tails[at + 1], LANES // 2, 1)
                tiles.append(tile)
        else:
            tiles.extend(tails)
    return tiles


def unpack_tiles(tiles, rows, hands):
    full, rest = divmod(rows, 8)
    whole, tail = divmod(hands, LANES)
    groups = [[tiles[group * whole + at] for at in range(whole)] for group in range(full)]
    used = full * whole
    if rest:
        part = pad_rows(rest)
        each = 8 // part
        last = []
        for at in range(whole):
            tile = tiles[used + at // each]
            begin = part * (at % each)
            last.append(pltpu.roll(tile, (8 - begin) % 8, 0) if begin else tile)
        used += -(-whole // each)
        groups.append(last)
    if tail:
        for at, group in enumerate(groups):
            if tail <= LANES // 2:
                tile = tiles[used + at // 2]
                if at % 2:
                    tile = pltpu.roll(tile, LANES // 2, 1)
            else:
                tile = tiles[used + at]
            group.append(tile[:, :tail])
    return [jnp.concatenate(group, axis=1) for group in groups]


def copy_all(pairs, sems):
    copies = [
        pltpu.make_async_copy(source, target, sems.at[at])
        for at, (source, target) in enumerate(pairs)
    ]
    for copy in copies:
        copy.start()
    return copies


def pack_kernel(
    rounds,
    seq_count,
    reach_ref,
    parent_ref,
    pot_ref,
    rank_ref,
    board_ref,
    count_ref,
    small_ref,
    info_ref,
    reach_tmp,
    parent_tmp,
    pot_tmp,
    rank_tmp,
    board_tmp,
    count_tmp,
    small,
    info,
    sems,
    out_sems,
):
    hands, padded = small.shape[-1], info.shape[-1]
    nodes, leaves = reach_tmp.shape[1], parent_tmp.shape[-1]
    rivers = rank_tmp.shape[0]
    here = lax.axis_index("seq")
    loads = copy_all(
        [
            (reach_ref, reach_tmp),
            (parent_ref, parent_tmp),
            (pot_ref, pot_tmp),
            (rank_ref, rank_tmp),
            (board_ref, board_tmp),
            (count_ref, count_tmp),
        ],
        sems,
    )
    low, high = hand_cards(padded)
    info[...] = jnp.zeros_like(info)
    for copy in loads[:3]:
        copy.wait()
    pot = pot_tmp[...]
    parent = parent_tmp[...].astype(jnp.float32)
    reach = reach_tmp[0].astype(jnp.float32)
    top = pot.astype(jnp.bfloat16).astype(jnp.float32)
    middle = (pot - top).astype(jnp.bfloat16).astype(jnp.float32)
    labels = jnp.concatenate([parent, top, middle, pot - top - middle], axis=0)
    rows = [reach, jnp.concatenate([labels, jnp.zeros((4, hands - leaves), jnp.float32)], axis=1)]
    extra = small.shape[0]
    if extra > nodes + 4:
        rows.append(jnp.zeros((extra - nodes - 4, hands), jnp.float32))
    small[...] = jnp.concatenate(rows, axis=0).astype(jnp.bfloat16)
    sent = pltpu.make_async_copy(small, small_ref, out_sems.at[0])
    sent.start()

    for copy in loads[3:]:
        copy.wait()
    live_count = count_tmp[0]
    base = 2 * rounds
    for at in range(rounds):
        river = jnp.minimum(at * seq_count + here, rivers - 1)
        info[at : at + 1, :hands] = rank_tmp[river].astype(jnp.float32)
        live = jnp.where(low >= 0, 1.0, 0.0)
        for slot in range(board_tmp.shape[0]):
            card = board_tmp[slot, 0, river]
            live = jnp.where((low == card) | (high == card), 0.0, live)
        info[rounds + at : rounds + at + 1, :] = live
    info[base : base + 1, :] = 1.0 / (hands * jnp.full((1, padded), live_count.astype(jnp.float32)))
    live_rounds = lax.div(live_count - here + seq_count - 1, seq_count)
    info[base + 1 : base + 2, :] = jnp.full((1, padded), live_rounds.astype(jnp.float32))
    info[base + 2 : base + 3, :leaves] = parent
    info[base + 3 : base + 4, :leaves] = pot
    info[base + 4 : base + 4 + nodes, :hands] = reach
    kept = pltpu.make_async_copy(info, info_ref, out_sems.at[1])
    kept.start()
    sent.wait()
    kept.wait()


def build_kernel(rounds, info_ref, payoff_ref, kept_ref, ranks, gaps, holds, lacks):
    padded = payoff_ref.shape[-1]
    kept_ref[...] = info_ref[...]

    low, high = hand_cards(padded)
    card = lax.broadcasted_iota(jnp.int32, (holds.shape[0], padded), 0)
    held = jnp.where((card == low) | (card == high), 1.0, 0.0)
    holds[...] = jnp.where(card == DECK, 1.0, held).astype(jnp.bfloat16)
    lacks[...] = jnp.where(card == DECK, 1.0, -held).astype(jnp.bfloat16)
    row = lax.broadcasted_iota(jnp.int32, (ranks.shape[1], padded), 0)
    for at in range(rounds):
        rank = info_ref[at : at + 1, :]
        top = jnp.floor(rank * (1.0 / LANES)) * LANES
        rest = rank - top
        sides = jnp.where(row % 2 == 0, top, rest)
        ones = jnp.where(row < 4, 1.0, 0.0)
        ranks[at] = jnp.where(row < 2, -sides, ones).astype(jnp.bfloat16)
        gaps[at] = jnp.where(row < 2, ones, jnp.where(row < 4, sides, 0.0)).astype(jnp.bfloat16)

    def product(left, right):
        return lax.dot_general(
            left, right, (((0,), (0,)), ((), ())), preferred_element_type=jnp.float32
        ).astype(jnp.bfloat16)

    for start in range(0, padded, LANES):
        rows = slice(start, start + LANES)
        for lane in range(0, padded, 2 * LANES):
            here = slice(lane, min(lane + 2 * LANES, padded))
            mask = product(holds[:, rows], lacks[:, here])
            if here.start <= start < here.stop:
                mask = jnp.maximum(mask, 0.0)
            for at in range(rounds):
                gap = product(ranks[at, :, rows], gaps[at, :, here])
                payoff_ref[at, rows, here] = jnp.maximum(jnp.minimum(gap, mask), -mask)


def value_kernel(rounds, seq_count, nodes, leaves, *refs):
    payoff_ref, info_ref, own_ref = refs[:3]
    came = refs[3 : 2 + seq_count]
    smalls = refs[2 + seq_count : 1 + 2 * seq_count]
    outs, (total, reach_all) = refs[1 + 2 * seq_count : -2], refs[-2:]
    hands = own_ref.shape[-1]
    padded = payoff_ref.shape[-1]
    local_leaves, local_nodes = leaves // seq_count, nodes // seq_count
    here = lax.axis_index("seq")
    base = 2 * rounds

    reach, places, pots = [], [], []
    for at in range(seq_count):
        if at == 0:
            reach.append(info_ref[base + 4 : base + 4 + local_nodes, :hands])
            parent = info_ref[base + 2 : base + 3, :LANES]
            pots.append(info_ref[base + 3 : base + 4, :LANES])
        else:
            small = smalls[at - 1][...].astype(jnp.float32)
            reach.append(small[:local_nodes])
            labels = small[local_nodes : local_nodes + 4, :LANES]
            parent = labels[0:1]
            pots.append(labels[1:2] + labels[2:3] + labels[3:4])
        place = parent
        for owner in range(seq_count):
            inside = (parent >= owner * local_nodes) & (parent < (owner + 1) * local_nodes)
            move = (lax.rem(here - owner + seq_count, seq_count) - owner) * local_nodes
            place = jnp.where(inside, parent + move.astype(jnp.float32), place)
        lane = lax.broadcasted_iota(jnp.int32, (1, LANES), 1)
        places.append(jnp.where(lane < local_leaves, place, -1.0))

    sub = lax.broadcasted_iota(jnp.int32, (LANES, LANES), 0)
    lane = lax.broadcasted_iota(jnp.int32, (LANES, LANES), 1)
    columns = [jnp.broadcast_to(place, (LANES, LANES)).T for place in places]
    picks = []
    pot_sorted = jnp.zeros((leaves, 1), jnp.float32)
    target = lax.broadcasted_iota(jnp.int32, (leaves, LANES), 0).astype(jnp.float32)
    for at in range(seq_count):
        nth = jnp.sum(
            jnp.where((columns[at] == places[at]) & (sub < lane), 1.0, 0.0), axis=0, keepdims=True
        )
        for before in range(at):
            nth = nth + jnp.sum(
                jnp.where(columns[before] == places[at], 1.0, 0.0), axis=0, keepdims=True
            )
        slot = jnp.where(places[at] >= 0.0, nth * nodes + places[at], -1.0)
        pick = jnp.where(target == slot, 1.0, 0.0)
        pot_sorted = pot_sorted + jnp.sum(pick * pots[at], axis=1, keepdims=True)
        picks.append(pick.astype(jnp.bfloat16)[:, :local_leaves])
    lookup = jnp.concatenate(reach * (leaves // nodes), axis=0)

    reach_all[...] = jnp.zeros_like(reach_all)
    total[...] = jnp.zeros_like(total)
    live_rounds = jnp.max(info_ref[base + 1 : base + 2, :LANES])
    for at in range(rounds):

        @pl.when(live_rounds > at)
        def _():
            rows = slice(at * local_leaves, (at + 1) * local_leaves)
            live = info_ref[rounds + at : rounds + at + 1, :]
            strat = jnp.dot(picks[0], own_ref[rows, :], preferred_element_type=jnp.float32)
            for pick, pack in zip(picks[1:], came):
                strat = strat + jnp.dot(pick, pack[rows, :], preferred_element_type=jnp.float32)
            reach_all[:, :hands] = (lookup * strat * live[:, :hands]).astype(jnp.bfloat16)
            shown = jnp.dot(reach_all[...], payoff_ref[at], preferred_element_type=jnp.float32)
            value = shown * pot_sorted
            best = value[:nodes]
            for row in range(nodes, leaves, nodes):
                best = jnp.maximum(best, value[row : row + nodes])
            gain = best * (live * info_ref[base : base + 1, :])
            total[...] += gain

    short = round_up(local_nodes, 8) - local_nodes
    for step in range(seq_count):
        rows = total[step * local_nodes : (step + 1) * local_nodes, :]
        if short:
            rows = jnp.concatenate([rows, jnp.zeros((short, padded), jnp.float32)], axis=0)
        for at, tile in enumerate(pack_tiles(rows, local_nodes, hands)):
            outs[step][at] = tile


def share_kernel(rows, hands, tiles_ref, out_ref, tmp, sem):
    tiles = [tiles_ref[at] for at in range(tile_count(rows, hands))]
    for at, group in enumerate(unpack_tiles(tiles, rows, hands)):
        for row in range(8 * at, min(8 * at + 8, rows)):
            tmp[row] = group[row - 8 * at : row - 8 * at + 1]
    copy = pltpu.make_async_copy(tmp, out_ref, sem)
    copy.start()
    copy.wait()


def root_kernel(rows, hands, mine_ref, other_ref, out_ref, tmp, sem):
    first = lax.rem(lax.axis_index("board"), 2) == 0
    lower = jnp.where(first, mine_ref[...], other_ref[...])
    upper = jnp.where(first, other_ref[...], mine_ref[...])
    half = mine_ref.shape[0]
    count = tile_count(rows, hands)
    tiles = [lower[at] for at in range(half)] + [upper[at] for at in range(count - half)]
    for at, group in enumerate(unpack_tiles(tiles, rows, hands)):
        height = min(8, rows - 8 * at)
        tmp[8 * at : 8 * at + height, :] = group[:height]
    copy = pltpu.make_async_copy(tmp, out_ref, sem)
    copy.start()
    copy.wait()


def body(
    board_cards, hand_ranks, river_count, reach_in, strategy, parent_node, pot_size, flop_weight
):
    seq_count = lax.axis_size("seq")
    seq_here = lax.axis_index("seq")
    board_count = lax.axis_size("board")
    rivers, local_leaves, hands = strategy.shape[1:]
    local_nodes = reach_in.shape[1]
    nodes, leaves = local_nodes * seq_count, local_leaves * seq_count
    rounds = -(-rivers // seq_count)
    padded = round_up(hands, LANES)
    anywhere = pl.BlockSpec(memory_space=pltpu.HBM)
    vmem = pl.BlockSpec(memory_space=pltpu.VMEM)
    params = pltpu.CompilerParams(vmem_limit_bytes=16 * MIB)

    def shift(array, step):
        return lax.ppermute(
            array, "seq", [(at, (at + step) % seq_count) for at in range(seq_count)]
        )

    def strategy_for(step):
        owner = (seq_here + step) % seq_count
        if rivers % seq_count == 0:
            split = strategy.reshape(rounds, seq_count, local_leaves, hands)
            rows = lax.dynamic_slice_in_dim(split, owner, 1, axis=1)
        else:
            picked = [
                lax.dynamic_slice_in_dim(
                    strategy[0], jnp.minimum(at * seq_count + owner, rivers - 1), 1, axis=0
                )
                for at in range(rounds)
            ]
            rows = jnp.concatenate(picked, axis=0)
        return rows.reshape(rounds * local_leaves, hands)

    own = strategy_for(0)
    came = [shift(strategy_for(step), step) for step in range(1, seq_count)]

    small_rows = round_up(local_nodes + 4, 16)
    info_rows = round_up(2 * rounds + 4 + local_nodes, 8)
    small, info = pl.pallas_call(
        functools.partial(pack_kernel, rounds, seq_count),
        out_shape=[
            jax.ShapeDtypeStruct((small_rows, hands), jnp.bfloat16),
            jax.ShapeDtypeStruct((info_rows, padded), jnp.float32),
        ],
        in_specs=[anywhere] * 6,
        out_specs=[anywhere] * 2,
        scratch_shapes=[
            pltpu.VMEM(reach_in.shape, jnp.bfloat16),
            pltpu.VMEM((1, local_leaves), jnp.int32),
            pltpu.VMEM((1, local_leaves), jnp.float32),
            pltpu.VMEM((rivers, 1, hands), jnp.int32),
            pltpu.SMEM((board_cards.shape[2], 1, rivers), jnp.int32),
            pltpu.SMEM((1,), jnp.int32),
            pltpu.VMEM((small_rows, hands), jnp.bfloat16),
            pltpu.VMEM((info_rows, padded), jnp.float32),
            pltpu.SemaphoreType.DMA((6,)),
            pltpu.SemaphoreType.DMA((2,)),
        ],
        compiler_params=pltpu.CompilerParams(vmem_limit_bytes=60 * MIB),
        name="pack",
    )(
        reach_in,
        parent_node[None],
        pot_size[None],
        hand_ranks.transpose(1, 0, 2),
        board_cards.transpose(2, 0, 1),
        river_count,
    )
    smalls = [shift(small, step) for step in range(1, seq_count)]

    payoff, info = pl.pallas_call(
        functools.partial(build_kernel, rounds),
        out_shape=[
            jax.ShapeDtypeStruct((rounds, padded, padded), jnp.bfloat16),
            jax.ShapeDtypeStruct((info_rows, padded), jnp.float32),
        ],
        in_specs=[vmem],
        out_specs=[vmem] * 2,
        scratch_shapes=[
            pltpu.VMEM((rounds, 16, padded), jnp.bfloat16),
            pltpu.VMEM((rounds, 16, padded), jnp.bfloat16),
            pltpu.VMEM((round_up(DECK + 1, 16), padded), jnp.bfloat16),
            pltpu.VMEM((round_up(DECK + 1, 16), padded), jnp.bfloat16),
        ],
        compiler_params=pltpu.CompilerParams(vmem_limit_bytes=30 * MIB),
        cost_estimate=pl.CostEstimate(
            flops=10 * rounds * padded * padded, bytes_accessed=4 * padded * padded, transcendentals=0
        ),
        name="build",
    )(info)

    count = tile_count(local_nodes, hands)
    shares = pl.pallas_call(
        functools.partial(value_kernel, rounds, seq_count, nodes, leaves),
        out_shape=[jax.ShapeDtypeStruct((count, 8, LANES), jnp.float32)] * seq_count,
        in_specs=[vmem] * (1 + 2 * seq_count),
        out_specs=[vmem] * seq_count,
        scratch_shapes=[
            pltpu.VMEM((nodes, padded), jnp.float32),
            pltpu.VMEM((leaves, padded), jnp.bfloat16),
        ],
        compiler_params=params,
        name="value",
    )(payoff, info, own, *came, *smalls)

    share = shares[0]
    for step in range(1, seq_count):
        share = share + shift(shares[step], -step)
    def swap(array, step):
        return lax.ppermute(array, "board", [(at, at ^ step) for at in range(board_count)])

    half = -(-count // 2)
    parity = lax.axis_index("board") % 2
    root = share * (flop_weight[0] / board_count)
    if count % 2:
        root = jnp.concatenate([root, jnp.zeros((1, 8, LANES), jnp.float32)], axis=0)
    root = root.reshape(2, half, 8, LANES)
    mine = lax.dynamic_index_in_dim(root, parity, 0, keepdims=False)
    mine = mine + swap(lax.dynamic_index_in_dim(root, 1 - parity, 0, keepdims=False), 1)
    step = 2
    while step < board_count:
        mine = mine + swap(mine, step)
        step *= 2
    other = swap(mine, 1)

    turn_value = pl.pallas_call(
        functools.partial(share_kernel, local_nodes, hands),
        out_shape=jax.ShapeDtypeStruct((local_nodes, 1, hands), jnp.float32),
        in_specs=[vmem],
        out_specs=anywhere,
        scratch_shapes=[
            pltpu.VMEM((local_nodes, 1, hands), jnp.float32),
            pltpu.SemaphoreType.DMA,
        ],
        compiler_params=params,
        name="share",
    )(share)
    root_value = pl.pallas_call(
        functools.partial(root_kernel, local_nodes, hands),
        out_shape=jax.ShapeDtypeStruct((local_nodes, hands), jnp.float32),
        in_specs=[vmem] * 2,
        out_specs=anywhere,
        scratch_shapes=[pltpu.VMEM((local_nodes, hands), jnp.float32), pltpu.SemaphoreType.DMA],
        compiler_params=params,
        name="root",
    )(mine, other)
    return (turn_value.transpose(1, 0, 2), root_value)


def solution(mesh):
    return jax.shard_map(
        body,
        mesh=mesh,
        in_specs=(
            P("board", None, None),
            P("board", None, None),
            P("board"),
            P("board", "seq", None),
            P("board", None, "seq", None),
            P("seq"),
            P("seq"),
            P("board"),
        ),
        out_specs=(P("board", "seq", None), P("seq", None)),
        check_vma=False,
    )
```

```python
import functools

import jax
import jax.numpy as jnp
from jax import lax
from jax.experimental import pallas as pl
from jax.experimental.pallas import tpu as pltpu
from jax.sharding import PartitionSpec as P

DECK = 52
LANES = 128
MIB = 1024 * 1024


def round_up(value, step):
    return -(-value // step) * step


def hand_cards(padded):
    hand = lax.broadcasted_iota(jnp.int32, (1, padded), 1)
    low = jnp.zeros((1, padded), jnp.int32)
    start = jnp.zeros((1, padded), jnp.int32)
    first = 0
    for card in range(DECK - 1):
        if card:
            low = jnp.where(hand >= first, card, low)
            start = jnp.where(hand >= first, first, start)
        first += DECK - 1 - card
    high = hand - start + low + 1
    real = hand < first
    return jnp.where(real, low, -1), jnp.where(real, high, -1)


def pad_rows(rows):
    return 1 << max(rows - 1, 0).bit_length()


def tile_count(rows, hands):
    full, rest = divmod(rows, 8)
    whole, tail = divmod(hands, LANES)
    count = full * whole
    if rest:
        count += -(-whole // (8 // pad_rows(rest)))
    groups = full + (rest > 0)
    if tail:
        count += -(-groups // 2) if tail <= LANES // 2 else groups
    return count


def pack_tiles(value, rows, hands):
    full, rest = divmod(rows, 8)
    whole, tail = divmod(hands, LANES)
    tiles = [
        value[8 * group : 8 * group + 8, LANES * at : LANES * (at + 1)]
        for group in range(full)
        for at in range(whole)
    ]
    if rest:
        part = pad_rows(rest)
        each = 8 // part
        for start in range(0, whole, each):
            pieces = [
                value[8 * full : 8 * full + part, LANES * at : LANES * (at + 1)]
                for at in range(start, min(start + each, whole))
            ]
            if len(pieces) < each:
                pieces.append(jnp.zeros((8 - part * len(pieces), LANES), value.dtype))
            tiles.append(jnp.concatenate(pieces, axis=0) if len(pieces) > 1 else pieces[0])
    if tail:
        groups = full + (rest > 0)
        tails = [value[8 * group : 8 * group + 8, LANES * whole :] for group in range(groups)]
        if tail <= LANES // 2:
            for at in range(0, groups, 2):
                tile = tails[at]
                if at + 1 < groups:
                    tile = tile + pltpu.roll(tails[at + 1], LANES // 2, 1)
                tiles.append(tile)
        else:
            tiles.extend(tails)
    return tiles


def unpack_tiles(tiles, rows, hands):
    full, rest = divmod(rows, 8)
    whole, tail = divmod(hands, LANES)
    groups = [[tiles[group * whole + at] for at in range(whole)] for group in range(full)]
    used = full * whole
    if rest:
        part = pad_rows(rest)
        each = 8 // part
        last = []
        for at in range(whole):
            tile = tiles[used + at // each]
            begin = part * (at % each)
            last.append(pltpu.roll(tile, (8 - begin) % 8, 0) if begin else tile)
        used += -(-whole // each)
        groups.append(last)
    if tail:
        for at, group in enumerate(groups):
            if tail <= LANES // 2:
                tile = tiles[used + at // 2]
                if at % 2:
                    tile = pltpu.roll(tile, LANES // 2, 1)
            else:
                tile = tiles[used + at]
            group.append(tile[:, :tail])
    return [jnp.concatenate(group, axis=1) for group in groups]


def copy_all(pairs, sems):
    copies = [
        pltpu.make_async_copy(source, target, sems.at[at])
        for at, (source, target) in enumerate(pairs)
    ]
    for copy in copies:
        copy.start()
    return copies


def pack_kernel(
    rounds,
    seq_count,
    reach_ref,
    parent_ref,
    pot_ref,
    rank_ref,
    board_ref,
    count_ref,
    weight_ref,
    small_ref,
    info_ref,
    reach_tmp,
    parent_tmp,
    pot_tmp,
    rank_tmp,
    board_tmp,
    count_tmp,
    weight_tmp,
    small,
    info,
    sems,
    out_sems,
):
    hands, padded = small.shape[-1], info.shape[-1]
    nodes, leaves = reach_tmp.shape[1], parent_tmp.shape[-1]
    rivers = rank_tmp.shape[0]
    here = lax.axis_index("seq")
    loads = copy_all(
        [
            (reach_ref, reach_tmp),
            (parent_ref, parent_tmp),
            (pot_ref, pot_tmp),
            (rank_ref, rank_tmp),
            (board_ref, board_tmp),
            (count_ref, count_tmp),
            (weight_ref, weight_tmp),
        ],
        sems,
    )
    low, high = hand_cards(padded)
    info[...] = jnp.zeros_like(info)
    for copy in loads[:3]:
        copy.wait()
    pot = pot_tmp[...]
    parent = parent_tmp[...].astype(jnp.float32)
    reach = reach_tmp[0].astype(jnp.float32)
    top = pot.astype(jnp.bfloat16).astype(jnp.float32)
    middle = (pot - top).astype(jnp.bfloat16).astype(jnp.float32)
    labels = jnp.concatenate([parent, top, middle, pot - top - middle], axis=0)
    rows = [reach, jnp.concatenate([labels, jnp.zeros((4, hands - leaves), jnp.float32)], axis=1)]
    extra = small.shape[0]
    if extra > nodes + 4:
        rows.append(jnp.zeros((extra - nodes - 4, hands), jnp.float32))
    small[...] = jnp.concatenate(rows, axis=0).astype(jnp.bfloat16)
    sent = pltpu.make_async_copy(small, small_ref, out_sems.at[0])
    sent.start()

    for copy in loads[3:]:
        copy.wait()
    live_count = count_tmp[0]
    base = 2 * rounds
    for at in range(rounds):
        river = jnp.minimum(at * seq_count + here, rivers - 1)
        info[at : at + 1, :hands] = rank_tmp[river].astype(jnp.float32)
        live = jnp.where(low >= 0, 1.0, 0.0)
        for slot in range(board_tmp.shape[0]):
            card = board_tmp[slot, 0, river]
            live = jnp.where((low == card) | (high == card), 0.0, live)
        info[rounds + at : rounds + at + 1, :] = live
    info[base : base + 1, :] = 1.0 / (hands * jnp.full((1, padded), live_count.astype(jnp.float32)))
    live_rounds = lax.div(live_count - here + seq_count - 1, seq_count)
    info[base + 1 : base + 2, :] = jnp.full((1, padded), live_rounds.astype(jnp.float32))
    info[base + 2 : base + 3, :leaves] = parent
    info[base + 4 + nodes : base + 5 + nodes, :] = jnp.full(
        (1, padded), weight_tmp[0] / lax.axis_size("board")
    )
    info[base + 3 : base + 4, :leaves] = pot
    info[base + 4 : base + 4 + nodes, :hands] = reach
    kept = pltpu.make_async_copy(info, info_ref, out_sems.at[1])
    kept.start()
    sent.wait()
    kept.wait()


def build_kernel(rounds, info_ref, payoff_ref, kept_ref, ranks, gaps, holds, lacks):
    padded = payoff_ref.shape[-1]
    kept_ref[...] = info_ref[...]

    low, high = hand_cards(padded)
    card = lax.broadcasted_iota(jnp.int32, (holds.shape[0], padded), 0)
    held = jnp.where((card == low) | (card == high), 1.0, 0.0)
    holds[...] = jnp.where(card == DECK, 1.0, held).astype(jnp.bfloat16)
    lacks[...] = jnp.where(card == DECK, 1.0, -held).astype(jnp.bfloat16)
    row = lax.broadcasted_iota(jnp.int32, (ranks.shape[1], padded), 0)
    for at in range(rounds):
        rank = info_ref[at : at + 1, :]
        top = jnp.floor(rank * (1.0 / LANES)) * LANES
        rest = rank - top
        sides = jnp.where(row % 2 == 0, top, rest)
        ones = jnp.where(row < 4, 1.0, 0.0)
        ranks[at] = jnp.where(row < 2, -sides, ones).astype(jnp.bfloat16)
        gaps[at] = jnp.where(row < 2, ones, jnp.where(row < 4, sides, 0.0)).astype(jnp.bfloat16)

    def product(left, right):
        return lax.dot_general(
            left, right, (((0,), (0,)), ((), ())), preferred_element_type=jnp.float32
        ).astype(jnp.bfloat16)

    for start in range(0, padded, LANES):
        rows = slice(start, start + LANES)
        for lane in range(0, padded, 2 * LANES):
            here = slice(lane, min(lane + 2 * LANES, padded))
            mask = product(holds[:, rows], lacks[:, here])
            if here.start <= start < here.stop:
                mask = jnp.maximum(mask, 0.0)
            for at in range(rounds):
                gap = product(ranks[at, :, rows], gaps[at, :, here])
                payoff_ref[at, rows, here] = jnp.maximum(jnp.minimum(gap, mask), -mask)


def value_kernel(rounds, seq_count, nodes, leaves, *refs):
    payoff_ref, info_ref, own_ref = refs[:3]
    came = refs[3 : 2 + seq_count]
    smalls = refs[2 + seq_count : 1 + 2 * seq_count]
    outs, (total, reach_all) = refs[1 + 2 * seq_count : -2], refs[-2:]
    hands = own_ref.shape[-1]
    padded = payoff_ref.shape[-1]
    local_leaves, local_nodes = leaves // seq_count, nodes // seq_count
    here = lax.axis_index("seq")
    base = 2 * rounds

    reach, places, pots = [], [], []
    for at in range(seq_count):
        if at == 0:
            reach.append(info_ref[base + 4 : base + 4 + local_nodes, :hands])
            parent = info_ref[base + 2 : base + 3, :LANES]
            pots.append(info_ref[base + 3 : base + 4, :LANES])
        else:
            small = smalls[at - 1][...].astype(jnp.float32)
            reach.append(small[:local_nodes])
            labels = small[local_nodes : local_nodes + 4, :LANES]
            parent = labels[0:1]
            pots.append(labels[1:2] + labels[2:3] + labels[3:4])
        place = parent
        for owner in range(seq_count):
            inside = (parent >= owner * local_nodes) & (parent < (owner + 1) * local_nodes)
            move = (lax.rem(here - owner + seq_count, seq_count) - owner) * local_nodes
            place = jnp.where(inside, parent + move.astype(jnp.float32), place)
        lane = lax.broadcasted_iota(jnp.int32, (1, LANES), 1)
        places.append(jnp.where(lane < local_leaves, place, -1.0))

    sub = lax.broadcasted_iota(jnp.int32, (LANES, LANES), 0)
    lane = lax.broadcasted_iota(jnp.int32, (LANES, LANES), 1)
    columns = [jnp.broadcast_to(place, (LANES, LANES)).T for place in places]
    picks = []
    pot_sorted = jnp.zeros((leaves, 1), jnp.float32)
    target = lax.broadcasted_iota(jnp.int32, (leaves, LANES), 0).astype(jnp.float32)
    for at in range(seq_count):
        nth = jnp.sum(
            jnp.where((columns[at] == places[at]) & (sub < lane), 1.0, 0.0), axis=0, keepdims=True
        )
        for before in range(at):
            nth = nth + jnp.sum(
                jnp.where(columns[before] == places[at], 1.0, 0.0), axis=0, keepdims=True
            )
        slot = jnp.where(places[at] >= 0.0, nth * nodes + places[at], -1.0)
        pick = jnp.where(target == slot, 1.0, 0.0)
        pot_sorted = pot_sorted + jnp.sum(pick * pots[at], axis=1, keepdims=True)
        picks.append(pick.astype(jnp.bfloat16)[:, :local_leaves])
    lookup = jnp.concatenate(reach * (leaves // nodes), axis=0)

    reach_all[...] = jnp.zeros_like(reach_all)
    total[...] = jnp.zeros_like(total)
    live_rounds = jnp.max(info_ref[base + 1 : base + 2, :LANES])
    for at in range(rounds):

        @pl.when(live_rounds > at)
        def _():
            rows = slice(at * local_leaves, (at + 1) * local_leaves)
            live = info_ref[rounds + at : rounds + at + 1, :]
            strat = jnp.dot(picks[0], own_ref[rows, :], preferred_element_type=jnp.float32)
            for pick, pack in zip(picks[1:], came):
                strat = strat + jnp.dot(pick, pack[rows, :], preferred_element_type=jnp.float32)
            reach_all[:, :hands] = (lookup * strat * live[:, :hands]).astype(jnp.bfloat16)
            shown = jnp.dot(reach_all[...], payoff_ref[at], preferred_element_type=jnp.float32)
            value = shown * pot_sorted
            best = value[:nodes]
            for row in range(nodes, leaves, nodes):
                best = jnp.maximum(best, value[row : row + nodes])
            gain = best * (live * info_ref[base : base + 1, :])
            total[...] += gain

    weight = info_ref[base + 4 + local_nodes : base + 5 + local_nodes, :LANES]
    short = round_up(local_nodes, 8) - local_nodes
    for step in range(seq_count):
        rows = total[step * local_nodes : (step + 1) * local_nodes, :]
        if short:
            rows = jnp.concatenate([rows, jnp.zeros((short, padded), jnp.float32)], axis=0)
        for at, tile in enumerate(pack_tiles(rows, local_nodes, hands)):
            outs[step][at] = tile
            outs[-1][step, at] = tile * weight


def share_kernel(rows, hands, tiles_ref, out_ref, tmp, sem):
    tiles = [tiles_ref[at] for at in range(tile_count(rows, hands))]
    for at, group in enumerate(unpack_tiles(tiles, rows, hands)):
        for row in range(8 * at, min(8 * at + 8, rows)):
            tmp[row] = group[row - 8 * at : row - 8 * at + 1]
    copy = pltpu.make_async_copy(tmp, out_ref, sem)
    copy.start()
    copy.wait()


def root_kernel(rows, hands, mine_ref, came_ref, out_ref, tmp, sem):
    mine = lax.rem(lax.axis_index("board"), 2) == 1
    tiles = [
        jnp.where(mine, mine_ref[at], came_ref[at]) for at in range(tile_count(rows, hands))
    ]
    for at, group in enumerate(unpack_tiles(tiles, rows, hands)):
        height = min(8, rows - 8 * at)
        tmp[8 * at : 8 * at + height, :] = group[:height]
    copy = pltpu.make_async_copy(tmp, out_ref, sem)
    copy.start()
    copy.wait()


def body(
    board_cards, hand_ranks, river_count, reach_in, strategy, parent_node, pot_size, flop_weight
):
    seq_count = lax.axis_size("seq")
    seq_here = lax.axis_index("seq")
    board_count = lax.axis_size("board")
    rivers, local_leaves, hands = strategy.shape[1:]
    local_nodes = reach_in.shape[1]
    nodes, leaves = local_nodes * seq_count, local_leaves * seq_count
    rounds = -(-rivers // seq_count)
    padded = round_up(hands, LANES)
    anywhere = pl.BlockSpec(memory_space=pltpu.HBM)
    vmem = pl.BlockSpec(memory_space=pltpu.VMEM)
    params = pltpu.CompilerParams(vmem_limit_bytes=16 * MIB)

    def shift(array, step):
        return lax.ppermute(
            array, "seq", [(at, (at + step) % seq_count) for at in range(seq_count)]
        )

    def strategy_for(step):
        owner = (seq_here + step) % seq_count
        if rivers % seq_count == 0:
            split = strategy.reshape(rounds, seq_count, local_leaves, hands)
            rows = lax.dynamic_slice_in_dim(split, owner, 1, axis=1)
        else:
            picked = [
                lax.dynamic_slice_in_dim(
                    strategy[0], jnp.minimum(at * seq_count + owner, rivers - 1), 1, axis=0
                )
                for at in range(rounds)
            ]
            rows = jnp.concatenate(picked, axis=0)
        return rows.reshape(rounds * local_leaves, hands)

    own = strategy_for(0)
    came = [shift(strategy_for(step), step) for step in range(1, seq_count)]

    small_rows = round_up(local_nodes + 4, 16)
    info_rows = round_up(2 * rounds + 5 + local_nodes, 8)
    small, info = pl.pallas_call(
        functools.partial(pack_kernel, rounds, seq_count),
        out_shape=[
            jax.ShapeDtypeStruct((small_rows, hands), jnp.bfloat16),
            jax.ShapeDtypeStruct((info_rows, padded), jnp.float32),
        ],
        in_specs=[anywhere] * 7,
        out_specs=[anywhere] * 2,
        scratch_shapes=[
            pltpu.VMEM(reach_in.shape, jnp.bfloat16),
            pltpu.VMEM((1, local_leaves), jnp.int32),
            pltpu.VMEM((1, local_leaves), jnp.float32),
            pltpu.VMEM((rivers, 1, hands), jnp.int32),
            pltpu.SMEM((board_cards.shape[2], 1, rivers), jnp.int32),
            pltpu.SMEM((1,), jnp.int32),
            pltpu.SMEM((1,), jnp.float32),
            pltpu.VMEM((small_rows, hands), jnp.bfloat16),
            pltpu.VMEM((info_rows, padded), jnp.float32),
            pltpu.SemaphoreType.DMA((7,)),
            pltpu.SemaphoreType.DMA((2,)),
        ],
        compiler_params=pltpu.CompilerParams(vmem_limit_bytes=60 * MIB),
        name="pack",
    )(
        reach_in,
        parent_node[None],
        pot_size[None],
        hand_ranks.transpose(1, 0, 2),
        board_cards.transpose(2, 0, 1),
        river_count,
        flop_weight,
    )
    smalls = [shift(small, step) for step in range(1, seq_count)]

    payoff, info = pl.pallas_call(
        functools.partial(build_kernel, rounds),
        out_shape=[
            jax.ShapeDtypeStruct((rounds, padded, padded), jnp.bfloat16),
            jax.ShapeDtypeStruct((info_rows, padded), jnp.float32),
        ],
        in_specs=[vmem],
        out_specs=[vmem] * 2,
        scratch_shapes=[
            pltpu.VMEM((rounds, 16, padded), jnp.bfloat16),
            pltpu.VMEM((rounds, 16, padded), jnp.bfloat16),
            pltpu.VMEM((round_up(DECK + 1, 16), padded), jnp.bfloat16),
            pltpu.VMEM((round_up(DECK + 1, 16), padded), jnp.bfloat16),
        ],
        compiler_params=pltpu.CompilerParams(vmem_limit_bytes=30 * MIB),
        cost_estimate=pl.CostEstimate(
            flops=10 * rounds * padded * padded, bytes_accessed=4 * padded * padded, transcendentals=0
        ),
        name="build",
    )(info)

    count = tile_count(local_nodes, hands)
    *shares, root = pl.pallas_call(
        functools.partial(value_kernel, rounds, seq_count, nodes, leaves),
        out_shape=[jax.ShapeDtypeStruct((count, 8, LANES), jnp.float32)] * seq_count
        + [jax.ShapeDtypeStruct((seq_count, count, 8, LANES), jnp.float32)],
        in_specs=[vmem] * (1 + 2 * seq_count),
        out_specs=[vmem] * (seq_count + 1),
        scratch_shapes=[
            pltpu.VMEM((nodes, padded), jnp.float32),
            pltpu.VMEM((leaves, padded), jnp.bfloat16),
        ],
        compiler_params=params,
        name="value",
    )(payoff, info, own, *came, *smalls)

    odd = range(1, board_count, 2)
    root = root + lax.ppermute(root, "board", [(at - 1, at) for at in odd])
    parts = root
    root = parts[0]
    for step in range(1, seq_count):
        pairs = [
            (at * seq_count + seq, at * seq_count + (seq - step) % seq_count)
            for at in odd
            for seq in range(seq_count)
        ]
        root = root + lax.ppermute(parts[step], ("board", "seq"), pairs)

    *rest, root = lax.optimization_barrier((*shares[1:], root))
    share = shares[0]
    for step, block in enumerate(rest, 1):
        share = share + shift(block, -step)
    step = 2
    while step < board_count:
        root = root + lax.ppermute(root, "board", [(at, at ^ step) for at in odd])
        step *= 2
    came = lax.ppermute(root, "board", [(at, at - 1) for at in odd])

    turn_value = pl.pallas_call(
        functools.partial(share_kernel, local_nodes, hands),
        out_shape=jax.ShapeDtypeStruct((local_nodes, 1, hands), jnp.float32),
        in_specs=[vmem],
        out_specs=anywhere,
        scratch_shapes=[
            pltpu.VMEM((local_nodes, 1, hands), jnp.float32),
            pltpu.SemaphoreType.DMA,
        ],
        compiler_params=params,
        name="share",
    )(share)
    root_value = pl.pallas_call(
        functools.partial(root_kernel, local_nodes, hands),
        out_shape=jax.ShapeDtypeStruct((local_nodes, hands), jnp.float32),
        in_specs=[vmem] * 2,
        out_specs=anywhere,
        scratch_shapes=[pltpu.VMEM((local_nodes, hands), jnp.float32), pltpu.SemaphoreType.DMA],
        compiler_params=params,
        name="root",
    )(root, came)
    return (turn_value.transpose(1, 0, 2), root_value)


def solution(mesh):
    return jax.shard_map(
        body,
        mesh=mesh,
        in_specs=(
            P("board", None, None),
            P("board", None, None),
            P("board"),
            P("board", "seq", None),
            P("board", None, "seq", None),
            P("seq"),
            P("seq"),
            P("board"),
        ),
        out_specs=(P("board", "seq", None), P("seq", None)),
        check_vma=False,
    )
```

```python
import functools

import jax
import jax.numpy as jnp
from jax import lax
from jax.experimental import pallas as pl
from jax.experimental.pallas import tpu as pltpu
from jax.sharding import PartitionSpec as P

DECK = 52
LANES = 128
MIB = 1024 * 1024


def round_up(value, step):
    return -(-value // step) * step


def hand_cards(padded):
    hand = lax.broadcasted_iota(jnp.int32, (1, padded), 1)
    low = jnp.zeros((1, padded), jnp.int32)
    start = jnp.zeros((1, padded), jnp.int32)
    first = 0
    for card in range(DECK - 1):
        if card:
            low = jnp.where(hand >= first, card, low)
            start = jnp.where(hand >= first, first, start)
        first += DECK - 1 - card
    high = hand - start + low + 1
    real = hand < first
    return jnp.where(real, low, -1), jnp.where(real, high, -1)


def pad_rows(rows):
    return 1 << max(rows - 1, 0).bit_length()


def tile_count(rows, hands):
    full, rest = divmod(rows, 8)
    whole, tail = divmod(hands, LANES)
    count = full * whole
    if rest:
        count += -(-whole // (8 // pad_rows(rest)))
    groups = full + (rest > 0)
    if tail:
        count += -(-groups // 2) if tail <= LANES // 2 else groups
    return count


def pack_tiles(value, rows, hands):
    full, rest = divmod(rows, 8)
    whole, tail = divmod(hands, LANES)
    tiles = [
        value[8 * group : 8 * group + 8, LANES * at : LANES * (at + 1)]
        for group in range(full)
        for at in range(whole)
    ]
    if rest:
        part = pad_rows(rest)
        each = 8 // part
        for start in range(0, whole, each):
            pieces = [
                value[8 * full : 8 * full + part, LANES * at : LANES * (at + 1)]
                for at in range(start, min(start + each, whole))
            ]
            if len(pieces) < each:
                pieces.append(jnp.zeros((8 - part * len(pieces), LANES), value.dtype))
            tiles.append(jnp.concatenate(pieces, axis=0) if len(pieces) > 1 else pieces[0])
    if tail:
        groups = full + (rest > 0)
        tails = [value[8 * group : 8 * group + 8, LANES * whole :] for group in range(groups)]
        if tail <= LANES // 2:
            for at in range(0, groups, 2):
                tile = tails[at]
                if at + 1 < groups:
                    tile = tile + pltpu.roll(tails[at + 1], LANES // 2, 1)
                tiles.append(tile)
        else:
            tiles.extend(tails)
    return tiles


def unpack_tiles(tiles, rows, hands):
    full, rest = divmod(rows, 8)
    whole, tail = divmod(hands, LANES)
    groups = [[tiles[group * whole + at] for at in range(whole)] for group in range(full)]
    used = full * whole
    if rest:
        part = pad_rows(rest)
        each = 8 // part
        last = []
        for at in range(whole):
            tile = tiles[used + at // each]
            begin = part * (at % each)
            last.append(pltpu.roll(tile, (8 - begin) % 8, 0) if begin else tile)
        used += -(-whole // each)
        groups.append(last)
    if tail:
        for at, group in enumerate(groups):
            if tail <= LANES // 2:
                tile = tiles[used + at // 2]
                if at % 2:
                    tile = pltpu.roll(tile, LANES // 2, 1)
            else:
                tile = tiles[used + at]
            group.append(tile[:, :tail])
    return [jnp.concatenate(group, axis=1) for group in groups]


def copy_all(pairs, sems):
    copies = [
        pltpu.make_async_copy(source, target, sems.at[at])
        for at, (source, target) in enumerate(pairs)
    ]
    for copy in copies:
        copy.start()
    return copies


def pack_kernel(
    rounds,
    seq_count,
    reach_ref,
    parent_ref,
    pot_ref,
    rank_ref,
    board_ref,
    count_ref,
    weight_ref,
    small_ref,
    info_ref,
    reach_tmp,
    parent_tmp,
    pot_tmp,
    rank_tmp,
    board_tmp,
    count_tmp,
    weight_tmp,
    small,
    info,
    sems,
    out_sems,
):
    hands, padded = small.shape[-1], info.shape[-1]
    nodes, leaves = reach_tmp.shape[1], parent_tmp.shape[-1]
    rivers = rank_tmp.shape[0]
    here = lax.axis_index("seq")
    loads = copy_all(
        [
            (reach_ref, reach_tmp),
            (parent_ref, parent_tmp),
            (pot_ref, pot_tmp),
            (rank_ref, rank_tmp),
            (board_ref, board_tmp),
            (count_ref, count_tmp),
            (weight_ref, weight_tmp),
        ],
        sems,
    )
    low, high = hand_cards(padded)
    info[...] = jnp.zeros_like(info)
    for copy in loads[:3]:
        copy.wait()
    pot = pot_tmp[...]
    parent = parent_tmp[...].astype(jnp.float32)
    reach = reach_tmp[0].astype(jnp.float32)
    top = pot.astype(jnp.bfloat16).astype(jnp.float32)
    middle = (pot - top).astype(jnp.bfloat16).astype(jnp.float32)
    labels = jnp.concatenate([parent, top, middle, pot - top - middle], axis=0)
    rows = [reach, jnp.concatenate([labels, jnp.zeros((4, hands - leaves), jnp.float32)], axis=1)]
    extra = small.shape[0]
    if extra > nodes + 4:
        rows.append(jnp.zeros((extra - nodes - 4, hands), jnp.float32))
    small[...] = jnp.concatenate(rows, axis=0).astype(jnp.bfloat16)
    sent = pltpu.make_async_copy(small, small_ref, out_sems.at[0])
    sent.start()

    for copy in loads[3:]:
        copy.wait()
    live_count = count_tmp[0]
    base = 2 * rounds
    for at in range(rounds):
        river = jnp.minimum(at * seq_count + here, rivers - 1)
        info[at : at + 1, :hands] = rank_tmp[river].astype(jnp.float32)
        live = jnp.where(low >= 0, 1.0, 0.0)
        for slot in range(board_tmp.shape[0]):
            card = board_tmp[slot, 0, river]
            live = jnp.where((low == card) | (high == card), 0.0, live)
        info[rounds + at : rounds + at + 1, :] = live
    info[base : base + 1, :] = 1.0 / (hands * jnp.full((1, padded), live_count.astype(jnp.float32)))
    live_rounds = lax.div(live_count - here + seq_count - 1, seq_count)
    info[base + 1 : base + 2, :] = jnp.full((1, padded), live_rounds.astype(jnp.float32))
    info[base + 2 : base + 3, :leaves] = parent
    info[base + 4 + nodes : base + 5 + nodes, :] = jnp.full(
        (1, padded), weight_tmp[0] / lax.axis_size("board")
    )
    info[base + 3 : base + 4, :leaves] = pot
    info[base + 4 : base + 4 + nodes, :hands] = reach
    kept = pltpu.make_async_copy(info, info_ref, out_sems.at[1])
    kept.start()
    sent.wait()
    kept.wait()


def build_kernel(rounds, info_ref, payoff_ref, kept_ref, ranks, gaps, holds, lacks):
    padded = payoff_ref.shape[-1]
    kept_ref[...] = info_ref[...]

    low, high = hand_cards(padded)
    card = lax.broadcasted_iota(jnp.int32, (holds.shape[0], padded), 0)
    held = jnp.where((card == low) | (card == high), 1.0, 0.0)
    holds[...] = jnp.where(card == DECK, 1.0, held).astype(jnp.bfloat16)
    lacks[...] = jnp.where(card == DECK, 1.0, -held).astype(jnp.bfloat16)
    row = lax.broadcasted_iota(jnp.int32, (ranks.shape[1], padded), 0)
    for at in range(rounds):
        rank = info_ref[at : at + 1, :]
        top = jnp.floor(rank * (1.0 / LANES)) * LANES
        rest = rank - top
        sides = jnp.where(row % 2 == 0, top, rest)
        ones = jnp.where(row < 4, 1.0, 0.0)
        ranks[at] = jnp.where(row < 2, -sides, ones).astype(jnp.bfloat16)
        gaps[at] = jnp.where(row < 2, ones, jnp.where(row < 4, sides, 0.0)).astype(jnp.bfloat16)

    def product(left, right):
        return lax.dot_general(
            left, right, (((0,), (0,)), ((), ())), preferred_element_type=jnp.float32
        ).astype(jnp.bfloat16)

    for start in range(0, padded, LANES):
        rows = slice(start, start + LANES)
        for lane in range(0, padded, 2 * LANES):
            here = slice(lane, min(lane + 2 * LANES, padded))
            mask = product(holds[:, rows], lacks[:, here])
            if here.start <= start < here.stop:
                mask = jnp.maximum(mask, 0.0)
            for at in range(rounds):
                gap = product(ranks[at, :, rows], gaps[at, :, here])
                payoff_ref[at, rows, here] = jnp.maximum(jnp.minimum(gap, mask), -mask)


def value_kernel(rounds, seq_count, nodes, leaves, *refs):
    payoff_ref, info_ref, own_ref = refs[:3]
    came = refs[3 : 2 + seq_count]
    smalls = refs[2 + seq_count : 1 + 2 * seq_count]
    outs, (total, reach_all) = refs[1 + 2 * seq_count : -2], refs[-2:]
    hands = own_ref.shape[-1]
    padded = payoff_ref.shape[-1]
    local_leaves, local_nodes = leaves // seq_count, nodes // seq_count
    here = lax.axis_index("seq")
    base = 2 * rounds

    reach, places, pots = [], [], []
    for at in range(seq_count):
        if at == 0:
            reach.append(info_ref[base + 4 : base + 4 + local_nodes, :hands])
            parent = info_ref[base + 2 : base + 3, :LANES]
            pots.append(info_ref[base + 3 : base + 4, :LANES])
        else:
            small = smalls[at - 1][...].astype(jnp.float32)
            reach.append(small[:local_nodes])
            labels = small[local_nodes : local_nodes + 4, :LANES]
            parent = labels[0:1]
            pots.append(labels[1:2] + labels[2:3] + labels[3:4])
        place = parent
        for owner in range(seq_count):
            inside = (parent >= owner * local_nodes) & (parent < (owner + 1) * local_nodes)
            move = (lax.rem(here - owner + seq_count, seq_count) - owner) * local_nodes
            place = jnp.where(inside, parent + move.astype(jnp.float32), place)
        lane = lax.broadcasted_iota(jnp.int32, (1, LANES), 1)
        places.append(jnp.where(lane < local_leaves, place, -1.0))

    sub = lax.broadcasted_iota(jnp.int32, (LANES, LANES), 0)
    lane = lax.broadcasted_iota(jnp.int32, (LANES, LANES), 1)
    columns = [jnp.broadcast_to(place, (LANES, LANES)).T for place in places]
    picks = []
    pot_sorted = jnp.zeros((leaves, 1), jnp.float32)
    target = lax.broadcasted_iota(jnp.int32, (leaves, LANES), 0).astype(jnp.float32)
    for at in range(seq_count):
        nth = jnp.sum(
            jnp.where((columns[at] == places[at]) & (sub < lane), 1.0, 0.0), axis=0, keepdims=True
        )
        for before in range(at):
            nth = nth + jnp.sum(
                jnp.where(columns[before] == places[at], 1.0, 0.0), axis=0, keepdims=True
            )
        slot = jnp.where(places[at] >= 0.0, nth * nodes + places[at], -1.0)
        pick = jnp.where(target == slot, 1.0, 0.0)
        pot_sorted = pot_sorted + jnp.sum(pick * pots[at], axis=1, keepdims=True)
        picks.append(pick.astype(jnp.bfloat16)[:, :local_leaves])
    lookup = jnp.concatenate(reach * (leaves // nodes), axis=0)

    reach_all[...] = jnp.zeros_like(reach_all)
    total[...] = jnp.zeros_like(total)
    live_rounds = jnp.max(info_ref[base + 1 : base + 2, :LANES])
    for at in range(rounds):

        @pl.when(live_rounds > at)
        def _():
            rows = slice(at * local_leaves, (at + 1) * local_leaves)
            live = info_ref[rounds + at : rounds + at + 1, :]
            strat = jnp.dot(picks[0], own_ref[rows, :], preferred_element_type=jnp.float32)
            for pick, pack in zip(picks[1:], came):
                strat = strat + jnp.dot(pick, pack[rows, :], preferred_element_type=jnp.float32)
            reach_all[:, :hands] = (lookup * strat * live[:, :hands]).astype(jnp.bfloat16)
            shown = jnp.dot(reach_all[...], payoff_ref[at], preferred_element_type=jnp.float32)
            value = shown * pot_sorted
            best = value[:nodes]
            for row in range(nodes, leaves, nodes):
                best = jnp.maximum(best, value[row : row + nodes])
            gain = best * (live * info_ref[base : base + 1, :])
            total[...] += gain

    weight = info_ref[base + 4 + local_nodes : base + 5 + local_nodes, :LANES]
    short = round_up(local_nodes, 8) - local_nodes
    for step in range(seq_count):
        rows = total[step * local_nodes : (step + 1) * local_nodes, :]
        if short:
            rows = jnp.concatenate([rows, jnp.zeros((short, padded), jnp.float32)], axis=0)
        for at, tile in enumerate(pack_tiles(rows, local_nodes, hands)):
            outs[step][at] = tile
            outs[-1][step, at] = tile * weight


def share_kernel(rows, hands, tiles_ref, out_ref, tmp, sem):
    tiles = [tiles_ref[at] for at in range(tile_count(rows, hands))]
    for at, group in enumerate(unpack_tiles(tiles, rows, hands)):
        for row in range(8 * at, min(8 * at + 8, rows)):
            tmp[row] = group[row - 8 * at : row - 8 * at + 1]
    copy = pltpu.make_async_copy(tmp, out_ref, sem)
    copy.start()
    copy.wait()


def root_kernel(rows, hands, mine_ref, came_ref, out_ref, tmp, sem):
    mine = lax.rem(lax.axis_index("board"), 2) == 1
    tiles = [
        jnp.where(mine, mine_ref[at], came_ref[at]) for at in range(tile_count(rows, hands))
    ]
    for at, group in enumerate(unpack_tiles(tiles, rows, hands)):
        height = min(8, rows - 8 * at)
        tmp[8 * at : 8 * at + height, :] = group[:height]
    copy = pltpu.make_async_copy(tmp, out_ref, sem)
    copy.start()
    copy.wait()


def body(
    board_cards, hand_ranks, river_count, reach_in, strategy, parent_node, pot_size, flop_weight
):
    seq_count = lax.axis_size("seq")
    seq_here = lax.axis_index("seq")
    board_count = lax.axis_size("board")
    rivers, local_leaves, hands = strategy.shape[1:]
    local_nodes = reach_in.shape[1]
    nodes, leaves = local_nodes * seq_count, local_leaves * seq_count
    rounds = -(-rivers // seq_count)
    padded = round_up(hands, LANES)
    anywhere = pl.BlockSpec(memory_space=pltpu.HBM)
    vmem = pl.BlockSpec(memory_space=pltpu.VMEM)
    params = pltpu.CompilerParams(vmem_limit_bytes=16 * MIB)

    def shift(array, step):
        return lax.ppermute(
            array, "seq", [(at, (at + step) % seq_count) for at in range(seq_count)]
        )

    def strategy_for(step):
        owner = (seq_here + step) % seq_count
        if rivers % seq_count == 0:
            split = strategy.reshape(rounds, seq_count, local_leaves, hands)
            rows = lax.dynamic_slice_in_dim(split, owner, 1, axis=1)
        else:
            picked = [
                lax.dynamic_slice_in_dim(
                    strategy[0], jnp.minimum(at * seq_count + owner, rivers - 1), 1, axis=0
                )
                for at in range(rounds)
            ]
            rows = jnp.concatenate(picked, axis=0)
        return rows.reshape(rounds * local_leaves, hands)

    own = strategy_for(0)
    came = [shift(strategy_for(step), step) for step in range(1, seq_count)]

    small_rows = round_up(local_nodes + 4, 16)
    info_rows = round_up(2 * rounds + 5 + local_nodes, 8)
    small, info = pl.pallas_call(
        functools.partial(pack_kernel, rounds, seq_count),
        out_shape=[
            jax.ShapeDtypeStruct((small_rows, hands), jnp.bfloat16),
            jax.ShapeDtypeStruct((info_rows, padded), jnp.float32),
        ],
        in_specs=[anywhere] * 7,
        out_specs=[anywhere] * 2,
        scratch_shapes=[
            pltpu.VMEM(reach_in.shape, jnp.bfloat16),
            pltpu.VMEM((1, local_leaves), jnp.int32),
            pltpu.VMEM((1, local_leaves), jnp.float32),
            pltpu.VMEM((rivers, 1, hands), jnp.int32),
            pltpu.SMEM((board_cards.shape[2], 1, rivers), jnp.int32),
            pltpu.SMEM((1,), jnp.int32),
            pltpu.SMEM((1,), jnp.float32),
            pltpu.VMEM((small_rows, hands), jnp.bfloat16),
            pltpu.VMEM((info_rows, padded), jnp.float32),
            pltpu.SemaphoreType.DMA((7,)),
            pltpu.SemaphoreType.DMA((2,)),
        ],
        compiler_params=pltpu.CompilerParams(vmem_limit_bytes=60 * MIB),
        name="pack",
    )(
        reach_in,
        parent_node[None],
        pot_size[None],
        hand_ranks.transpose(1, 0, 2),
        board_cards.transpose(2, 0, 1),
        river_count,
        flop_weight,
    )
    smalls = [shift(small, step) for step in range(1, seq_count)]

    payoff, info = pl.pallas_call(
        functools.partial(build_kernel, rounds),
        out_shape=[
            jax.ShapeDtypeStruct((rounds, padded, padded), jnp.bfloat16),
            jax.ShapeDtypeStruct((info_rows, padded), jnp.float32),
        ],
        in_specs=[vmem],
        out_specs=[vmem] * 2,
        scratch_shapes=[
            pltpu.VMEM((rounds, 16, padded), jnp.bfloat16),
            pltpu.VMEM((rounds, 16, padded), jnp.bfloat16),
            pltpu.VMEM((round_up(DECK + 1, 16), padded), jnp.bfloat16),
            pltpu.VMEM((round_up(DECK + 1, 16), padded), jnp.bfloat16),
        ],
        compiler_params=pltpu.CompilerParams(vmem_limit_bytes=30 * MIB),
        cost_estimate=pl.CostEstimate(
            flops=10 * rounds * padded * padded, bytes_accessed=4 * padded * padded, transcendentals=0
        ),
        name="build",
    )(info)

    count = tile_count(local_nodes, hands)
    *shares, root = pl.pallas_call(
        functools.partial(value_kernel, rounds, seq_count, nodes, leaves),
        out_shape=[jax.ShapeDtypeStruct((count, 8, LANES), jnp.float32)] * seq_count
        + [jax.ShapeDtypeStruct((seq_count, count, 8, LANES), jnp.float32)],
        in_specs=[vmem] * (1 + 2 * seq_count),
        out_specs=[vmem] * (seq_count + 1),
        scratch_shapes=[
            pltpu.VMEM((nodes, padded), jnp.float32),
            pltpu.VMEM((leaves, padded), jnp.bfloat16),
        ],
        compiler_params=params,
        name="value",
    )(payoff, info, own, *came, *smalls)

    boards = range(board_count)

    def swap(array, step):
        return lax.ppermute(array, "board", [(at, at ^ step) for at in boards])

    parts = root + swap(root, 1)
    root = parts[0]
    for step in range(1, seq_count):
        pairs = [
            (at * seq_count + seq, at * seq_count + (seq - step * (at % 2)) % seq_count)
            for at in boards
            for seq in range(seq_count)
        ]
        root = root + lax.ppermute(parts[step], ("board", "seq"), pairs)

    *rest, root = lax.optimization_barrier((*shares[1:], root))
    share = shares[0]
    for step, block in enumerate(rest, 1):
        share = share + shift(block, -step)
    step = 2
    while step < board_count:
        pairs = [(at, at ^ step if at % 2 else at) for at in boards]
        root = root + lax.ppermute(root, "board", pairs)
        step *= 2
    came = swap(root, 1)

    turn_value = pl.pallas_call(
        functools.partial(share_kernel, local_nodes, hands),
        out_shape=jax.ShapeDtypeStruct((local_nodes, 1, hands), jnp.float32),
        in_specs=[vmem],
        out_specs=anywhere,
        scratch_shapes=[
            pltpu.VMEM((local_nodes, 1, hands), jnp.float32),
            pltpu.SemaphoreType.DMA,
        ],
        compiler_params=params,
        name="share",
    )(share)
    root_value = pl.pallas_call(
        functools.partial(root_kernel, local_nodes, hands),
        out_shape=jax.ShapeDtypeStruct((local_nodes, hands), jnp.float32),
        in_specs=[vmem] * 2,
        out_specs=anywhere,
        scratch_shapes=[pltpu.VMEM((local_nodes, hands), jnp.float32), pltpu.SemaphoreType.DMA],
        compiler_params=params,
        name="root",
    )(root, came)
    return (turn_value.transpose(1, 0, 2), root_value)


def solution(mesh):
    return jax.shard_map(
        body,
        mesh=mesh,
        in_specs=(
            P("board", None, None),
            P("board", None, None),
            P("board"),
            P("board", "seq", None),
            P("board", None, "seq", None),
            P("seq"),
            P("seq"),
            P("board"),
        ),
        out_specs=(P("board", "seq", None), P("seq", None)),
        check_vma=False,
    )
```

```python
import functools

import jax
import jax.numpy as jnp
from jax import lax
from jax.experimental import pallas as pl
from jax.experimental.pallas import tpu as pltpu
from jax.sharding import PartitionSpec as P

DECK = 52
LANES = 128
MIB = 1024 * 1024


def round_up(value, step):
    return -(-value // step) * step


def hand_cards(padded):
    hand = lax.broadcasted_iota(jnp.int32, (1, padded), 1)
    low = jnp.zeros((1, padded), jnp.int32)
    start = jnp.zeros((1, padded), jnp.int32)
    first = 0
    for card in range(DECK - 1):
        if card:
            low = jnp.where(hand >= first, card, low)
            start = jnp.where(hand >= first, first, start)
        first += DECK - 1 - card
    high = hand - start + low + 1
    real = hand < first
    return jnp.where(real, low, -1), jnp.where(real, high, -1)


def pad_rows(rows):
    return 1 << max(rows - 1, 0).bit_length()


def tile_count(rows, hands):
    full, rest = divmod(rows, 8)
    whole, tail = divmod(hands, LANES)
    count = full * whole
    if rest:
        count += -(-whole // (8 // pad_rows(rest)))
    groups = full + (rest > 0)
    if tail:
        count += -(-groups // 2) if tail <= LANES // 2 else groups
    return count


def pack_tiles(value, rows, hands):
    full, rest = divmod(rows, 8)
    whole, tail = divmod(hands, LANES)
    tiles = [
        value[8 * group : 8 * group + 8, LANES * at : LANES * (at + 1)]
        for group in range(full)
        for at in range(whole)
    ]
    if rest:
        part = pad_rows(rest)
        each = 8 // part
        for start in range(0, whole, each):
            pieces = [
                value[8 * full : 8 * full + part, LANES * at : LANES * (at + 1)]
                for at in range(start, min(start + each, whole))
            ]
            if len(pieces) < each:
                pieces.append(jnp.zeros((8 - part * len(pieces), LANES), value.dtype))
            tiles.append(jnp.concatenate(pieces, axis=0) if len(pieces) > 1 else pieces[0])
    if tail:
        groups = full + (rest > 0)
        tails = [value[8 * group : 8 * group + 8, LANES * whole :] for group in range(groups)]
        if tail <= LANES // 2:
            for at in range(0, groups, 2):
                tile = tails[at]
                if at + 1 < groups:
                    tile = tile + pltpu.roll(tails[at + 1], LANES // 2, 1)
                tiles.append(tile)
        else:
            tiles.extend(tails)
    return tiles


def unpack_tiles(tiles, rows, hands):
    full, rest = divmod(rows, 8)
    whole, tail = divmod(hands, LANES)
    groups = [[tiles[group * whole + at] for at in range(whole)] for group in range(full)]
    used = full * whole
    if rest:
        part = pad_rows(rest)
        each = 8 // part
        last = []
        for at in range(whole):
            tile = tiles[used + at // each]
            begin = part * (at % each)
            last.append(pltpu.roll(tile, (8 - begin) % 8, 0) if begin else tile)
        used += -(-whole // each)
        groups.append(last)
    if tail:
        for at, group in enumerate(groups):
            if tail <= LANES // 2:
                tile = tiles[used + at // 2]
                if at % 2:
                    tile = pltpu.roll(tile, LANES // 2, 1)
            else:
                tile = tiles[used + at]
            group.append(tile[:, :tail])
    return [jnp.concatenate(group, axis=1) for group in groups]


def copy_all(pairs, sems):
    copies = [
        pltpu.make_async_copy(source, target, sems.at[at])
        for at, (source, target) in enumerate(pairs)
    ]
    for copy in copies:
        copy.start()
    return copies


def pack_kernel(
    rounds,
    seq_count,
    reach_ref,
    parent_ref,
    pot_ref,
    rank_ref,
    board_ref,
    count_ref,
    small_ref,
    info_ref,
    reach_tmp,
    parent_tmp,
    pot_tmp,
    rank_tmp,
    board_tmp,
    count_tmp,
    small,
    info,
    sems,
    out_sems,
):
    hands, padded = small.shape[-1], info.shape[-1]
    nodes, leaves = reach_tmp.shape[1], parent_tmp.shape[-1]
    rivers = rank_tmp.shape[0]
    here = lax.axis_index("seq")
    loads = copy_all(
        [
            (reach_ref, reach_tmp),
            (parent_ref, parent_tmp),
            (pot_ref, pot_tmp),
            (rank_ref, rank_tmp),
            (board_ref, board_tmp),
            (count_ref, count_tmp),
        ],
        sems,
    )
    low, high = hand_cards(padded)
    info[...] = jnp.zeros_like(info)
    for copy in loads[:3]:
        copy.wait()
    pot = pot_tmp[...]
    parent = parent_tmp[...].astype(jnp.float32)
    reach = reach_tmp[0].astype(jnp.float32)
    top = pot.astype(jnp.bfloat16).astype(jnp.float32)
    middle = (pot - top).astype(jnp.bfloat16).astype(jnp.float32)
    labels = jnp.concatenate([parent, top, middle, pot - top - middle], axis=0)
    rows = [reach, jnp.concatenate([labels, jnp.zeros((4, hands - leaves), jnp.float32)], axis=1)]
    extra = small.shape[0]
    if extra > nodes + 4:
        rows.append(jnp.zeros((extra - nodes - 4, hands), jnp.float32))
    small[...] = jnp.concatenate(rows, axis=0).astype(jnp.bfloat16)
    sent = pltpu.make_async_copy(small, small_ref, out_sems.at[0])
    sent.start()

    for copy in loads[3:]:
        copy.wait()
    live_count = count_tmp[0]
    base = 2 * rounds
    for at in range(rounds):
        river = jnp.minimum(at * seq_count + here, rivers - 1)
        info[at : at + 1, :hands] = rank_tmp[river].astype(jnp.float32)
        live = jnp.where(low >= 0, 1.0, 0.0)
        for slot in range(board_tmp.shape[0]):
            card = board_tmp[slot, 0, river]
            live = jnp.where((low == card) | (high == card), 0.0, live)
        info[rounds + at : rounds + at + 1, :] = live
    info[base : base + 1, :] = 1.0 / (hands * jnp.full((1, padded), live_count.astype(jnp.float32)))
    live_rounds = lax.div(live_count - here + seq_count - 1, seq_count)
    info[base + 1 : base + 2, :] = jnp.full((1, padded), live_rounds.astype(jnp.float32))
    info[base + 2 : base + 3, :leaves] = parent
    info[base + 3 : base + 4, :leaves] = pot
    info[base + 4 : base + 4 + nodes, :hands] = reach
    kept = pltpu.make_async_copy(info, info_ref, out_sems.at[1])
    kept.start()
    sent.wait()
    kept.wait()


def build_kernel(rounds, info_ref, payoff_ref, kept_ref, ranks, gaps, holds, lacks):
    padded = payoff_ref.shape[-1]
    kept_ref[...] = info_ref[...]

    low, high = hand_cards(padded)
    card = lax.broadcasted_iota(jnp.int32, (holds.shape[0], padded), 0)
    held = jnp.where((card == low) | (card == high), 1.0, 0.0)
    holds[...] = jnp.where(card == DECK, 1.0, held).astype(jnp.bfloat16)
    lacks[...] = jnp.where(card == DECK, 1.0, -held).astype(jnp.bfloat16)
    row = lax.broadcasted_iota(jnp.int32, (ranks.shape[1], padded), 0)
    for at in range(rounds):
        rank = info_ref[at : at + 1, :]
        top = jnp.floor(rank * (1.0 / LANES)) * LANES
        rest = rank - top
        sides = jnp.where(row % 2 == 0, top, rest)
        ones = jnp.where(row < 4, 1.0, 0.0)
        ranks[at] = jnp.where(row < 2, -sides, ones).astype(jnp.bfloat16)
        gaps[at] = jnp.where(row < 2, ones, jnp.where(row < 4, sides, 0.0)).astype(jnp.bfloat16)

    def product(left, right):
        return lax.dot_general(
            left, right, (((0,), (0,)), ((), ())), preferred_element_type=jnp.float32
        ).astype(jnp.bfloat16)

    for start in range(0, padded, LANES):
        rows = slice(start, start + LANES)
        for lane in range(0, padded, 2 * LANES):
            here = slice(lane, min(lane + 2 * LANES, padded))
            mask = product(holds[:, rows], lacks[:, here])
            if here.start <= start < here.stop:
                mask = jnp.maximum(mask, 0.0)
            for at in range(rounds):
                gap = product(ranks[at, :, rows], gaps[at, :, here])
                payoff_ref[at, rows, here] = jnp.maximum(jnp.minimum(gap, mask), -mask)


def value_kernel(rounds, seq_count, nodes, leaves, *refs):
    payoff_ref, info_ref, own_ref = refs[:3]
    came = refs[3 : 2 + seq_count]
    smalls = refs[2 + seq_count : 1 + 2 * seq_count]
    outs, (total, reach_all) = refs[1 + 2 * seq_count : -2], refs[-2:]
    hands = own_ref.shape[-1]
    padded = payoff_ref.shape[-1]
    local_leaves, local_nodes = leaves // seq_count, nodes // seq_count
    here = lax.axis_index("seq")
    base = 2 * rounds

    reach, places, pots = [], [], []
    for at in range(seq_count):
        if at == 0:
            reach.append(info_ref[base + 4 : base + 4 + local_nodes, :hands])
            parent = info_ref[base + 2 : base + 3, :LANES]
            pots.append(info_ref[base + 3 : base + 4, :LANES])
        else:
            small = smalls[at - 1][...].astype(jnp.float32)
            reach.append(small[:local_nodes])
            labels = small[local_nodes : local_nodes + 4, :LANES]
            parent = labels[0:1]
            pots.append(labels[1:2] + labels[2:3] + labels[3:4])
        place = parent
        for owner in range(seq_count):
            inside = (parent >= owner * local_nodes) & (parent < (owner + 1) * local_nodes)
            move = (lax.rem(here - owner + seq_count, seq_count) - owner) * local_nodes
            place = jnp.where(inside, parent + move.astype(jnp.float32), place)
        lane = lax.broadcasted_iota(jnp.int32, (1, LANES), 1)
        places.append(jnp.where(lane < local_leaves, place, -1.0))

    sub = lax.broadcasted_iota(jnp.int32, (LANES, LANES), 0)
    lane = lax.broadcasted_iota(jnp.int32, (LANES, LANES), 1)
    columns = [jnp.broadcast_to(place, (LANES, LANES)).T for place in places]
    picks = []
    pot_sorted = jnp.zeros((leaves, 1), jnp.float32)
    target = lax.broadcasted_iota(jnp.int32, (leaves, LANES), 0).astype(jnp.float32)
    for at in range(seq_count):
        nth = jnp.sum(
            jnp.where((columns[at] == places[at]) & (sub < lane), 1.0, 0.0), axis=0, keepdims=True
        )
        for before in range(at):
            nth = nth + jnp.sum(
                jnp.where(columns[before] == places[at], 1.0, 0.0), axis=0, keepdims=True
            )
        slot = jnp.where(places[at] >= 0.0, nth * nodes + places[at], -1.0)
        pick = jnp.where(target == slot, 1.0, 0.0)
        pot_sorted = pot_sorted + jnp.sum(pick * pots[at], axis=1, keepdims=True)
        picks.append(pick.astype(jnp.bfloat16)[:, :local_leaves])
    lookup = jnp.concatenate(reach * (leaves // nodes), axis=0)

    reach_all[...] = jnp.zeros_like(reach_all)
    total[...] = jnp.zeros_like(total)
    live_rounds = jnp.max(info_ref[base + 1 : base + 2, :LANES])
    for at in range(rounds):

        @pl.when(live_rounds > at)
        def _():
            rows = slice(at * local_leaves, (at + 1) * local_leaves)
            live = info_ref[rounds + at : rounds + at + 1, :]
            strat = jnp.dot(picks[0], own_ref[rows, :], preferred_element_type=jnp.float32)
            for pick, pack in zip(picks[1:], came):
                strat = strat + jnp.dot(pick, pack[rows, :], preferred_element_type=jnp.float32)
            reach_all[:, :hands] = (lookup * strat * live[:, :hands]).astype(jnp.bfloat16)
            shown = jnp.dot(reach_all[...], payoff_ref[at], preferred_element_type=jnp.float32)
            value = shown * pot_sorted
            best = value[:nodes]
            for row in range(nodes, leaves, nodes):
                best = jnp.maximum(best, value[row : row + nodes])
            gain = best * (live * info_ref[base : base + 1, :])
            total[...] += gain

    short = round_up(local_nodes, 8) - local_nodes
    for step in range(seq_count):
        rows = total[step * local_nodes : (step + 1) * local_nodes, :]
        if short:
            rows = jnp.concatenate([rows, jnp.zeros((short, padded), jnp.float32)], axis=0)
        for at, tile in enumerate(pack_tiles(rows, local_nodes, hands)):
            outs[step][at] = tile


def share_kernel(rows, hands, tiles_ref, out_ref, tmp, sem):
    tiles = [tiles_ref[at] for at in range(tile_count(rows, hands))]
    for at, group in enumerate(unpack_tiles(tiles, rows, hands)):
        for row in range(8 * at, min(8 * at + 8, rows)):
            tmp[row] = group[row - 8 * at : row - 8 * at + 1]
    copy = pltpu.make_async_copy(tmp, out_ref, sem)
    copy.start()
    copy.wait()


def root_kernel(rows, hands, mine_ref, other_ref, out_ref, tmp, sem):
    first = lax.rem(lax.axis_index("board"), 2) == 0
    lower = jnp.where(first, mine_ref[...], other_ref[...])
    upper = jnp.where(first, other_ref[...], mine_ref[...])
    half = mine_ref.shape[0]
    count = tile_count(rows, hands)
    tiles = [lower[at] for at in range(half)] + [upper[at] for at in range(count - half)]
    for at, group in enumerate(unpack_tiles(tiles, rows, hands)):
        height = min(8, rows - 8 * at)
        tmp[8 * at : 8 * at + height, :] = group[:height]
    copy = pltpu.make_async_copy(tmp, out_ref, sem)
    copy.start()
    copy.wait()


def body(
    board_cards, hand_ranks, river_count, reach_in, strategy, parent_node, pot_size, flop_weight
):
    seq_count = lax.axis_size("seq")
    seq_here = lax.axis_index("seq")
    board_count = lax.axis_size("board")
    rivers, local_leaves, hands = strategy.shape[1:]
    local_nodes = reach_in.shape[1]
    nodes, leaves = local_nodes * seq_count, local_leaves * seq_count
    rounds = -(-rivers // seq_count)
    padded = round_up(hands, LANES)
    anywhere = pl.BlockSpec(memory_space=pltpu.HBM)
    vmem = pl.BlockSpec(memory_space=pltpu.VMEM)
    params = pltpu.CompilerParams(vmem_limit_bytes=16 * MIB)

    def shift(array, step):
        return lax.ppermute(
            array, "seq", [(at, (at + step) % seq_count) for at in range(seq_count)]
        )

    def strategy_for(step):
        owner = (seq_here + step) % seq_count
        if rivers % seq_count == 0:
            split = strategy.reshape(rounds, seq_count, local_leaves, hands)
            rows = lax.dynamic_slice_in_dim(split, owner, 1, axis=1)
        else:
            picked = [
                lax.dynamic_slice_in_dim(
                    strategy[0], jnp.minimum(at * seq_count + owner, rivers - 1), 1, axis=0
                )
                for at in range(rounds)
            ]
            rows = jnp.concatenate(picked, axis=0)
        return rows.reshape(rounds * local_leaves, hands)

    own = strategy_for(0)
    came = [shift(strategy_for(step), step) for step in range(1, seq_count)]

    small_rows = round_up(local_nodes + 4, 16)
    info_rows = round_up(2 * rounds + 4 + local_nodes, 8)
    small, info = pl.pallas_call(
        functools.partial(pack_kernel, rounds, seq_count),
        out_shape=[
            jax.ShapeDtypeStruct((small_rows, hands), jnp.bfloat16),
            jax.ShapeDtypeStruct((info_rows, padded), jnp.float32),
        ],
        in_specs=[anywhere] * 6,
        out_specs=[anywhere] * 2,
        scratch_shapes=[
            pltpu.VMEM(reach_in.shape, jnp.bfloat16),
            pltpu.VMEM((1, local_leaves), jnp.int32),
            pltpu.VMEM((1, local_leaves), jnp.float32),
            pltpu.VMEM((rivers, 1, hands), jnp.int32),
            pltpu.SMEM((board_cards.shape[2], 1, rivers), jnp.int32),
            pltpu.SMEM((1,), jnp.int32),
            pltpu.VMEM((small_rows, hands), jnp.bfloat16),
            pltpu.VMEM((info_rows, padded), jnp.float32),
            pltpu.SemaphoreType.DMA((6,)),
            pltpu.SemaphoreType.DMA((2,)),
        ],
        compiler_params=pltpu.CompilerParams(vmem_limit_bytes=60 * MIB),
        name="pack",
    )(
        reach_in,
        parent_node[None],
        pot_size[None],
        hand_ranks.transpose(1, 0, 2),
        board_cards.transpose(2, 0, 1),
        river_count,
    )
    smalls = [shift(small, step) for step in range(1, seq_count)]

    payoff, info = pl.pallas_call(
        functools.partial(build_kernel, rounds),
        out_shape=[
            jax.ShapeDtypeStruct((rounds, padded, padded), jnp.bfloat16),
            jax.ShapeDtypeStruct((info_rows, padded), jnp.float32),
        ],
        in_specs=[vmem],
        out_specs=[vmem] * 2,
        scratch_shapes=[
            pltpu.VMEM((rounds, 16, padded), jnp.bfloat16),
            pltpu.VMEM((rounds, 16, padded), jnp.bfloat16),
            pltpu.VMEM((round_up(DECK + 1, 16), padded), jnp.bfloat16),
            pltpu.VMEM((round_up(DECK + 1, 16), padded), jnp.bfloat16),
        ],
        compiler_params=pltpu.CompilerParams(vmem_limit_bytes=30 * MIB),
        cost_estimate=pl.CostEstimate(
            flops=10 * rounds * padded * padded, bytes_accessed=4 * padded * padded, transcendentals=0
        ),
        name="build",
    )(info)

    count = tile_count(local_nodes, hands)
    shares = pl.pallas_call(
        functools.partial(value_kernel, rounds, seq_count, nodes, leaves),
        out_shape=[jax.ShapeDtypeStruct((count, 8, LANES), jnp.float32)] * seq_count,
        in_specs=[vmem] * (1 + 2 * seq_count),
        out_specs=[vmem] * seq_count,
        scratch_shapes=[
            pltpu.VMEM((nodes, padded), jnp.float32),
            pltpu.VMEM((leaves, padded), jnp.bfloat16),
        ],
        compiler_params=params,
        name="value",
    )(payoff, info, own, *came, *smalls)

    share = shares[0]
    for step in range(1, seq_count):
        share = share + shift(shares[step], -step)
    def swap(array, step):
        return lax.ppermute(array, "board", [(at, at ^ step) for at in range(board_count)])

    half = -(-count // 2)
    parity = lax.axis_index("board") % 2
    root = share * (flop_weight[0] / board_count)
    if count % 2:
        root = jnp.concatenate([root, jnp.zeros((1, 8, LANES), jnp.float32)], axis=0)
    root = root.reshape(2, half, 8, LANES)
    mine = lax.dynamic_index_in_dim(root, parity, 0, keepdims=False)
    mine = mine + swap(lax.dynamic_index_in_dim(root, 1 - parity, 0, keepdims=False), 1)
    step = 2
    while step < board_count:
        if step == 2 and board_count >= 8:
            near, far, across = [swap(mine, at) for at in (2, 4, 6)]
            mine = (mine + near) + (far + across)
            step *= 4
        else:
            mine = mine + swap(mine, step)
            step *= 2
    other = swap(mine, 1)

    turn_value = pl.pallas_call(
        functools.partial(share_kernel, local_nodes, hands),
        out_shape=jax.ShapeDtypeStruct((local_nodes, 1, hands), jnp.float32),
        in_specs=[vmem],
        out_specs=anywhere,
        scratch_shapes=[
            pltpu.VMEM((local_nodes, 1, hands), jnp.float32),
            pltpu.SemaphoreType.DMA,
        ],
        compiler_params=params,
        name="share",
    )(share)
    root_value = pl.pallas_call(
        functools.partial(root_kernel, local_nodes, hands),
        out_shape=jax.ShapeDtypeStruct((local_nodes, hands), jnp.float32),
        in_specs=[vmem] * 2,
        out_specs=anywhere,
        scratch_shapes=[pltpu.VMEM((local_nodes, hands), jnp.float32), pltpu.SemaphoreType.DMA],
        compiler_params=params,
        name="root",
    )(mine, other)
    return (turn_value.transpose(1, 0, 2), root_value)


def solution(mesh):
    return jax.shard_map(
        body,
        mesh=mesh,
        in_specs=(
            P("board", None, None),
            P("board", None, None),
            P("board"),
            P("board", "seq", None),
            P("board", None, "seq", None),
            P("seq"),
            P("seq"),
            P("board"),
        ),
        out_specs=(P("board", "seq", None), P("seq", None)),
        check_vma=False,
    )
```

```python
import functools

import jax
import jax.numpy as jnp
from jax import lax
from jax.experimental import pallas as pl
from jax.experimental.pallas import tpu as pltpu
from jax.sharding import PartitionSpec as P

DECK = 52
LANES = 128
MIB = 1024 * 1024


def round_up(value, step):
    return -(-value // step) * step


def hand_cards(padded):
    hand = lax.broadcasted_iota(jnp.int32, (1, padded), 1)
    low = jnp.zeros((1, padded), jnp.int32)
    start = jnp.zeros((1, padded), jnp.int32)
    first = 0
    for card in range(DECK - 1):
        if card:
            low = jnp.where(hand >= first, card, low)
            start = jnp.where(hand >= first, first, start)
        first += DECK - 1 - card
    high = hand - start + low + 1
    real = hand < first
    return jnp.where(real, low, -1), jnp.where(real, high, -1)


def pad_rows(rows):
    return 1 << max(rows - 1, 0).bit_length()


def tile_count(rows, hands):
    full, rest = divmod(rows, 8)
    whole, tail = divmod(hands, LANES)
    count = full * whole
    if rest:
        count += -(-whole // (8 // pad_rows(rest)))
    groups = full + (rest > 0)
    if tail:
        count += -(-groups // 2) if tail <= LANES // 2 else groups
    return count


def pack_tiles(value, rows, hands):
    full, rest = divmod(rows, 8)
    whole, tail = divmod(hands, LANES)
    tiles = [
        value[8 * group : 8 * group + 8, LANES * at : LANES * (at + 1)]
        for group in range(full)
        for at in range(whole)
    ]
    if rest:
        part = pad_rows(rest)
        each = 8 // part
        for start in range(0, whole, each):
            pieces = [
                value[8 * full : 8 * full + part, LANES * at : LANES * (at + 1)]
                for at in range(start, min(start + each, whole))
            ]
            if len(pieces) < each:
                pieces.append(jnp.zeros((8 - part * len(pieces), LANES), value.dtype))
            tiles.append(jnp.concatenate(pieces, axis=0) if len(pieces) > 1 else pieces[0])
    if tail:
        groups = full + (rest > 0)
        tails = [value[8 * group : 8 * group + 8, LANES * whole :] for group in range(groups)]
        if tail <= LANES // 2:
            for at in range(0, groups, 2):
                tile = tails[at]
                if at + 1 < groups:
                    tile = tile + pltpu.roll(tails[at + 1], LANES // 2, 1)
                tiles.append(tile)
        else:
            tiles.extend(tails)
    return tiles


def unpack_tiles(tiles, rows, hands):
    full, rest = divmod(rows, 8)
    whole, tail = divmod(hands, LANES)
    groups = [[tiles[group * whole + at] for at in range(whole)] for group in range(full)]
    used = full * whole
    if rest:
        part = pad_rows(rest)
        each = 8 // part
        last = []
        for at in range(whole):
            tile = tiles[used + at // each]
            begin = part * (at % each)
            last.append(pltpu.roll(tile, (8 - begin) % 8, 0) if begin else tile)
        used += -(-whole // each)
        groups.append(last)
    if tail:
        for at, group in enumerate(groups):
            if tail <= LANES // 2:
                tile = tiles[used + at // 2]
                if at % 2:
                    tile = pltpu.roll(tile, LANES // 2, 1)
            else:
                tile = tiles[used + at]
            group.append(tile[:, :tail])
    return [jnp.concatenate(group, axis=1) for group in groups]


def copy_all(pairs, sems):
    copies = [
        pltpu.make_async_copy(source, target, sems.at[at])
        for at, (source, target) in enumerate(pairs)
    ]
    for copy in copies:
        copy.start()
    return copies


def pack_kernel(
    rounds,
    seq_count,
    reach_ref,
    parent_ref,
    pot_ref,
    rank_ref,
    board_ref,
    count_ref,
    small_ref,
    info_ref,
    reach_tmp,
    parent_tmp,
    pot_tmp,
    rank_tmp,
    board_tmp,
    count_tmp,
    small,
    info,
    sems,
    out_sems,
):
    hands, padded = small.shape[-1], info.shape[-1]
    nodes, leaves = reach_tmp.shape[1], parent_tmp.shape[-1]
    rivers = rank_tmp.shape[0]
    here = lax.axis_index("seq")
    loads = copy_all(
        [
            (reach_ref, reach_tmp),
            (parent_ref, parent_tmp),
            (pot_ref, pot_tmp),
            (rank_ref, rank_tmp),
            (board_ref, board_tmp),
            (count_ref, count_tmp),
        ],
        sems,
    )
    low, high = hand_cards(padded)
    info[...] = jnp.zeros_like(info)
    for copy in loads[:3]:
        copy.wait()
    pot = pot_tmp[...]
    parent = parent_tmp[...].astype(jnp.float32)
    reach = reach_tmp[0].astype(jnp.float32)
    top = pot.astype(jnp.bfloat16).astype(jnp.float32)
    middle = (pot - top).astype(jnp.bfloat16).astype(jnp.float32)
    labels = jnp.concatenate([parent, top, middle, pot - top - middle], axis=0)
    rows = [reach, jnp.concatenate([labels, jnp.zeros((4, hands - leaves), jnp.float32)], axis=1)]
    extra = small.shape[0]
    if extra > nodes + 4:
        rows.append(jnp.zeros((extra - nodes - 4, hands), jnp.float32))
    small[...] = jnp.concatenate(rows, axis=0).astype(jnp.bfloat16)
    sent = pltpu.make_async_copy(small, small_ref, out_sems.at[0])
    sent.start()

    for copy in loads[3:]:
        copy.wait()
    live_count = count_tmp[0]
    base = 2 * rounds
    for at in range(rounds):
        river = jnp.minimum(at * seq_count + here, rivers - 1)
        info[at : at + 1, :hands] = rank_tmp[river].astype(jnp.float32)
        alive = jnp.where(at * seq_count + here < live_count, 1.0, 0.0)
        live = jnp.where(low >= 0, alive, 0.0)
        for slot in range(board_tmp.shape[0]):
            card = board_tmp[slot, 0, river]
            live = jnp.where((low == card) | (high == card), 0.0, live)
        info[rounds + at : rounds + at + 1, :] = live
    info[base : base + 1, :] = 1.0 / (hands * jnp.full((1, padded), live_count.astype(jnp.float32)))
    info[base + 1 : base + 2, :leaves] = parent
    info[base + 2 : base + 3, :leaves] = pot
    info[base + 3 : base + 3 + nodes, :hands] = reach
    kept = pltpu.make_async_copy(info, info_ref, out_sems.at[1])
    kept.start()
    sent.wait()
    kept.wait()


def build_kernel(rounds, info_ref, payoff_ref, kept_ref, ranks, gaps, holds, lacks):
    padded = payoff_ref.shape[-1]
    kept_ref[...] = info_ref[...]

    low, high = hand_cards(padded)
    card = lax.broadcasted_iota(jnp.int32, (holds.shape[0], padded), 0)
    held = jnp.where((card == low) | (card == high), 1.0, 0.0)
    holds[...] = jnp.where(card == DECK, 1.0, held).astype(jnp.bfloat16)
    lacks[...] = jnp.where(card == DECK, 1.0, -held).astype(jnp.bfloat16)
    row = lax.broadcasted_iota(jnp.int32, (ranks.shape[1], padded), 0)
    for at in range(rounds):
        rank = info_ref[at : at + 1, :]
        top = jnp.floor(rank * (1.0 / LANES)) * LANES
        rest = rank - top
        sides = jnp.where(row % 2 == 0, top, rest)
        ones = jnp.where(row < 4, 1.0, 0.0)
        ranks[at] = jnp.where(row < 2, -sides, ones).astype(jnp.bfloat16)
        gaps[at] = jnp.where(row < 2, ones, jnp.where(row < 4, sides, 0.0)).astype(jnp.bfloat16)

    def product(left, right):
        return lax.dot_general(
            left, right, (((0,), (0,)), ((), ())), preferred_element_type=jnp.float32
        ).astype(jnp.bfloat16)

    for start in range(0, padded, LANES):
        rows = slice(start, start + LANES)
        for lane in range(0, padded, 2 * LANES):
            here = slice(lane, min(lane + 2 * LANES, padded))
            mask = product(holds[:, rows], lacks[:, here])
            if here.start <= start < here.stop:
                mask = jnp.maximum(mask, 0.0)
            for at in range(rounds):
                gap = product(ranks[at, :, rows], gaps[at, :, here])
                payoff_ref[at, rows, here] = jnp.maximum(jnp.minimum(gap, mask), -mask)


def value_kernel(rounds, seq_count, nodes, leaves, *refs):
    payoff_ref, info_ref, own_ref = refs[:3]
    came = refs[3 : 2 + seq_count]
    smalls = refs[2 + seq_count : 1 + 2 * seq_count]
    outs, (total, reach_all) = refs[1 + 2 * seq_count : -2], refs[-2:]
    hands = own_ref.shape[-1]
    padded = payoff_ref.shape[-1]
    local_leaves, local_nodes = leaves // seq_count, nodes // seq_count
    here = lax.axis_index("seq")
    base = 2 * rounds

    reach, places, pots = [], [], []
    for at in range(seq_count):
        if at == 0:
            reach.append(info_ref[base + 3 : base + 3 + local_nodes, :hands])
            parent = info_ref[base + 1 : base + 2, :LANES]
            pots.append(info_ref[base + 2 : base + 3, :LANES])
        else:
            small = smalls[at - 1][...].astype(jnp.float32)
            reach.append(small[:local_nodes])
            labels = small[local_nodes : local_nodes + 4, :LANES]
            parent = labels[0:1]
            pots.append(labels[1:2] + labels[2:3] + labels[3:4])
        place = parent
        for owner in range(seq_count):
            inside = (parent >= owner * local_nodes) & (parent < (owner + 1) * local_nodes)
            move = (lax.rem(here - owner + seq_count, seq_count) - owner) * local_nodes
            place = jnp.where(inside, parent + move.astype(jnp.float32), place)
        lane = lax.broadcasted_iota(jnp.int32, (1, LANES), 1)
        places.append(jnp.where(lane < local_leaves, place, -1.0))

    sub = lax.broadcasted_iota(jnp.int32, (LANES, LANES), 0)
    lane = lax.broadcasted_iota(jnp.int32, (LANES, LANES), 1)
    columns = [jnp.broadcast_to(place, (LANES, LANES)).T for place in places]
    picks = []
    pot_sorted = jnp.zeros((leaves, 1), jnp.float32)
    target = lax.broadcasted_iota(jnp.int32, (leaves, LANES), 0).astype(jnp.float32)
    for at in range(seq_count):
        nth = jnp.sum(
            jnp.where((columns[at] == places[at]) & (sub < lane), 1.0, 0.0), axis=0, keepdims=True
        )
        for before in range(at):
            nth = nth + jnp.sum(
                jnp.where(columns[before] == places[at], 1.0, 0.0), axis=0, keepdims=True
            )
        slot = jnp.where(places[at] >= 0.0, nth * nodes + places[at], -1.0)
        pick = jnp.where(target == slot, 1.0, 0.0)
        pot_sorted = pot_sorted + jnp.sum(pick * pots[at], axis=1, keepdims=True)
        picks.append(pick.astype(jnp.bfloat16)[:, :local_leaves])
    lookup = jnp.concatenate(reach * (leaves // nodes), axis=0)

    reach_all[...] = jnp.zeros_like(reach_all)
    gains = []
    for at in range(rounds):
        rows = slice(at * local_leaves, (at + 1) * local_leaves)
        live = info_ref[rounds + at : rounds + at + 1, :]
        strat = jnp.dot(picks[0], own_ref[rows, :], preferred_element_type=jnp.float32)
        for pick, pack in zip(picks[1:], came):
            strat = strat + jnp.dot(pick, pack[rows, :], preferred_element_type=jnp.float32)
        reach_all[at, :, :hands] = (lookup * strat * live[:, :hands]).astype(jnp.bfloat16)
    for at in range(rounds):
        live = info_ref[rounds + at : rounds + at + 1, :]
        shown = jnp.dot(reach_all[at], payoff_ref[at], preferred_element_type=jnp.float32)
        value = shown * pot_sorted
        best = value[:nodes]
        for row in range(nodes, leaves, nodes):
            best = jnp.maximum(best, value[row : row + nodes])
        gains.append(best * (live * info_ref[base : base + 1, :]))
    total[...] = sum(gains[1:], gains[0])

    short = round_up(local_nodes, 8) - local_nodes
    for step in range(seq_count):
        rows = total[step * local_nodes : (step + 1) * local_nodes, :]
        if short:
            rows = jnp.concatenate([rows, jnp.zeros((short, padded), jnp.float32)], axis=0)
        for at, tile in enumerate(pack_tiles(rows, local_nodes, hands)):
            outs[step][at] = tile


def share_kernel(rows, hands, tiles_ref, out_ref, tmp, sem):
    tiles = [tiles_ref[at] for at in range(tile_count(rows, hands))]
    for at, group in enumerate(unpack_tiles(tiles, rows, hands)):
        for row in range(8 * at, min(8 * at + 8, rows)):
            tmp[row] = group[row - 8 * at : row - 8 * at + 1]
    copy = pltpu.make_async_copy(tmp, out_ref, sem)
    copy.start()
    copy.wait()


def root_kernel(rows, hands, mine_ref, other_ref, out_ref, tmp, sem):
    first = lax.rem(lax.axis_index("board"), 2) == 0
    lower = jnp.where(first, mine_ref[...], other_ref[...])
    upper = jnp.where(first, other_ref[...], mine_ref[...])
    half = mine_ref.shape[0]
    count = tile_count(rows, hands)
    tiles = [lower[at] for at in range(half)] + [upper[at] for at in range(count - half)]
    for at, group in enumerate(unpack_tiles(tiles, rows, hands)):
        height = min(8, rows - 8 * at)
        tmp[8 * at : 8 * at + height, :] = group[:height]
    copy = pltpu.make_async_copy(tmp, out_ref, sem)
    copy.start()
    copy.wait()


def body(
    board_cards, hand_ranks, river_count, reach_in, strategy, parent_node, pot_size, flop_weight
):
    seq_count = lax.axis_size("seq")
    seq_here = lax.axis_index("seq")
    board_count = lax.axis_size("board")
    rivers, local_leaves, hands = strategy.shape[1:]
    local_nodes = reach_in.shape[1]
    nodes, leaves = local_nodes * seq_count, local_leaves * seq_count
    rounds = -(-rivers // seq_count)
    padded = round_up(hands, LANES)
    anywhere = pl.BlockSpec(memory_space=pltpu.HBM)
    vmem = pl.BlockSpec(memory_space=pltpu.VMEM)
    params = pltpu.CompilerParams(vmem_limit_bytes=16 * MIB)

    def shift(array, step):
        return lax.ppermute(
            array, "seq", [(at, (at + step) % seq_count) for at in range(seq_count)]
        )

    def strategy_for(step):
        owner = (seq_here + step) % seq_count
        if rivers % seq_count == 0:
            split = strategy.reshape(rounds, seq_count, local_leaves, hands)
            rows = lax.dynamic_slice_in_dim(split, owner, 1, axis=1)
        else:
            picked = [
                lax.dynamic_slice_in_dim(
                    strategy[0], jnp.minimum(at * seq_count + owner, rivers - 1), 1, axis=0
                )
                for at in range(rounds)
            ]
            rows = jnp.concatenate(picked, axis=0)
        return rows.reshape(rounds * local_leaves, hands)

    own = strategy_for(0)
    came = [shift(strategy_for(step), step) for step in range(1, seq_count)]

    small_rows = round_up(local_nodes + 4, 16)
    info_rows = round_up(2 * rounds + 3 + local_nodes, 8)
    small, info = pl.pallas_call(
        functools.partial(pack_kernel, rounds, seq_count),
        out_shape=[
            jax.ShapeDtypeStruct((small_rows, hands), jnp.bfloat16),
            jax.ShapeDtypeStruct((info_rows, padded), jnp.float32),
        ],
        in_specs=[anywhere] * 6,
        out_specs=[anywhere] * 2,
        scratch_shapes=[
            pltpu.VMEM(reach_in.shape, jnp.bfloat16),
            pltpu.VMEM((1, local_leaves), jnp.int32),
            pltpu.VMEM((1, local_leaves), jnp.float32),
            pltpu.VMEM((rivers, 1, hands), jnp.int32),
            pltpu.SMEM((board_cards.shape[2], 1, rivers), jnp.int32),
            pltpu.SMEM((1,), jnp.int32),
            pltpu.VMEM((small_rows, hands), jnp.bfloat16),
            pltpu.VMEM((info_rows, padded), jnp.float32),
            pltpu.SemaphoreType.DMA((6,)),
            pltpu.SemaphoreType.DMA((2,)),
        ],
        compiler_params=pltpu.CompilerParams(vmem_limit_bytes=60 * MIB),
        name="pack",
    )(
        reach_in,
        parent_node[None],
        pot_size[None],
        hand_ranks.transpose(1, 0, 2),
        board_cards.transpose(2, 0, 1),
        river_count,
    )
    smalls = [shift(small, step) for step in range(1, seq_count)]

    payoff, info = pl.pallas_call(
        functools.partial(build_kernel, rounds),
        out_shape=[
            jax.ShapeDtypeStruct((rounds, padded, padded), jnp.bfloat16),
            jax.ShapeDtypeStruct((info_rows, padded), jnp.float32),
        ],
        in_specs=[vmem],
        out_specs=[vmem] * 2,
        scratch_shapes=[
            pltpu.VMEM((rounds, 16, padded), jnp.bfloat16),
            pltpu.VMEM((rounds, 16, padded), jnp.bfloat16),
            pltpu.VMEM((round_up(DECK + 1, 16), padded), jnp.bfloat16),
            pltpu.VMEM((round_up(DECK + 1, 16), padded), jnp.bfloat16),
        ],
        compiler_params=pltpu.CompilerParams(vmem_limit_bytes=30 * MIB),
        cost_estimate=pl.CostEstimate(
            flops=10 * rounds * padded * padded, bytes_accessed=4 * padded * padded, transcendentals=0
        ),
        name="build",
    )(info)

    count = tile_count(local_nodes, hands)
    shares = pl.pallas_call(
        functools.partial(value_kernel, rounds, seq_count, nodes, leaves),
        out_shape=[jax.ShapeDtypeStruct((count, 8, LANES), jnp.float32)] * seq_count,
        in_specs=[vmem] * (1 + 2 * seq_count),
        out_specs=[vmem] * seq_count,
        scratch_shapes=[
            pltpu.VMEM((nodes, padded), jnp.float32),
            pltpu.VMEM((rounds, leaves, padded), jnp.bfloat16),
        ],
        compiler_params=params,
        name="value",
    )(payoff, info, own, *came, *smalls)

    share = shares[0]
    for step in range(1, seq_count):
        share = share + shift(shares[step], -step)
    def swap(array, step):
        return lax.ppermute(array, "board", [(at, at ^ step) for at in range(board_count)])

    half = -(-count // 2)
    parity = lax.axis_index("board") % 2
    root = share * (flop_weight[0] / board_count)
    if count % 2:
        root = jnp.concatenate([root, jnp.zeros((1, 8, LANES), jnp.float32)], axis=0)
    root = root.reshape(2, half, 8, LANES)
    mine = lax.dynamic_index_in_dim(root, parity, 0, keepdims=False)
    mine = mine + swap(lax.dynamic_index_in_dim(root, 1 - parity, 0, keepdims=False), 1)
    step = 2
    while step < board_count:
        if step == 2 and board_count >= 8:
            near, far, across = [swap(mine, at) for at in (2, 4, 6)]
            mine = (mine + near) + (far + across)
            step *= 4
        else:
            mine = mine + swap(mine, step)
            step *= 2
    other = swap(mine, 1)

    turn_value = pl.pallas_call(
        functools.partial(share_kernel, local_nodes, hands),
        out_shape=jax.ShapeDtypeStruct((local_nodes, 1, hands), jnp.float32),
        in_specs=[vmem],
        out_specs=anywhere,
        scratch_shapes=[
            pltpu.VMEM((local_nodes, 1, hands), jnp.float32),
            pltpu.SemaphoreType.DMA,
        ],
        compiler_params=params,
        name="share",
    )(share)
    root_value = pl.pallas_call(
        functools.partial(root_kernel, local_nodes, hands),
        out_shape=jax.ShapeDtypeStruct((local_nodes, hands), jnp.float32),
        in_specs=[vmem] * 2,
        out_specs=anywhere,
        scratch_shapes=[pltpu.VMEM((local_nodes, hands), jnp.float32), pltpu.SemaphoreType.DMA],
        compiler_params=params,
        name="root",
    )(mine, other)
    return (turn_value.transpose(1, 0, 2), root_value)


def solution(mesh):
    return jax.shard_map(
        body,
        mesh=mesh,
        in_specs=(
            P("board", None, None),
            P("board", None, None),
            P("board"),
            P("board", "seq", None),
            P("board", None, "seq", None),
            P("seq"),
            P("seq"),
            P("board"),
        ),
        out_specs=(P("board", "seq", None), P("seq", None)),
        check_vma=False,
    )
```

```python
import functools

import jax
import jax.numpy as jnp
from jax import lax
from jax.experimental import pallas as pl
from jax.experimental.pallas import tpu as pltpu
from jax.sharding import PartitionSpec as P

DECK = 52
LANES = 128
MIB = 1024 * 1024


def round_up(value, step):
    return -(-value // step) * step


def hand_cards(padded):
    hand = lax.broadcasted_iota(jnp.int32, (1, padded), 1)
    low = jnp.zeros((1, padded), jnp.int32)
    start = jnp.zeros((1, padded), jnp.int32)
    first = 0
    for card in range(DECK - 1):
        if card:
            low = jnp.where(hand >= first, card, low)
            start = jnp.where(hand >= first, first, start)
        first += DECK - 1 - card
    high = hand - start + low + 1
    real = hand < first
    return jnp.where(real, low, -1), jnp.where(real, high, -1)


def pad_rows(rows):
    return 1 << max(rows - 1, 0).bit_length()


def tile_count(rows, hands):
    full, rest = divmod(rows, 8)
    whole, tail = divmod(hands, LANES)
    count = full * whole
    if rest:
        count += -(-whole // (8 // pad_rows(rest)))
    groups = full + (rest > 0)
    if tail:
        count += -(-groups // 2) if tail <= LANES // 2 else groups
    return count


def pack_tiles(value, rows, hands):
    full, rest = divmod(rows, 8)
    whole, tail = divmod(hands, LANES)
    tiles = [
        value[8 * group : 8 * group + 8, LANES * at : LANES * (at + 1)]
        for group in range(full)
        for at in range(whole)
    ]
    if rest:
        part = pad_rows(rest)
        each = 8 // part
        for start in range(0, whole, each):
            pieces = [
                value[8 * full : 8 * full + part, LANES * at : LANES * (at + 1)]
                for at in range(start, min(start + each, whole))
            ]
            if len(pieces) < each:
                pieces.append(jnp.zeros((8 - part * len(pieces), LANES), value.dtype))
            tiles.append(jnp.concatenate(pieces, axis=0) if len(pieces) > 1 else pieces[0])
    if tail:
        groups = full + (rest > 0)
        tails = [value[8 * group : 8 * group + 8, LANES * whole :] for group in range(groups)]
        if tail <= LANES // 2:
            for at in range(0, groups, 2):
                tile = tails[at]
                if at + 1 < groups:
                    tile = tile + pltpu.roll(tails[at + 1], LANES // 2, 1)
                tiles.append(tile)
        else:
            tiles.extend(tails)
    return tiles


def unpack_tiles(tiles, rows, hands):
    full, rest = divmod(rows, 8)
    whole, tail = divmod(hands, LANES)
    groups = [[tiles[group * whole + at] for at in range(whole)] for group in range(full)]
    used = full * whole
    if rest:
        part = pad_rows(rest)
        each = 8 // part
        last = []
        for at in range(whole):
            tile = tiles[used + at // each]
            begin = part * (at % each)
            last.append(pltpu.roll(tile, (8 - begin) % 8, 0) if begin else tile)
        used += -(-whole // each)
        groups.append(last)
    if tail:
        for at, group in enumerate(groups):
            if tail <= LANES // 2:
                tile = tiles[used + at // 2]
                if at % 2:
                    tile = pltpu.roll(tile, LANES // 2, 1)
            else:
                tile = tiles[used + at]
            group.append(tile[:, :tail])
    return [jnp.concatenate(group, axis=1) for group in groups]


def copy_all(pairs, sems):
    copies = [
        pltpu.make_async_copy(source, target, sems.at[at])
        for at, (source, target) in enumerate(pairs)
    ]
    for copy in copies:
        copy.start()
    return copies


def pack_kernel(
    rounds,
    seq_count,
    reach_ref,
    parent_ref,
    pot_ref,
    rank_ref,
    board_ref,
    count_ref,
    small_ref,
    info_ref,
    reach_tmp,
    parent_tmp,
    pot_tmp,
    rank_tmp,
    board_tmp,
    count_tmp,
    small,
    info,
    sems,
    out_sems,
):
    hands, padded = small.shape[-1], info.shape[-1]
    nodes, leaves = reach_tmp.shape[1], parent_tmp.shape[-1]
    rivers = rank_tmp.shape[0]
    here = lax.axis_index("seq")
    loads = copy_all(
        [
            (reach_ref, reach_tmp),
            (parent_ref, parent_tmp),
            (pot_ref, pot_tmp),
            (rank_ref, rank_tmp),
            (board_ref, board_tmp),
            (count_ref, count_tmp),
        ],
        sems,
    )
    low, high = hand_cards(padded)
    info[...] = jnp.zeros_like(info)
    for copy in loads[:3]:
        copy.wait()
    pot = pot_tmp[...]
    parent = parent_tmp[...].astype(jnp.float32)
    reach = reach_tmp[0].astype(jnp.float32)
    top = pot.astype(jnp.bfloat16).astype(jnp.float32)
    middle = (pot - top).astype(jnp.bfloat16).astype(jnp.float32)
    labels = jnp.concatenate([parent, top, middle, pot - top - middle], axis=0)
    rows = [reach, jnp.concatenate([labels, jnp.zeros((4, hands - leaves), jnp.float32)], axis=1)]
    extra = small.shape[0]
    if extra > nodes + 4:
        rows.append(jnp.zeros((extra - nodes - 4, hands), jnp.float32))
    small[...] = jnp.concatenate(rows, axis=0).astype(jnp.bfloat16)
    sent = pltpu.make_async_copy(small, small_ref, out_sems.at[0])
    sent.start()

    for copy in loads[3:]:
        copy.wait()
    live_count = count_tmp[0]
    base = 2 * rounds
    for at in range(rounds):
        river = jnp.minimum(at * seq_count + here, rivers - 1)
        info[at : at + 1, :hands] = rank_tmp[river].astype(jnp.float32)
        alive = jnp.where(at * seq_count + here < live_count, 1.0, 0.0)
        live = jnp.where(low >= 0, alive, 0.0)
        for slot in range(board_tmp.shape[0]):
            card = board_tmp[slot, 0, river]
            live = jnp.where((low == card) | (high == card), 0.0, live)
        info[rounds + at : rounds + at + 1, :] = live
    info[base : base + 1, :] = 1.0 / (hands * jnp.full((1, padded), live_count.astype(jnp.float32)))
    live_rounds = lax.div(live_count - here + seq_count - 1, seq_count)
    info[base + 3 + nodes : base + 4 + nodes, :] = jnp.full(
        (1, padded), live_rounds.astype(jnp.float32)
    )
    info[base + 1 : base + 2, :leaves] = parent
    info[base + 2 : base + 3, :leaves] = pot
    info[base + 3 : base + 3 + nodes, :hands] = reach
    kept = pltpu.make_async_copy(info, info_ref, out_sems.at[1])
    kept.start()
    sent.wait()
    kept.wait()


def build_kernel(rounds, info_ref, payoff_ref, kept_ref, ranks, gaps, holds, lacks):
    padded = payoff_ref.shape[-1]
    kept_ref[...] = info_ref[...]

    low, high = hand_cards(padded)
    card = lax.broadcasted_iota(jnp.int32, (holds.shape[0], padded), 0)
    held = jnp.where((card == low) | (card == high), 1.0, 0.0)
    holds[...] = jnp.where(card == DECK, 1.0, held).astype(jnp.bfloat16)
    lacks[...] = jnp.where(card == DECK, 1.0, -held).astype(jnp.bfloat16)
    row = lax.broadcasted_iota(jnp.int32, (ranks.shape[1], padded), 0)
    for at in range(rounds):
        rank = info_ref[at : at + 1, :]
        top = jnp.floor(rank * (1.0 / LANES)) * LANES
        rest = rank - top
        sides = jnp.where(row % 2 == 0, top, rest)
        ones = jnp.where(row < 4, 1.0, 0.0)
        ranks[at] = jnp.where(row < 2, -sides, ones).astype(jnp.bfloat16)
        gaps[at] = jnp.where(row < 2, ones, jnp.where(row < 4, sides, 0.0)).astype(jnp.bfloat16)

    def product(left, right):
        return lax.dot_general(
            left, right, (((0,), (0,)), ((), ())), preferred_element_type=jnp.float32
        ).astype(jnp.bfloat16)

    for start in range(0, padded, LANES):
        rows = slice(start, start + LANES)
        for lane in range(0, padded, 2 * LANES):
            here = slice(lane, min(lane + 2 * LANES, padded))
            mask = product(holds[:, rows], lacks[:, here])
            if here.start <= start < here.stop:
                mask = jnp.maximum(mask, 0.0)
            for at in range(rounds):
                gap = product(ranks[at, :, rows], gaps[at, :, here])
                payoff_ref[at, rows, here] = jnp.maximum(jnp.minimum(gap, mask), -mask)


def value_kernel(rounds, seq_count, nodes, leaves, *refs):
    payoff_ref, info_ref, own_ref = refs[:3]
    came = refs[3 : 2 + seq_count]
    smalls = refs[2 + seq_count : 1 + 2 * seq_count]
    outs, (total, reach_all) = refs[1 + 2 * seq_count : -2], refs[-2:]
    hands = own_ref.shape[-1]
    padded = payoff_ref.shape[-1]
    local_leaves, local_nodes = leaves // seq_count, nodes // seq_count
    here = lax.axis_index("seq")
    base = 2 * rounds

    reach, places, pots = [], [], []
    for at in range(seq_count):
        if at == 0:
            reach.append(info_ref[base + 3 : base + 3 + local_nodes, :hands])
            parent = info_ref[base + 1 : base + 2, :LANES]
            pots.append(info_ref[base + 2 : base + 3, :LANES])
        else:
            small = smalls[at - 1][...].astype(jnp.float32)
            reach.append(small[:local_nodes])
            labels = small[local_nodes : local_nodes + 4, :LANES]
            parent = labels[0:1]
            pots.append(labels[1:2] + labels[2:3] + labels[3:4])
        place = parent
        for owner in range(seq_count):
            inside = (parent >= owner * local_nodes) & (parent < (owner + 1) * local_nodes)
            move = (lax.rem(here - owner + seq_count, seq_count) - owner) * local_nodes
            place = jnp.where(inside, parent + move.astype(jnp.float32), place)
        lane = lax.broadcasted_iota(jnp.int32, (1, LANES), 1)
        places.append(jnp.where(lane < local_leaves, place, -1.0))

    sub = lax.broadcasted_iota(jnp.int32, (LANES, LANES), 0)
    lane = lax.broadcasted_iota(jnp.int32, (LANES, LANES), 1)
    columns = [jnp.broadcast_to(place, (LANES, LANES)).T for place in places]
    picks = []
    pot_sorted = jnp.zeros((leaves, 1), jnp.float32)
    target = lax.broadcasted_iota(jnp.int32, (leaves, LANES), 0).astype(jnp.float32)
    for at in range(seq_count):
        nth = jnp.sum(
            jnp.where((columns[at] == places[at]) & (sub < lane), 1.0, 0.0), axis=0, keepdims=True
        )
        for before in range(at):
            nth = nth + jnp.sum(
                jnp.where(columns[before] == places[at], 1.0, 0.0), axis=0, keepdims=True
            )
        slot = jnp.where(places[at] >= 0.0, nth * nodes + places[at], -1.0)
        pick = jnp.where(target == slot, 1.0, 0.0)
        pot_sorted = pot_sorted + jnp.sum(pick * pots[at], axis=1, keepdims=True)
        picks.append(pick.astype(jnp.bfloat16)[:, :local_leaves])
    lookup = jnp.concatenate(reach * (leaves // nodes), axis=0)

    reach_all[...] = jnp.zeros_like(reach_all)
    live_rounds = jnp.max(info_ref[base + 3 + local_nodes : base + 4 + local_nodes, :LANES])

    def sum_rounds(number):
        gains = []
        for at in range(number):
            rows = slice(at * local_leaves, (at + 1) * local_leaves)
            live = info_ref[rounds + at : rounds + at + 1, :]
            strat = jnp.dot(picks[0], own_ref[rows, :], preferred_element_type=jnp.float32)
            for pick, pack in zip(picks[1:], came):
                strat = strat + jnp.dot(pick, pack[rows, :], preferred_element_type=jnp.float32)
            reach_all[at, :, :hands] = (lookup * strat * live[:, :hands]).astype(jnp.bfloat16)
        for at in range(number):
            live = info_ref[rounds + at : rounds + at + 1, :]
            shown = jnp.dot(reach_all[at], payoff_ref[at], preferred_element_type=jnp.float32)
            value = shown * pot_sorted
            best = value[:nodes]
            for row in range(nodes, leaves, nodes):
                best = jnp.maximum(best, value[row : row + nodes])
            gains.append(best * (live * info_ref[base : base + 1, :]))
        total[...] = sum(gains[1:], gains[0])

    total[...] = jnp.zeros_like(total)
    for number in range(1, rounds + 1):
        pl.when(live_rounds == number)(functools.partial(sum_rounds, number))

    short = round_up(local_nodes, 8) - local_nodes
    for step in range(seq_count):
        rows = total[step * local_nodes : (step + 1) * local_nodes, :]
        if short:
            rows = jnp.concatenate([rows, jnp.zeros((short, padded), jnp.float32)], axis=0)
        for at, tile in enumerate(pack_tiles(rows, local_nodes, hands)):
            outs[step][at] = tile


def share_kernel(rows, hands, tiles_ref, out_ref, tmp, sem):
    tiles = [tiles_ref[at] for at in range(tile_count(rows, hands))]
    for at, group in enumerate(unpack_tiles(tiles, rows, hands)):
        for row in range(8 * at, min(8 * at + 8, rows)):
            tmp[row] = group[row - 8 * at : row - 8 * at + 1]
    copy = pltpu.make_async_copy(tmp, out_ref, sem)
    copy.start()
    copy.wait()


def root_kernel(rows, hands, mine_ref, other_ref, out_ref, tmp, sem):
    first = lax.rem(lax.axis_index("board"), 2) == 0
    lower = jnp.where(first, mine_ref[...], other_ref[...])
    upper = jnp.where(first, other_ref[...], mine_ref[...])
    half = mine_ref.shape[0]
    count = tile_count(rows, hands)
    tiles = [lower[at] for at in range(half)] + [upper[at] for at in range(count - half)]
    for at, group in enumerate(unpack_tiles(tiles, rows, hands)):
        height = min(8, rows - 8 * at)
        tmp[8 * at : 8 * at + height, :] = group[:height]
    copy = pltpu.make_async_copy(tmp, out_ref, sem)
    copy.start()
    copy.wait()


def body(
    board_cards, hand_ranks, river_count, reach_in, strategy, parent_node, pot_size, flop_weight
):
    seq_count = lax.axis_size("seq")
    seq_here = lax.axis_index("seq")
    board_count = lax.axis_size("board")
    rivers, local_leaves, hands = strategy.shape[1:]
    local_nodes = reach_in.shape[1]
    nodes, leaves = local_nodes * seq_count, local_leaves * seq_count
    rounds = -(-rivers // seq_count)
    padded = round_up(hands, LANES)
    anywhere = pl.BlockSpec(memory_space=pltpu.HBM)
    vmem = pl.BlockSpec(memory_space=pltpu.VMEM)
    params = pltpu.CompilerParams(vmem_limit_bytes=16 * MIB)

    def shift(array, step):
        return lax.ppermute(
            array, "seq", [(at, (at + step) % seq_count) for at in range(seq_count)]
        )

    def strategy_for(step):
        owner = (seq_here + step) % seq_count
        if rivers % seq_count == 0:
            split = strategy.reshape(rounds, seq_count, local_leaves, hands)
            rows = lax.dynamic_slice_in_dim(split, owner, 1, axis=1)
        else:
            picked = [
                lax.dynamic_slice_in_dim(
                    strategy[0], jnp.minimum(at * seq_count + owner, rivers - 1), 1, axis=0
                )
                for at in range(rounds)
            ]
            rows = jnp.concatenate(picked, axis=0)
        return rows.reshape(rounds * local_leaves, hands)

    own = strategy_for(0)
    came = [shift(strategy_for(step), step) for step in range(1, seq_count)]

    small_rows = round_up(local_nodes + 4, 16)
    info_rows = round_up(2 * rounds + 4 + local_nodes, 8)
    small, info = pl.pallas_call(
        functools.partial(pack_kernel, rounds, seq_count),
        out_shape=[
            jax.ShapeDtypeStruct((small_rows, hands), jnp.bfloat16),
            jax.ShapeDtypeStruct((info_rows, padded), jnp.float32),
        ],
        in_specs=[anywhere] * 6,
        out_specs=[anywhere] * 2,
        scratch_shapes=[
            pltpu.VMEM(reach_in.shape, jnp.bfloat16),
            pltpu.VMEM((1, local_leaves), jnp.int32),
            pltpu.VMEM((1, local_leaves), jnp.float32),
            pltpu.VMEM((rivers, 1, hands), jnp.int32),
            pltpu.SMEM((board_cards.shape[2], 1, rivers), jnp.int32),
            pltpu.SMEM((1,), jnp.int32),
            pltpu.VMEM((small_rows, hands), jnp.bfloat16),
            pltpu.VMEM((info_rows, padded), jnp.float32),
            pltpu.SemaphoreType.DMA((6,)),
            pltpu.SemaphoreType.DMA((2,)),
        ],
        compiler_params=pltpu.CompilerParams(vmem_limit_bytes=60 * MIB),
        name="pack",
    )(
        reach_in,
        parent_node[None],
        pot_size[None],
        hand_ranks.transpose(1, 0, 2),
        board_cards.transpose(2, 0, 1),
        river_count,
    )
    smalls = [shift(small, step) for step in range(1, seq_count)]

    payoff, info = pl.pallas_call(
        functools.partial(build_kernel, rounds),
        out_shape=[
            jax.ShapeDtypeStruct((rounds, padded, padded), jnp.bfloat16),
            jax.ShapeDtypeStruct((info_rows, padded), jnp.float32),
        ],
        in_specs=[vmem],
        out_specs=[vmem] * 2,
        scratch_shapes=[
            pltpu.VMEM((rounds, 16, padded), jnp.bfloat16),
            pltpu.VMEM((rounds, 16, padded), jnp.bfloat16),
            pltpu.VMEM((round_up(DECK + 1, 16), padded), jnp.bfloat16),
            pltpu.VMEM((round_up(DECK + 1, 16), padded), jnp.bfloat16),
        ],
        compiler_params=pltpu.CompilerParams(vmem_limit_bytes=30 * MIB),
        cost_estimate=pl.CostEstimate(
            flops=10 * rounds * padded * padded, bytes_accessed=4 * padded * padded, transcendentals=0
        ),
        name="build",
    )(info)

    count = tile_count(local_nodes, hands)
    shares = pl.pallas_call(
        functools.partial(value_kernel, rounds, seq_count, nodes, leaves),
        out_shape=[jax.ShapeDtypeStruct((count, 8, LANES), jnp.float32)] * seq_count,
        in_specs=[vmem] * (1 + 2 * seq_count),
        out_specs=[vmem] * seq_count,
        scratch_shapes=[
            pltpu.VMEM((nodes, padded), jnp.float32),
            pltpu.VMEM((rounds, leaves, padded), jnp.bfloat16),
        ],
        compiler_params=params,
        name="value",
    )(payoff, info, own, *came, *smalls)

    share = shares[0]
    for step in range(1, seq_count):
        share = share + shift(shares[step], -step)
    def swap(array, step):
        return lax.ppermute(array, "board", [(at, at ^ step) for at in range(board_count)])

    half = -(-count // 2)
    parity = lax.axis_index("board") % 2
    root = share * (flop_weight[0] / board_count)
    if count % 2:
        root = jnp.concatenate([root, jnp.zeros((1, 8, LANES), jnp.float32)], axis=0)
    root = root.reshape(2, half, 8, LANES)
    mine = lax.dynamic_index_in_dim(root, parity, 0, keepdims=False)
    mine = mine + swap(lax.dynamic_index_in_dim(root, 1 - parity, 0, keepdims=False), 1)
    step = 2
    while step < board_count:
        if step == 2 and board_count >= 8:
            near, far, across = [swap(mine, at) for at in (2, 4, 6)]
            mine = (mine + near) + (far + across)
            step *= 4
        else:
            mine = mine + swap(mine, step)
            step *= 2
    other = swap(mine, 1)

    turn_value = pl.pallas_call(
        functools.partial(share_kernel, local_nodes, hands),
        out_shape=jax.ShapeDtypeStruct((local_nodes, 1, hands), jnp.float32),
        in_specs=[vmem],
        out_specs=anywhere,
        scratch_shapes=[
            pltpu.VMEM((local_nodes, 1, hands), jnp.float32),
            pltpu.SemaphoreType.DMA,
        ],
        compiler_params=params,
        name="share",
    )(share)
    root_value = pl.pallas_call(
        functools.partial(root_kernel, local_nodes, hands),
        out_shape=jax.ShapeDtypeStruct((local_nodes, hands), jnp.float32),
        in_specs=[vmem] * 2,
        out_specs=anywhere,
        scratch_shapes=[pltpu.VMEM((local_nodes, hands), jnp.float32), pltpu.SemaphoreType.DMA],
        compiler_params=params,
        name="root",
    )(mine, other)
    return (turn_value.transpose(1, 0, 2), root_value)


def solution(mesh):
    return jax.shard_map(
        body,
        mesh=mesh,
        in_specs=(
            P("board", None, None),
            P("board", None, None),
            P("board"),
            P("board", "seq", None),
            P("board", None, "seq", None),
            P("seq"),
            P("seq"),
            P("board"),
        ),
        out_specs=(P("board", "seq", None), P("seq", None)),
        check_vma=False,
    )
```

```python
import functools

import jax
import jax.numpy as jnp
from jax import lax
from jax.experimental import pallas as pl
from jax.experimental.pallas import tpu as pltpu
from jax.sharding import PartitionSpec as P

DECK = 52
LANES = 128
MIB = 1024 * 1024


def round_up(value, step):
    return -(-value // step) * step


def hand_cards(padded):
    hand = lax.broadcasted_iota(jnp.int32, (1, padded), 1)
    low = jnp.zeros((1, padded), jnp.int32)
    start = jnp.zeros((1, padded), jnp.int32)
    first = 0
    for card in range(DECK - 1):
        if card:
            low = jnp.where(hand >= first, card, low)
            start = jnp.where(hand >= first, first, start)
        first += DECK - 1 - card
    high = hand - start + low + 1
    real = hand < first
    return jnp.where(real, low, -1), jnp.where(real, high, -1)


def pad_rows(rows):
    return 1 << max(rows - 1, 0).bit_length()


def tile_count(rows, hands):
    full, rest = divmod(rows, 8)
    whole, tail = divmod(hands, LANES)
    count = full * whole
    if rest:
        count += -(-whole // (8 // pad_rows(rest)))
    groups = full + (rest > 0)
    if tail:
        count += -(-groups // 2) if tail <= LANES // 2 else groups
    return count


def pack_tiles(value, rows, hands):
    full, rest = divmod(rows, 8)
    whole, tail = divmod(hands, LANES)
    tiles = [
        value[8 * group : 8 * group + 8, LANES * at : LANES * (at + 1)]
        for group in range(full)
        for at in range(whole)
    ]
    if rest:
        part = pad_rows(rest)
        each = 8 // part
        for start in range(0, whole, each):
            pieces = [
                value[8 * full : 8 * full + part, LANES * at : LANES * (at + 1)]
                for at in range(start, min(start + each, whole))
            ]
            if len(pieces) < each:
                pieces.append(jnp.zeros((8 - part * len(pieces), LANES), value.dtype))
            tiles.append(jnp.concatenate(pieces, axis=0) if len(pieces) > 1 else pieces[0])
    if tail:
        groups = full + (rest > 0)
        tails = [value[8 * group : 8 * group + 8, LANES * whole :] for group in range(groups)]
        if tail <= LANES // 2:
            for at in range(0, groups, 2):
                tile = tails[at]
                if at + 1 < groups:
                    tile = tile + pltpu.roll(tails[at + 1], LANES // 2, 1)
                tiles.append(tile)
        else:
            tiles.extend(tails)
    return tiles


def unpack_tiles(tiles, rows, hands):
    full, rest = divmod(rows, 8)
    whole, tail = divmod(hands, LANES)
    groups = [[tiles[group * whole + at] for at in range(whole)] for group in range(full)]
    used = full * whole
    if rest:
        part = pad_rows(rest)
        each = 8 // part
        last = []
        for at in range(whole):
            tile = tiles[used + at // each]
            begin = part * (at % each)
            last.append(pltpu.roll(tile, (8 - begin) % 8, 0) if begin else tile)
        used += -(-whole // each)
        groups.append(last)
    if tail:
        for at, group in enumerate(groups):
            if tail <= LANES // 2:
                tile = tiles[used + at // 2]
                if at % 2:
                    tile = pltpu.roll(tile, LANES // 2, 1)
            else:
                tile = tiles[used + at]
            group.append(tile[:, :tail])
    return [jnp.concatenate(group, axis=1) for group in groups]


def copy_all(pairs, sems):
    copies = [
        pltpu.make_async_copy(source, target, sems.at[at])
        for at, (source, target) in enumerate(pairs)
    ]
    for copy in copies:
        copy.start()
    return copies


def pack_kernel(
    rounds,
    seq_count,
    reach_ref,
    parent_ref,
    pot_ref,
    rank_ref,
    board_ref,
    count_ref,
    small_ref,
    info_ref,
    reach_tmp,
    parent_tmp,
    pot_tmp,
    rank_tmp,
    board_tmp,
    count_tmp,
    small,
    info,
    sems,
    out_sems,
):
    hands, padded = small.shape[-1], info.shape[-1]
    nodes, leaves = reach_tmp.shape[1], parent_tmp.shape[-1]
    rivers = rank_tmp.shape[0]
    here = lax.axis_index("seq")
    loads = copy_all(
        [
            (reach_ref, reach_tmp),
            (parent_ref, parent_tmp),
            (pot_ref, pot_tmp),
            (rank_ref, rank_tmp),
            (board_ref, board_tmp),
            (count_ref, count_tmp),
        ],
        sems,
    )
    low, high = hand_cards(padded)
    info[...] = jnp.zeros_like(info)
    for copy in loads[:3]:
        copy.wait()
    pot = pot_tmp[...]
    parent = parent_tmp[...].astype(jnp.float32)
    reach = reach_tmp[0].astype(jnp.float32)
    top = pot.astype(jnp.bfloat16).astype(jnp.float32)
    middle = (pot - top).astype(jnp.bfloat16).astype(jnp.float32)
    labels = jnp.concatenate([parent, top, middle, pot - top - middle], axis=0)
    rows = [reach, jnp.concatenate([labels, jnp.zeros((4, hands - leaves), jnp.float32)], axis=1)]
    extra = small.shape[0]
    if extra > nodes + 4:
        rows.append(jnp.zeros((extra - nodes - 4, hands), jnp.float32))
    small[...] = jnp.concatenate(rows, axis=0).astype(jnp.bfloat16)
    sent = pltpu.make_async_copy(small, small_ref, out_sems.at[0])
    sent.start()

    for copy in loads[3:]:
        copy.wait()
    live_count = count_tmp[0]
    base = 2 * rounds
    for at in range(rounds):
        river = jnp.minimum(at * seq_count + here, rivers - 1)
        info[at : at + 1, :hands] = rank_tmp[river].astype(jnp.float32)
        alive = jnp.where(at * seq_count + here < live_count, 1.0, 0.0)
        live = jnp.where(low >= 0, alive, 0.0)
        for slot in range(board_tmp.shape[0]):
            card = board_tmp[slot, 0, river]
            live = jnp.where((low == card) | (high == card), 0.0, live)
        info[rounds + at : rounds + at + 1, :] = live
    info[base : base + 1, :] = 1.0 / (hands * jnp.full((1, padded), live_count.astype(jnp.float32)))
    live_rounds = lax.div(live_count - here + seq_count - 1, seq_count)
    info[base + 3 + nodes : base + 4 + nodes, :] = jnp.full(
        (1, padded), live_rounds.astype(jnp.float32)
    )
    info[base + 1 : base + 2, :leaves] = parent
    info[base + 2 : base + 3, :leaves] = pot
    info[base + 3 : base + 3 + nodes, :hands] = reach
    kept = pltpu.make_async_copy(info, info_ref, out_sems.at[1])
    kept.start()
    sent.wait()
    kept.wait()


def build_kernel(rounds, info_ref, payoff_ref, kept_ref, ranks, gaps, holds, lacks):
    padded = payoff_ref.shape[-1]
    kept_ref[...] = info_ref[...]

    low, high = hand_cards(padded)
    card = lax.broadcasted_iota(jnp.int32, (holds.shape[0], padded), 0)
    held = jnp.where((card == low) | (card == high), 1.0, 0.0)
    holds[...] = jnp.where(card == DECK, 1.0, held).astype(jnp.bfloat16)
    lacks[...] = jnp.where(card == DECK, 1.0, -held).astype(jnp.bfloat16)
    row = lax.broadcasted_iota(jnp.int32, (ranks.shape[1], padded), 0)
    for at in range(rounds):
        rank = info_ref[at : at + 1, :]
        top = jnp.floor(rank * (1.0 / LANES)) * LANES
        rest = rank - top
        sides = jnp.where(row % 2 == 0, top, rest)
        ones = jnp.where(row < 4, 1.0, 0.0)
        ranks[at] = jnp.where(row < 2, -sides, ones).astype(jnp.bfloat16)
        gaps[at] = jnp.where(row < 2, ones, jnp.where(row < 4, sides, 0.0)).astype(jnp.bfloat16)

    def product(left, right):
        return lax.dot_general(
            left, right, (((0,), (0,)), ((), ())), preferred_element_type=jnp.float32
        ).astype(jnp.bfloat16)

    for start in range(0, padded, LANES):
        rows = slice(start, start + LANES)
        for lane in range(0, padded, 2 * LANES):
            here = slice(lane, min(lane + 2 * LANES, padded))
            mask = product(holds[:, rows], lacks[:, here])
            if here.start <= start < here.stop:
                mask = jnp.maximum(mask, 0.0)
            for at in range(rounds):
                gap = product(ranks[at, :, rows], gaps[at, :, here])
                payoff_ref[at, rows, here] = jnp.maximum(jnp.minimum(gap, mask), -mask)


def head_kernel(rounds, seq_count, nodes, leaves, *refs):
    payoff_ref, info_ref, own_ref = refs[:3]
    came = refs[3 : 2 + seq_count]
    smalls = refs[2 + seq_count : 1 + 2 * seq_count]
    total, picks_ref, pot_ref, lookup_ref, reach_all = refs[1 + 2 * seq_count :]
    hands = own_ref.shape[-1]
    padded = payoff_ref.shape[-1]
    local_leaves, local_nodes = leaves // seq_count, nodes // seq_count
    here = lax.axis_index("seq")
    base = 2 * rounds

    reach, places, pots = [], [], []
    for at in range(seq_count):
        if at == 0:
            reach.append(info_ref[base + 3 : base + 3 + local_nodes, :hands])
            parent = info_ref[base + 1 : base + 2, :LANES]
            pots.append(info_ref[base + 2 : base + 3, :LANES])
        else:
            small = smalls[at - 1][...].astype(jnp.float32)
            reach.append(small[:local_nodes])
            labels = small[local_nodes : local_nodes + 4, :LANES]
            parent = labels[0:1]
            pots.append(labels[1:2] + labels[2:3] + labels[3:4])
        place = parent
        for owner in range(seq_count):
            inside = (parent >= owner * local_nodes) & (parent < (owner + 1) * local_nodes)
            move = (lax.rem(here - owner + seq_count, seq_count) - owner) * local_nodes
            place = jnp.where(inside, parent + move.astype(jnp.float32), place)
        lane = lax.broadcasted_iota(jnp.int32, (1, LANES), 1)
        places.append(jnp.where(lane < local_leaves, place, -1.0))

    sub = lax.broadcasted_iota(jnp.int32, (LANES, LANES), 0)
    lane = lax.broadcasted_iota(jnp.int32, (LANES, LANES), 1)
    columns = [jnp.broadcast_to(place, (LANES, LANES)).T for place in places]
    picks = []
    pot_sorted = jnp.zeros((leaves, 1), jnp.float32)
    target = lax.broadcasted_iota(jnp.int32, (leaves, LANES), 0).astype(jnp.float32)
    for at in range(seq_count):
        nth = jnp.sum(
            jnp.where((columns[at] == places[at]) & (sub < lane), 1.0, 0.0), axis=0, keepdims=True
        )
        for before in range(at):
            nth = nth + jnp.sum(
                jnp.where(columns[before] == places[at], 1.0, 0.0), axis=0, keepdims=True
            )
        slot = jnp.where(places[at] >= 0.0, nth * nodes + places[at], -1.0)
        pick = jnp.where(target == slot, 1.0, 0.0)
        pot_sorted = pot_sorted + jnp.sum(pick * pots[at], axis=1, keepdims=True)
        picks_ref[at] = pick.astype(jnp.bfloat16)
        picks.append(picks_ref[at, :, :local_leaves])
    lookup = jnp.concatenate(reach * (leaves // nodes), axis=0)
    lookup_ref[...] = lookup
    pot_ref[...] = jnp.broadcast_to(pot_sorted, pot_ref.shape)

    reach_all[...] = jnp.zeros_like(reach_all)
    live_rounds = jnp.max(info_ref[base + 3 + local_nodes : base + 4 + local_nodes, :LANES])

    def sum_rounds(number):
        gains = []
        for at in range(number):
            rows = slice(at * local_leaves, (at + 1) * local_leaves)
            live = info_ref[rounds + at : rounds + at + 1, :]
            strat = jnp.dot(picks[0], own_ref[rows, :], preferred_element_type=jnp.float32)
            for pick, pack in zip(picks[1:], came):
                strat = strat + jnp.dot(pick, pack[rows, :], preferred_element_type=jnp.float32)
            reach_all[at, :, :hands] = (lookup * strat * live[:, :hands]).astype(jnp.bfloat16)
        for at in range(number):
            live = info_ref[rounds + at : rounds + at + 1, :]
            shown = jnp.dot(reach_all[at], payoff_ref[at], preferred_element_type=jnp.float32)
            value = shown * pot_sorted
            best = value[:nodes]
            for row in range(nodes, leaves, nodes):
                best = jnp.maximum(best, value[row : row + nodes])
            gains.append(best * (live * info_ref[base : base + 1, :]))
        total[...] = sum(gains[1:], gains[0])

    total[...] = jnp.zeros_like(total)
    for number in range(1, rounds - 1):
        pl.when(live_rounds == number)(functools.partial(sum_rounds, number))
    if rounds > 1:
        pl.when(live_rounds >= rounds - 1)(functools.partial(sum_rounds, rounds - 1))


def tail_kernel(rounds, seq_count, nodes, *refs):
    payoff_ref, info_ref, own_ref = refs[:3]
    came = refs[3 : 2 + seq_count]
    before_ref, picks_ref, pot_ref, lookup_ref = refs[2 + seq_count : 6 + seq_count]
    outs, (total, reach_all) = refs[6 + seq_count : -2], refs[-2:]
    hands = own_ref.shape[-1]
    padded = payoff_ref.shape[-1]
    leaves = lookup_ref.shape[0]
    local_leaves, local_nodes = leaves // seq_count, nodes // seq_count
    base = 2 * rounds
    last = rounds - 1
    live_rounds = jnp.max(info_ref[base + 3 + local_nodes : base + 4 + local_nodes, :LANES])
    total[...] = before_ref[...]

    @pl.when(live_rounds > last)
    def _():
        reach_all[...] = jnp.zeros_like(reach_all)
        live = info_ref[rounds + last : rounds + last + 1, :]
        own = own_ref[last * local_leaves : rounds * local_leaves, :]
        strat = jnp.dot(picks_ref[0, :, :local_leaves], own, preferred_element_type=jnp.float32)
        for at, block in enumerate(came, 1):
            pick = picks_ref[at, :, :local_leaves]
            strat = strat + jnp.dot(pick, block[...], preferred_element_type=jnp.float32)
        reach_all[:, :hands] = (lookup_ref[...] * strat * live[:, :hands]).astype(jnp.bfloat16)
        shown = jnp.dot(reach_all[...], payoff_ref[last], preferred_element_type=jnp.float32)
        value = shown * pot_ref[:, :1]
        best = value[:nodes]
        for row in range(nodes, leaves, nodes):
            best = jnp.maximum(best, value[row : row + nodes])
        total[...] += best * (live * info_ref[base : base + 1, :])

    short = round_up(local_nodes, 8) - local_nodes
    for step in range(seq_count):
        rows = total[step * local_nodes : (step + 1) * local_nodes, :]
        if short:
            rows = jnp.concatenate([rows, jnp.zeros((short, padded), jnp.float32)], axis=0)
        for at, tile in enumerate(pack_tiles(rows, local_nodes, hands)):
            outs[step][at] = tile


def share_kernel(rows, hands, tiles_ref, out_ref, tmp, sem):
    tiles = [tiles_ref[at] for at in range(tile_count(rows, hands))]
    for at, group in enumerate(unpack_tiles(tiles, rows, hands)):
        for row in range(8 * at, min(8 * at + 8, rows)):
            tmp[row] = group[row - 8 * at : row - 8 * at + 1]
    copy = pltpu.make_async_copy(tmp, out_ref, sem)
    copy.start()
    copy.wait()


def root_kernel(rows, hands, mine_ref, other_ref, out_ref, tmp, sem):
    first = lax.rem(lax.axis_index("board"), 2) == 0
    lower = jnp.where(first, mine_ref[...], other_ref[...])
    upper = jnp.where(first, other_ref[...], mine_ref[...])
    half = mine_ref.shape[0]
    count = tile_count(rows, hands)
    tiles = [lower[at] for at in range(half)] + [upper[at] for at in range(count - half)]
    for at, group in enumerate(unpack_tiles(tiles, rows, hands)):
        height = min(8, rows - 8 * at)
        tmp[8 * at : 8 * at + height, :] = group[:height]
    copy = pltpu.make_async_copy(tmp, out_ref, sem)
    copy.start()
    copy.wait()


def body(
    board_cards, hand_ranks, river_count, reach_in, strategy, parent_node, pot_size, flop_weight
):
    seq_count = lax.axis_size("seq")
    seq_here = lax.axis_index("seq")
    board_count = lax.axis_size("board")
    rivers, local_leaves, hands = strategy.shape[1:]
    local_nodes = reach_in.shape[1]
    nodes, leaves = local_nodes * seq_count, local_leaves * seq_count
    rounds = -(-rivers // seq_count)
    padded = round_up(hands, LANES)
    anywhere = pl.BlockSpec(memory_space=pltpu.HBM)
    vmem = pl.BlockSpec(memory_space=pltpu.VMEM)
    params = pltpu.CompilerParams(vmem_limit_bytes=16 * MIB)

    def shift(array, step):
        return lax.ppermute(
            array, "seq", [(at, (at + step) % seq_count) for at in range(seq_count)]
        )

    def strategy_for(step):
        owner = (seq_here + step) % seq_count
        if rivers % seq_count == 0:
            split = strategy.reshape(rounds, seq_count, local_leaves, hands)
            rows = lax.dynamic_slice_in_dim(split, owner, 1, axis=1)
        else:
            picked = [
                lax.dynamic_slice_in_dim(
                    strategy[0], jnp.minimum(at * seq_count + owner, rivers - 1), 1, axis=0
                )
                for at in range(rounds)
            ]
            rows = jnp.concatenate(picked, axis=0)
        return rows.reshape(rounds * local_leaves, hands)

    own = strategy_for(0)
    last = rounds - 1
    sent = [strategy_for(step) for step in range(1, seq_count)]
    own, *sent = lax.optimization_barrier((own, *sent))
    came_head = [shift(rows[: last * local_leaves], step) for step, rows in enumerate(sent, 1)]

    small_rows = round_up(local_nodes + 4, 16)
    info_rows = round_up(2 * rounds + 4 + local_nodes, 8)
    small, info = pl.pallas_call(
        functools.partial(pack_kernel, rounds, seq_count),
        out_shape=[
            jax.ShapeDtypeStruct((small_rows, hands), jnp.bfloat16),
            jax.ShapeDtypeStruct((info_rows, padded), jnp.float32),
        ],
        in_specs=[anywhere] * 6,
        out_specs=[anywhere] * 2,
        scratch_shapes=[
            pltpu.VMEM(reach_in.shape, jnp.bfloat16),
            pltpu.VMEM((1, local_leaves), jnp.int32),
            pltpu.VMEM((1, local_leaves), jnp.float32),
            pltpu.VMEM((rivers, 1, hands), jnp.int32),
            pltpu.SMEM((board_cards.shape[2], 1, rivers), jnp.int32),
            pltpu.SMEM((1,), jnp.int32),
            pltpu.VMEM((small_rows, hands), jnp.bfloat16),
            pltpu.VMEM((info_rows, padded), jnp.float32),
            pltpu.SemaphoreType.DMA((6,)),
            pltpu.SemaphoreType.DMA((2,)),
        ],
        compiler_params=pltpu.CompilerParams(vmem_limit_bytes=60 * MIB),
        name="pack",
    )(
        reach_in,
        parent_node[None],
        pot_size[None],
        hand_ranks.transpose(1, 0, 2),
        board_cards.transpose(2, 0, 1),
        river_count,
    )
    smalls = [shift(small, step) for step in range(1, seq_count)]
    *sent, info = lax.optimization_barrier((*sent, info))
    came_tail = [shift(rows[last * local_leaves :], step) for step, rows in enumerate(sent, 1)]

    payoff, info = pl.pallas_call(
        functools.partial(build_kernel, rounds),
        out_shape=[
            jax.ShapeDtypeStruct((rounds, padded, padded), jnp.bfloat16),
            jax.ShapeDtypeStruct((info_rows, padded), jnp.float32),
        ],
        in_specs=[vmem],
        out_specs=[vmem] * 2,
        scratch_shapes=[
            pltpu.VMEM((rounds, 16, padded), jnp.bfloat16),
            pltpu.VMEM((rounds, 16, padded), jnp.bfloat16),
            pltpu.VMEM((round_up(DECK + 1, 16), padded), jnp.bfloat16),
            pltpu.VMEM((round_up(DECK + 1, 16), padded), jnp.bfloat16),
        ],
        compiler_params=pltpu.CompilerParams(vmem_limit_bytes=30 * MIB),
        cost_estimate=pl.CostEstimate(
            flops=10 * rounds * padded * padded, bytes_accessed=4 * padded * padded, transcendentals=0
        ),
        name="build",
    )(info)

    count = tile_count(local_nodes, hands)
    total, *labels = pl.pallas_call(
        functools.partial(head_kernel, rounds, seq_count, nodes, leaves),
        out_shape=[
            jax.ShapeDtypeStruct((nodes, padded), jnp.float32),
            jax.ShapeDtypeStruct((seq_count, leaves, LANES), jnp.bfloat16),
            jax.ShapeDtypeStruct((leaves, LANES), jnp.float32),
            jax.ShapeDtypeStruct((leaves, hands), jnp.float32),
        ],
        in_specs=[vmem] * (1 + 2 * seq_count),
        out_specs=[vmem] * 4,
        scratch_shapes=[pltpu.VMEM((max(last, 1), leaves, padded), jnp.bfloat16)],
        compiler_params=params,
        cost_estimate=pl.CostEstimate(
            flops=2 * rounds * leaves * padded * padded, bytes_accessed=2 * rounds * padded * padded, transcendentals=0
        ),
        name="head",
    )(payoff, info, own, *came_head, *smalls)
    shares = pl.pallas_call(
        functools.partial(tail_kernel, rounds, seq_count, nodes),
        out_shape=[jax.ShapeDtypeStruct((count, 8, LANES), jnp.float32)] * seq_count,
        in_specs=[vmem] * (6 + seq_count),
        out_specs=[vmem] * seq_count,
        scratch_shapes=[
            pltpu.VMEM((nodes, padded), jnp.float32),
            pltpu.VMEM((leaves, padded), jnp.bfloat16),
        ],
        compiler_params=params,
        name="tail",
    )(payoff, info, own, *came_tail, total, *labels)

    share = shares[0]
    for step in range(1, seq_count):
        share = share + shift(shares[step], -step)
    def swap(array, step):
        return lax.ppermute(array, "board", [(at, at ^ step) for at in range(board_count)])

    half = -(-count // 2)
    parity = lax.axis_index("board") % 2
    root = share * (flop_weight[0] / board_count)
    if count % 2:
        root = jnp.concatenate([root, jnp.zeros((1, 8, LANES), jnp.float32)], axis=0)
    root = root.reshape(2, half, 8, LANES)
    mine = lax.dynamic_index_in_dim(root, parity, 0, keepdims=False)
    mine = mine + swap(lax.dynamic_index_in_dim(root, 1 - parity, 0, keepdims=False), 1)
    step = 2
    while step < board_count:
        if step == 2 and board_count >= 8:
            near, far, across = [swap(mine, at) for at in (2, 4, 6)]
            mine = (mine + near) + (far + across)
            step *= 4
        else:
            mine = mine + swap(mine, step)
            step *= 2
    other = swap(mine, 1)

    turn_value = pl.pallas_call(
        functools.partial(share_kernel, local_nodes, hands),
        out_shape=jax.ShapeDtypeStruct((local_nodes, 1, hands), jnp.float32),
        in_specs=[vmem],
        out_specs=anywhere,
        scratch_shapes=[
            pltpu.VMEM((local_nodes, 1, hands), jnp.float32),
            pltpu.SemaphoreType.DMA,
        ],
        compiler_params=params,
        name="share",
    )(share)
    root_value = pl.pallas_call(
        functools.partial(root_kernel, local_nodes, hands),
        out_shape=jax.ShapeDtypeStruct((local_nodes, hands), jnp.float32),
        in_specs=[vmem] * 2,
        out_specs=anywhere,
        scratch_shapes=[pltpu.VMEM((local_nodes, hands), jnp.float32), pltpu.SemaphoreType.DMA],
        compiler_params=params,
        name="root",
    )(mine, other)
    return (turn_value.transpose(1, 0, 2), root_value)


def solution(mesh):
    return jax.shard_map(
        body,
        mesh=mesh,
        in_specs=(
            P("board", None, None),
            P("board", None, None),
            P("board"),
            P("board", "seq", None),
            P("board", None, "seq", None),
            P("seq"),
            P("seq"),
            P("board"),
        ),
        out_specs=(P("board", "seq", None), P("seq", None)),
        check_vma=False,
    )
```

```python
import functools

import jax
import jax.numpy as jnp
from jax import lax
from jax.experimental import pallas as pl
from jax.experimental.pallas import tpu as pltpu
from jax.sharding import PartitionSpec as P

DECK = 52
LANES = 128
MIB = 1024 * 1024


def round_up(value, step):
    return -(-value // step) * step


def hand_cards(padded):
    hand = lax.broadcasted_iota(jnp.int32, (1, padded), 1)
    low = jnp.zeros((1, padded), jnp.int32)
    start = jnp.zeros((1, padded), jnp.int32)
    first = 0
    for card in range(DECK - 1):
        if card:
            low = jnp.where(hand >= first, card, low)
            start = jnp.where(hand >= first, first, start)
        first += DECK - 1 - card
    high = hand - start + low + 1
    real = hand < first
    return jnp.where(real, low, -1), jnp.where(real, high, -1)


def pad_rows(rows):
    return 1 << max(rows - 1, 0).bit_length()


def tile_count(rows, hands):
    full, rest = divmod(rows, 8)
    whole, tail = divmod(hands, LANES)
    count = full * whole
    if rest:
        count += -(-whole // (8 // pad_rows(rest)))
    groups = full + (rest > 0)
    if tail:
        count += -(-groups // 2) if tail <= LANES // 2 else groups
    return count


def pack_tiles(value, rows, hands):
    full, rest = divmod(rows, 8)
    whole, tail = divmod(hands, LANES)
    tiles = [
        value[8 * group : 8 * group + 8, LANES * at : LANES * (at + 1)]
        for group in range(full)
        for at in range(whole)
    ]
    if rest:
        part = pad_rows(rest)
        each = 8 // part
        for start in range(0, whole, each):
            pieces = [
                value[8 * full : 8 * full + part, LANES * at : LANES * (at + 1)]
                for at in range(start, min(start + each, whole))
            ]
            if len(pieces) < each:
                pieces.append(jnp.zeros((8 - part * len(pieces), LANES), value.dtype))
            tiles.append(jnp.concatenate(pieces, axis=0) if len(pieces) > 1 else pieces[0])
    if tail:
        groups = full + (rest > 0)
        tails = [value[8 * group : 8 * group + 8, LANES * whole :] for group in range(groups)]
        if tail <= LANES // 2:
            for at in range(0, groups, 2):
                tile = tails[at]
                if at + 1 < groups:
                    tile = tile + pltpu.roll(tails[at + 1], LANES // 2, 1)
                tiles.append(tile)
        else:
            tiles.extend(tails)
    return tiles


def unpack_tiles(tiles, rows, hands):
    full, rest = divmod(rows, 8)
    whole, tail = divmod(hands, LANES)
    groups = [[tiles[group * whole + at] for at in range(whole)] for group in range(full)]
    used = full * whole
    if rest:
        part = pad_rows(rest)
        each = 8 // part
        last = []
        for at in range(whole):
            tile = tiles[used + at // each]
            begin = part * (at % each)
            last.append(pltpu.roll(tile, (8 - begin) % 8, 0) if begin else tile)
        used += -(-whole // each)
        groups.append(last)
    if tail:
        for at, group in enumerate(groups):
            if tail <= LANES // 2:
                tile = tiles[used + at // 2]
                if at % 2:
                    tile = pltpu.roll(tile, LANES // 2, 1)
            else:
                tile = tiles[used + at]
            group.append(tile[:, :tail])
    return [jnp.concatenate(group, axis=1) for group in groups]


def copy_all(pairs, sems):
    copies = [
        pltpu.make_async_copy(source, target, sems.at[at])
        for at, (source, target) in enumerate(pairs)
    ]
    for copy in copies:
        copy.start()
    return copies


def pack_kernel(
    rounds,
    seq_count,
    reach_ref,
    parent_ref,
    pot_ref,
    rank_ref,
    board_ref,
    count_ref,
    small_ref,
    info_ref,
    reach_tmp,
    parent_tmp,
    pot_tmp,
    rank_tmp,
    board_tmp,
    count_tmp,
    small,
    info,
    sems,
    out_sems,
):
    hands, padded = small.shape[-1], info.shape[-1]
    nodes, leaves = reach_tmp.shape[1], parent_tmp.shape[-1]
    rivers = rank_tmp.shape[0]
    here = lax.axis_index("seq")
    loads = copy_all(
        [
            (reach_ref, reach_tmp),
            (parent_ref, parent_tmp),
            (pot_ref, pot_tmp),
            (rank_ref, rank_tmp),
            (board_ref, board_tmp),
            (count_ref, count_tmp),
        ],
        sems,
    )
    low, high = hand_cards(padded)
    info[...] = jnp.zeros_like(info)
    for copy in loads[:3]:
        copy.wait()
    pot = pot_tmp[...]
    parent = parent_tmp[...].astype(jnp.float32)
    reach = reach_tmp[0].astype(jnp.float32)
    top = pot.astype(jnp.bfloat16).astype(jnp.float32)
    middle = (pot - top).astype(jnp.bfloat16).astype(jnp.float32)
    labels = jnp.concatenate([parent, top, middle, pot - top - middle], axis=0)
    rows = [reach, jnp.concatenate([labels, jnp.zeros((4, hands - leaves), jnp.float32)], axis=1)]
    extra = small.shape[0]
    if extra > nodes + 4:
        rows.append(jnp.zeros((extra - nodes - 4, hands), jnp.float32))
    small[...] = jnp.concatenate(rows, axis=0).astype(jnp.bfloat16)
    sent = pltpu.make_async_copy(small, small_ref, out_sems.at[0])
    sent.start()

    for copy in loads[3:]:
        copy.wait()
    live_count = count_tmp[0]
    base = 2 * rounds
    for at in range(rounds):
        river = jnp.minimum(at * seq_count + here, rivers - 1)
        info[at : at + 1, :hands] = rank_tmp[river].astype(jnp.float32)
        alive = jnp.where(at * seq_count + here < live_count, 1.0, 0.0)
        live = jnp.where(low >= 0, alive, 0.0)
        for slot in range(board_tmp.shape[0]):
            card = board_tmp[slot, 0, river]
            live = jnp.where((low == card) | (high == card), 0.0, live)
        info[rounds + at : rounds + at + 1, :] = live
    info[base : base + 1, :] = 1.0 / (hands * jnp.full((1, padded), live_count.astype(jnp.float32)))
    live_rounds = lax.div(live_count - here + seq_count - 1, seq_count)
    info[base + 3 + nodes : base + 4 + nodes, :] = jnp.full(
        (1, padded), live_rounds.astype(jnp.float32)
    )
    info[base + 1 : base + 2, :leaves] = parent
    info[base + 2 : base + 3, :leaves] = pot
    info[base + 3 : base + 3 + nodes, :hands] = reach
    kept = pltpu.make_async_copy(info, info_ref, out_sems.at[1])
    kept.start()
    sent.wait()
    kept.wait()


def build_kernel(rounds, info_ref, payoff_ref, kept_ref, ranks, gaps, holds, lacks):
    padded = payoff_ref.shape[-1]
    kept_ref[...] = info_ref[...]

    low, high = hand_cards(padded)
    card = lax.broadcasted_iota(jnp.int32, (holds.shape[0], padded), 0)
    held = jnp.where((card == low) | (card == high), 1.0, 0.0)
    holds[...] = jnp.where(card == DECK, 1.0, held).astype(jnp.bfloat16)
    lacks[...] = jnp.where(card == DECK, 1.0, -held).astype(jnp.bfloat16)
    row = lax.broadcasted_iota(jnp.int32, (ranks.shape[1], padded), 0)
    for at in range(rounds):
        rank = info_ref[at : at + 1, :]
        top = jnp.floor(rank * (1.0 / LANES)) * LANES
        rest = rank - top
        sides = jnp.where(row % 2 == 0, top, rest)
        ones = jnp.where(row < 4, 1.0, 0.0)
        ranks[at] = jnp.where(row < 2, -sides, ones).astype(jnp.bfloat16)
        gaps[at] = jnp.where(row < 2, ones, jnp.where(row < 4, sides, 0.0)).astype(jnp.bfloat16)

    def product(left, right):
        return lax.dot_general(
            left, right, (((0,), (0,)), ((), ())), preferred_element_type=jnp.float32
        ).astype(jnp.bfloat16)

    for start in range(0, padded, 2 * LANES):
        rows = slice(start, min(start + 2 * LANES, padded))
        for lane in range(0, padded, 2 * LANES):
            here = slice(lane, min(lane + 2 * LANES, padded))
            mask = product(holds[:, rows], lacks[:, here])
            if lane == start:
                mask = jnp.maximum(mask, 0.0)
            for at in range(rounds):
                gap = product(ranks[at, :, rows], gaps[at, :, here])
                payoff_ref[at, rows, here] = jnp.maximum(jnp.minimum(gap, mask), -mask)


def head_kernel(rounds, seq_count, nodes, leaves, *refs):
    payoff_ref, info_ref, own_ref = refs[:3]
    came = refs[3 : 2 + seq_count]
    smalls = refs[2 + seq_count : 1 + 2 * seq_count]
    total, picks_ref, pot_ref, lookup_ref, reach_all = refs[1 + 2 * seq_count :]
    hands = own_ref.shape[-1]
    padded = payoff_ref.shape[-1]
    local_leaves, local_nodes = leaves // seq_count, nodes // seq_count
    here = lax.axis_index("seq")
    base = 2 * rounds

    reach, places, pots = [], [], []
    for at in range(seq_count):
        if at == 0:
            reach.append(info_ref[base + 3 : base + 3 + local_nodes, :hands])
            parent = info_ref[base + 1 : base + 2, :LANES]
            pots.append(info_ref[base + 2 : base + 3, :LANES])
        else:
            small = smalls[at - 1][...].astype(jnp.float32)
            reach.append(small[:local_nodes])
            labels = small[local_nodes : local_nodes + 4, :LANES]
            parent = labels[0:1]
            pots.append(labels[1:2] + labels[2:3] + labels[3:4])
        place = parent
        for owner in range(seq_count):
            inside = (parent >= owner * local_nodes) & (parent < (owner + 1) * local_nodes)
            move = (lax.rem(here - owner + seq_count, seq_count) - owner) * local_nodes
            place = jnp.where(inside, parent + move.astype(jnp.float32), place)
        lane = lax.broadcasted_iota(jnp.int32, (1, LANES), 1)
        places.append(jnp.where(lane < local_leaves, place, -1.0))

    sub = lax.broadcasted_iota(jnp.int32, (LANES, LANES), 0)
    lane = lax.broadcasted_iota(jnp.int32, (LANES, LANES), 1)
    columns = [jnp.broadcast_to(place, (LANES, LANES)).T for place in places]
    picks = []
    pot_sorted = jnp.zeros((leaves, 1), jnp.float32)
    target = lax.broadcasted_iota(jnp.int32, (leaves, LANES), 0).astype(jnp.float32)
    for at in range(seq_count):
        nth = jnp.sum(
            jnp.where((columns[at] == places[at]) & (sub < lane), 1.0, 0.0), axis=0, keepdims=True
        )
        for before in range(at):
            nth = nth + jnp.sum(
                jnp.where(columns[before] == places[at], 1.0, 0.0), axis=0, keepdims=True
            )
        slot = jnp.where(places[at] >= 0.0, nth * nodes + places[at], -1.0)
        pick = jnp.where(target == slot, 1.0, 0.0)
        pot_sorted = pot_sorted + jnp.sum(pick * pots[at], axis=1, keepdims=True)
        picks_ref[at] = pick.astype(jnp.bfloat16)
        picks.append(picks_ref[at, :, :local_leaves])
    lookup = jnp.concatenate(reach * (leaves // nodes), axis=0)
    lookup_ref[...] = lookup
    pot_ref[...] = jnp.broadcast_to(pot_sorted, pot_ref.shape)

    reach_all[...] = jnp.zeros_like(reach_all)
    live_rounds = jnp.max(info_ref[base + 3 + local_nodes : base + 4 + local_nodes, :LANES])

    def sum_rounds(number):
        gains = []
        for at in range(number):
            rows = slice(at * local_leaves, (at + 1) * local_leaves)
            live = info_ref[rounds + at : rounds + at + 1, :]
            strat = jnp.dot(picks[0], own_ref[rows, :], preferred_element_type=jnp.float32)
            for pick, pack in zip(picks[1:], came):
                strat = strat + jnp.dot(pick, pack[rows, :], preferred_element_type=jnp.float32)
            reach_all[at, :, :hands] = (lookup * strat * live[:, :hands]).astype(jnp.bfloat16)
        for at in range(number):
            live = info_ref[rounds + at : rounds + at + 1, :]
            shown = jnp.dot(reach_all[at], payoff_ref[at], preferred_element_type=jnp.float32)
            value = shown * pot_sorted
            best = value[:nodes]
            for row in range(nodes, leaves, nodes):
                best = jnp.maximum(best, value[row : row + nodes])
            gains.append(best * (live * info_ref[base : base + 1, :]))
        total[...] = sum(gains[1:], gains[0])

    total[...] = jnp.zeros_like(total)
    for number in range(1, rounds - 1):
        pl.when(live_rounds == number)(functools.partial(sum_rounds, number))
    if rounds > 1:
        pl.when(live_rounds >= rounds - 1)(functools.partial(sum_rounds, rounds - 1))


def tail_kernel(rounds, seq_count, nodes, *refs):
    payoff_ref, info_ref, own_ref = refs[:3]
    came = refs[3 : 2 + seq_count]
    before_ref, picks_ref, pot_ref, lookup_ref = refs[2 + seq_count : 6 + seq_count]
    outs, (total, reach_all) = refs[6 + seq_count : -2], refs[-2:]
    hands = own_ref.shape[-1]
    padded = payoff_ref.shape[-1]
    leaves = lookup_ref.shape[0]
    local_leaves, local_nodes = leaves // seq_count, nodes // seq_count
    base = 2 * rounds
    last = rounds - 1
    live_rounds = jnp.max(info_ref[base + 3 + local_nodes : base + 4 + local_nodes, :LANES])
    total[...] = before_ref[...]

    @pl.when(live_rounds > last)
    def _():
        reach_all[...] = jnp.zeros_like(reach_all)
        live = info_ref[rounds + last : rounds + last + 1, :]
        own = own_ref[last * local_leaves : rounds * local_leaves, :]
        strat = jnp.dot(picks_ref[0, :, :local_leaves], own, preferred_element_type=jnp.float32)
        for at, block in enumerate(came, 1):
            pick = picks_ref[at, :, :local_leaves]
            strat = strat + jnp.dot(pick, block[...], preferred_element_type=jnp.float32)
        reach_all[:, :hands] = (lookup_ref[...] * strat * live[:, :hands]).astype(jnp.bfloat16)
        shown = jnp.dot(reach_all[...], payoff_ref[last], preferred_element_type=jnp.float32)
        value = shown * pot_ref[:, :1]
        best = value[:nodes]
        for row in range(nodes, leaves, nodes):
            best = jnp.maximum(best, value[row : row + nodes])
        total[...] += best * (live * info_ref[base : base + 1, :])

    short = round_up(local_nodes, 8) - local_nodes
    for step in range(seq_count):
        rows = total[step * local_nodes : (step + 1) * local_nodes, :]
        if short:
            rows = jnp.concatenate([rows, jnp.zeros((short, padded), jnp.float32)], axis=0)
        for at, tile in enumerate(pack_tiles(rows, local_nodes, hands)):
            outs[step][at] = tile


def share_kernel(rows, hands, tiles_ref, out_ref, tmp, sem):
    tiles = [tiles_ref[at] for at in range(tile_count(rows, hands))]
    for at, group in enumerate(unpack_tiles(tiles, rows, hands)):
        for row in range(8 * at, min(8 * at + 8, rows)):
            tmp[row] = group[row - 8 * at : row - 8 * at + 1]
    copy = pltpu.make_async_copy(tmp, out_ref, sem)
    copy.start()
    copy.wait()


def root_kernel(rows, hands, mine_ref, other_ref, out_ref, tmp, sem):
    first = lax.rem(lax.axis_index("board"), 2) == 0
    lower = jnp.where(first, mine_ref[...], other_ref[...])
    upper = jnp.where(first, other_ref[...], mine_ref[...])
    half = mine_ref.shape[0]
    count = tile_count(rows, hands)
    tiles = [lower[at] for at in range(half)] + [upper[at] for at in range(count - half)]
    for at, group in enumerate(unpack_tiles(tiles, rows, hands)):
        height = min(8, rows - 8 * at)
        tmp[8 * at : 8 * at + height, :] = group[:height]
    copy = pltpu.make_async_copy(tmp, out_ref, sem)
    copy.start()
    copy.wait()


def body(
    board_cards, hand_ranks, river_count, reach_in, strategy, parent_node, pot_size, flop_weight
):
    seq_count = lax.axis_size("seq")
    seq_here = lax.axis_index("seq")
    board_count = lax.axis_size("board")
    rivers, local_leaves, hands = strategy.shape[1:]
    local_nodes = reach_in.shape[1]
    nodes, leaves = local_nodes * seq_count, local_leaves * seq_count
    rounds = -(-rivers // seq_count)
    padded = round_up(hands, LANES)
    anywhere = pl.BlockSpec(memory_space=pltpu.HBM)
    vmem = pl.BlockSpec(memory_space=pltpu.VMEM)
    params = pltpu.CompilerParams(vmem_limit_bytes=16 * MIB)

    def shift(array, step):
        return lax.ppermute(
            array, "seq", [(at, (at + step) % seq_count) for at in range(seq_count)]
        )

    def strategy_for(step):
        owner = (seq_here + step) % seq_count
        if rivers % seq_count == 0:
            split = strategy.reshape(rounds, seq_count, local_leaves, hands)
            rows = lax.dynamic_slice_in_dim(split, owner, 1, axis=1)
        else:
            picked = [
                lax.dynamic_slice_in_dim(
                    strategy[0], jnp.minimum(at * seq_count + owner, rivers - 1), 1, axis=0
                )
                for at in range(rounds)
            ]
            rows = jnp.concatenate(picked, axis=0)
        return rows.reshape(rounds * local_leaves, hands)

    own = strategy_for(0)
    last = rounds - 1
    sent = [strategy_for(step) for step in range(1, seq_count)]
    own, *sent = lax.optimization_barrier((own, *sent))
    came_head = [shift(rows[: last * local_leaves], step) for step, rows in enumerate(sent, 1)]

    small_rows = round_up(local_nodes + 4, 16)
    info_rows = round_up(2 * rounds + 4 + local_nodes, 8)
    small, info = pl.pallas_call(
        functools.partial(pack_kernel, rounds, seq_count),
        out_shape=[
            jax.ShapeDtypeStruct((small_rows, hands), jnp.bfloat16),
            jax.ShapeDtypeStruct((info_rows, padded), jnp.float32),
        ],
        in_specs=[anywhere] * 6,
        out_specs=[anywhere] * 2,
        scratch_shapes=[
            pltpu.VMEM(reach_in.shape, jnp.bfloat16),
            pltpu.VMEM((1, local_leaves), jnp.int32),
            pltpu.VMEM((1, local_leaves), jnp.float32),
            pltpu.VMEM((rivers, 1, hands), jnp.int32),
            pltpu.SMEM((board_cards.shape[2], 1, rivers), jnp.int32),
            pltpu.SMEM((1,), jnp.int32),
            pltpu.VMEM((small_rows, hands), jnp.bfloat16),
            pltpu.VMEM((info_rows, padded), jnp.float32),
            pltpu.SemaphoreType.DMA((6,)),
            pltpu.SemaphoreType.DMA((2,)),
        ],
        compiler_params=pltpu.CompilerParams(vmem_limit_bytes=60 * MIB),
        name="pack",
    )(
        reach_in,
        parent_node[None],
        pot_size[None],
        hand_ranks.transpose(1, 0, 2),
        board_cards.transpose(2, 0, 1),
        river_count,
    )
    smalls = [shift(small, step) for step in range(1, seq_count)]
    *sent, info = lax.optimization_barrier((*sent, info))
    came_tail = [shift(rows[last * local_leaves :], step) for step, rows in enumerate(sent, 1)]

    payoff, info = pl.pallas_call(
        functools.partial(build_kernel, rounds),
        out_shape=[
            jax.ShapeDtypeStruct((rounds, padded, padded), jnp.bfloat16),
            jax.ShapeDtypeStruct((info_rows, padded), jnp.float32),
        ],
        in_specs=[vmem],
        out_specs=[vmem] * 2,
        scratch_shapes=[
            pltpu.VMEM((rounds, 16, padded), jnp.bfloat16),
            pltpu.VMEM((rounds, 16, padded), jnp.bfloat16),
            pltpu.VMEM((round_up(DECK + 1, 16), padded), jnp.bfloat16),
            pltpu.VMEM((round_up(DECK + 1, 16), padded), jnp.bfloat16),
        ],
        compiler_params=pltpu.CompilerParams(vmem_limit_bytes=30 * MIB),
        cost_estimate=pl.CostEstimate(
            flops=10 * rounds * padded * padded, bytes_accessed=4 * padded * padded, transcendentals=0
        ),
        name="build",
    )(info)

    count = tile_count(local_nodes, hands)
    total, *labels = pl.pallas_call(
        functools.partial(head_kernel, rounds, seq_count, nodes, leaves),
        out_shape=[
            jax.ShapeDtypeStruct((nodes, padded), jnp.float32),
            jax.ShapeDtypeStruct((seq_count, leaves, LANES), jnp.bfloat16),
            jax.ShapeDtypeStruct((leaves, LANES), jnp.float32),
            jax.ShapeDtypeStruct((leaves, hands), jnp.float32),
        ],
        in_specs=[vmem] * (1 + 2 * seq_count),
        out_specs=[vmem] * 4,
        scratch_shapes=[pltpu.VMEM((max(last, 1), leaves, padded), jnp.bfloat16)],
        compiler_params=params,
        cost_estimate=pl.CostEstimate(
            flops=2 * rounds * leaves * padded * padded, bytes_accessed=2 * rounds * padded * padded, transcendentals=0
        ),
        name="head",
    )(payoff, info, own, *came_head, *smalls)
    shares = pl.pallas_call(
        functools.partial(tail_kernel, rounds, seq_count, nodes),
        out_shape=[jax.ShapeDtypeStruct((count, 8, LANES), jnp.float32)] * seq_count,
        in_specs=[vmem] * (6 + seq_count),
        out_specs=[vmem] * seq_count,
        scratch_shapes=[
            pltpu.VMEM((nodes, padded), jnp.float32),
            pltpu.VMEM((leaves, padded), jnp.bfloat16),
        ],
        compiler_params=params,
        name="tail",
    )(payoff, info, own, *came_tail, total, *labels)

    share = shares[0]
    for step in range(1, seq_count):
        share = share + shift(shares[step], -step)
    def swap(array, step):
        return lax.ppermute(array, "board", [(at, at ^ step) for at in range(board_count)])

    half = -(-count // 2)
    parity = lax.axis_index("board") % 2
    root = share * (flop_weight[0] / board_count)
    if count % 2:
        root = jnp.concatenate([root, jnp.zeros((1, 8, LANES), jnp.float32)], axis=0)
    root = root.reshape(2, half, 8, LANES)
    mine = lax.dynamic_index_in_dim(root, parity, 0, keepdims=False)
    mine = mine + swap(lax.dynamic_index_in_dim(root, 1 - parity, 0, keepdims=False), 1)
    step = 2
    while step < board_count:
        if step == 2 and board_count >= 8:
            near, far, across = [swap(mine, at) for at in (2, 4, 6)]
            mine = (mine + near) + (far + across)
            step *= 4
        else:
            mine = mine + swap(mine, step)
            step *= 2
    other = swap(mine, 1)

    turn_value = pl.pallas_call(
        functools.partial(share_kernel, local_nodes, hands),
        out_shape=jax.ShapeDtypeStruct((local_nodes, 1, hands), jnp.float32),
        in_specs=[vmem],
        out_specs=anywhere,
        scratch_shapes=[
            pltpu.VMEM((local_nodes, 1, hands), jnp.float32),
            pltpu.SemaphoreType.DMA,
        ],
        compiler_params=params,
        name="share",
    )(share)
    root_value = pl.pallas_call(
        functools.partial(root_kernel, local_nodes, hands),
        out_shape=jax.ShapeDtypeStruct((local_nodes, hands), jnp.float32),
        in_specs=[vmem] * 2,
        out_specs=anywhere,
        scratch_shapes=[pltpu.VMEM((local_nodes, hands), jnp.float32), pltpu.SemaphoreType.DMA],
        compiler_params=params,
        name="root",
    )(mine, other)
    return (turn_value.transpose(1, 0, 2), root_value)


def solution(mesh):
    return jax.shard_map(
        body,
        mesh=mesh,
        in_specs=(
            P("board", None, None),
            P("board", None, None),
            P("board"),
            P("board", "seq", None),
            P("board", None, "seq", None),
            P("seq"),
            P("seq"),
            P("board"),
        ),
        out_specs=(P("board", "seq", None), P("seq", None)),
        check_vma=False,
    )
```

```python
import functools

import jax
import jax.numpy as jnp
from jax import lax
from jax.experimental import pallas as pl
from jax.experimental.pallas import tpu as pltpu
from jax.sharding import PartitionSpec as P

DECK = 52
LANES = 128
MIB = 1024 * 1024


def round_up(value, step):
    return -(-value // step) * step


def hand_cards(padded):
    hand = lax.broadcasted_iota(jnp.int32, (1, padded), 1)
    low = jnp.zeros((1, padded), jnp.int32)
    start = jnp.zeros((1, padded), jnp.int32)
    first = 0
    for card in range(DECK - 1):
        if card:
            low = jnp.where(hand >= first, card, low)
            start = jnp.where(hand >= first, first, start)
        first += DECK - 1 - card
    high = hand - start + low + 1
    real = hand < first
    return jnp.where(real, low, -1), jnp.where(real, high, -1)


def pad_rows(rows):
    return 1 << max(rows - 1, 0).bit_length()


def tile_count(rows, hands):
    full, rest = divmod(rows, 8)
    whole, tail = divmod(hands, LANES)
    count = full * whole
    if rest:
        count += -(-whole // (8 // pad_rows(rest)))
    groups = full + (rest > 0)
    if tail:
        count += -(-groups // 2) if tail <= LANES // 2 else groups
    return count


def pack_tiles(value, rows, hands):
    full, rest = divmod(rows, 8)
    whole, tail = divmod(hands, LANES)
    tiles = [
        value[8 * group : 8 * group + 8, LANES * at : LANES * (at + 1)]
        for group in range(full)
        for at in range(whole)
    ]
    if rest:
        part = pad_rows(rest)
        each = 8 // part
        for start in range(0, whole, each):
            pieces = [
                value[8 * full : 8 * full + part, LANES * at : LANES * (at + 1)]
                for at in range(start, min(start + each, whole))
            ]
            if len(pieces) < each:
                pieces.append(jnp.zeros((8 - part * len(pieces), LANES), value.dtype))
            tiles.append(jnp.concatenate(pieces, axis=0) if len(pieces) > 1 else pieces[0])
    if tail:
        groups = full + (rest > 0)
        tails = [value[8 * group : 8 * group + 8, LANES * whole :] for group in range(groups)]
        if tail <= LANES // 2:
            for at in range(0, groups, 2):
                tile = tails[at]
                if at + 1 < groups:
                    tile = tile + pltpu.roll(tails[at + 1], LANES // 2, 1)
                tiles.append(tile)
        else:
            tiles.extend(tails)
    return tiles


def unpack_tiles(tiles, rows, hands):
    full, rest = divmod(rows, 8)
    whole, tail = divmod(hands, LANES)
    groups = [[tiles[group * whole + at] for at in range(whole)] for group in range(full)]
    used = full * whole
    if rest:
        part = pad_rows(rest)
        each = 8 // part
        last = []
        for at in range(whole):
            tile = tiles[used + at // each]
            begin = part * (at % each)
            last.append(pltpu.roll(tile, (8 - begin) % 8, 0) if begin else tile)
        used += -(-whole // each)
        groups.append(last)
    if tail:
        for at, group in enumerate(groups):
            if tail <= LANES // 2:
                tile = tiles[used + at // 2]
                if at % 2:
                    tile = pltpu.roll(tile, LANES // 2, 1)
            else:
                tile = tiles[used + at]
            group.append(tile[:, :tail])
    return [jnp.concatenate(group, axis=1) for group in groups]


def copy_all(pairs, sems):
    copies = [
        pltpu.make_async_copy(source, target, sems.at[at])
        for at, (source, target) in enumerate(pairs)
    ]
    for copy in copies:
        copy.start()
    return copies


def pack_kernel(
    rounds,
    seq_count,
    reach_ref,
    parent_ref,
    pot_ref,
    rank_ref,
    board_ref,
    count_ref,
    small_ref,
    info_ref,
    reach_tmp,
    parent_tmp,
    pot_tmp,
    rank_tmp,
    board_tmp,
    count_tmp,
    small,
    info,
    sems,
    out_sems,
):
    hands, padded = small.shape[-1], info.shape[-1]
    nodes, leaves = reach_tmp.shape[1], parent_tmp.shape[-1]
    rivers = rank_tmp.shape[0]
    here = lax.axis_index("seq")
    loads = copy_all(
        [
            (reach_ref, reach_tmp),
            (parent_ref, parent_tmp),
            (pot_ref, pot_tmp),
            (rank_ref, rank_tmp),
            (board_ref, board_tmp),
            (count_ref, count_tmp),
        ],
        sems,
    )
    low, high = hand_cards(padded)
    info[...] = jnp.zeros_like(info)
    for copy in loads[:3]:
        copy.wait()
    pot = pot_tmp[...]
    parent = parent_tmp[...].astype(jnp.float32)
    reach = reach_tmp[0].astype(jnp.float32)
    top = pot.astype(jnp.bfloat16).astype(jnp.float32)
    middle = (pot - top).astype(jnp.bfloat16).astype(jnp.float32)
    labels = jnp.concatenate([parent, top, middle, pot - top - middle], axis=0)
    rows = [reach, jnp.concatenate([labels, jnp.zeros((4, hands - leaves), jnp.float32)], axis=1)]
    extra = small.shape[0]
    if extra > nodes + 4:
        rows.append(jnp.zeros((extra - nodes - 4, hands), jnp.float32))
    small[...] = jnp.concatenate(rows, axis=0).astype(jnp.bfloat16)
    sent = pltpu.make_async_copy(small, small_ref, out_sems.at[0])
    sent.start()

    for copy in loads[3:]:
        copy.wait()
    live_count = count_tmp[0]
    base = 2 * rounds
    for at in range(rounds):
        river = jnp.minimum(at * seq_count + here, rivers - 1)
        info[at : at + 1, :hands] = rank_tmp[river].astype(jnp.float32)
        alive = jnp.where(at * seq_count + here < live_count, 1.0, 0.0)
        live = jnp.where(low >= 0, alive, 0.0)
        for slot in range(board_tmp.shape[0]):
            card = board_tmp[slot, 0, river]
            live = jnp.where((low == card) | (high == card), 0.0, live)
        info[rounds + at : rounds + at + 1, :] = live
    info[base : base + 1, :] = 1.0 / (hands * jnp.full((1, padded), live_count.astype(jnp.float32)))
    live_rounds = lax.div(live_count - here + seq_count - 1, seq_count)
    info[base + 3 + nodes : base + 4 + nodes, :] = jnp.full(
        (1, padded), live_rounds.astype(jnp.float32)
    )
    info[base + 1 : base + 2, :leaves] = parent
    info[base + 2 : base + 3, :leaves] = pot
    info[base + 3 : base + 3 + nodes, :hands] = reach
    kept = pltpu.make_async_copy(info, info_ref, out_sems.at[1])
    kept.start()
    sent.wait()
    kept.wait()


def build_kernel(rounds, info_ref, payoff_ref, kept_ref, ranks, gaps, holds, lacks):
    padded = payoff_ref.shape[-1]
    kept_ref[...] = info_ref[...]

    low, high = hand_cards(padded)
    card = lax.broadcasted_iota(jnp.int32, (holds.shape[0], padded), 0)
    held = jnp.where((card == low) | (card == high), 1.0, 0.0)
    holds[...] = jnp.where(card == DECK, 1.0, held).astype(jnp.bfloat16)
    lacks[...] = jnp.where(card == DECK, 1.0, -held).astype(jnp.bfloat16)
    row = lax.broadcasted_iota(jnp.int32, (ranks.shape[1], padded), 0)
    for at in range(rounds):
        rank = info_ref[at : at + 1, :]
        top = jnp.floor(rank * (1.0 / LANES)) * LANES
        rest = rank - top
        sides = jnp.where(row % 2 == 0, top, rest)
        ones = jnp.where(row < 4, 1.0, 0.0)
        ranks[at] = jnp.where(row < 2, -sides, ones).astype(jnp.bfloat16)
        gaps[at] = jnp.where(row < 2, ones, jnp.where(row < 4, sides, 0.0)).astype(jnp.bfloat16)

    def product(left, right):
        return lax.dot_general(
            left, right, (((0,), (0,)), ((), ())), preferred_element_type=jnp.float32
        ).astype(jnp.bfloat16)

    for start in range(0, padded, LANES):
        rows = slice(start, start + LANES)
        column = jnp.broadcast_to(info_ref[rounds - 1 : rounds, rows], (LANES, LANES)).T
        for lane in range(0, padded, 2 * LANES):
            here = slice(lane, min(lane + 2 * LANES, padded))
            mask = product(holds[:, rows], lacks[:, here])
            if here.start <= start < here.stop:
                mask = jnp.maximum(mask, 0.0)
            for at in range(rounds):
                if at < rounds - 1:
                    gap = product(ranks[at, :, rows], gaps[at, :, here])
                else:
                    pieces = [
                        (info_ref[at : at + 1, left : left + LANES] - column).astype(jnp.bfloat16)
                        for left in range(here.start, here.stop, LANES)
                    ]
                    gap = jnp.concatenate(pieces, axis=1)
                payoff_ref[at, rows, here] = jnp.maximum(jnp.minimum(gap, mask), -mask)


def head_kernel(rounds, seq_count, nodes, leaves, *refs):
    payoff_ref, info_ref, own_ref = refs[:3]
    came = refs[3 : 2 + seq_count]
    smalls = refs[2 + seq_count : 1 + 2 * seq_count]
    total, picks_ref, pot_ref, lookup_ref, reach_all = refs[1 + 2 * seq_count :]
    hands = own_ref.shape[-1]
    padded = payoff_ref.shape[-1]
    local_leaves, local_nodes = leaves // seq_count, nodes // seq_count
    here = lax.axis_index("seq")
    base = 2 * rounds

    reach, places, pots = [], [], []
    for at in range(seq_count):
        if at == 0:
            reach.append(info_ref[base + 3 : base + 3 + local_nodes, :hands])
            parent = info_ref[base + 1 : base + 2, :LANES]
            pots.append(info_ref[base + 2 : base + 3, :LANES])
        else:
            small = smalls[at - 1][...].astype(jnp.float32)
            reach.append(small[:local_nodes])
            labels = small[local_nodes : local_nodes + 4, :LANES]
            parent = labels[0:1]
            pots.append(labels[1:2] + labels[2:3] + labels[3:4])
        place = parent
        for owner in range(seq_count):
            inside = (parent >= owner * local_nodes) & (parent < (owner + 1) * local_nodes)
            move = (lax.rem(here - owner + seq_count, seq_count) - owner) * local_nodes
            place = jnp.where(inside, parent + move.astype(jnp.float32), place)
        lane = lax.broadcasted_iota(jnp.int32, (1, LANES), 1)
        places.append(jnp.where(lane < local_leaves, place, -1.0))

    sub = lax.broadcasted_iota(jnp.int32, (LANES, LANES), 0)
    lane = lax.broadcasted_iota(jnp.int32, (LANES, LANES), 1)
    columns = [jnp.broadcast_to(place, (LANES, LANES)).T for place in places]
    picks = []
    pot_sorted = jnp.zeros((leaves, 1), jnp.float32)
    target = lax.broadcasted_iota(jnp.int32, (leaves, LANES), 0).astype(jnp.float32)
    for at in range(seq_count):
        nth = jnp.sum(
            jnp.where((columns[at] == places[at]) & (sub < lane), 1.0, 0.0), axis=0, keepdims=True
        )
        for before in range(at):
            nth = nth + jnp.sum(
                jnp.where(columns[before] == places[at], 1.0, 0.0), axis=0, keepdims=True
            )
        slot = jnp.where(places[at] >= 0.0, nth * nodes + places[at], -1.0)
        pick = jnp.where(target == slot, 1.0, 0.0)
        pot_sorted = pot_sorted + jnp.sum(pick * pots[at], axis=1, keepdims=True)
        picks_ref[at] = pick.astype(jnp.bfloat16)
        picks.append(picks_ref[at, :, :local_leaves])
    lookup = jnp.concatenate(reach * (leaves // nodes), axis=0)
    lookup_ref[...] = lookup
    pot_ref[...] = jnp.broadcast_to(pot_sorted, pot_ref.shape)

    reach_all[...] = jnp.zeros_like(reach_all)
    live_rounds = jnp.max(info_ref[base + 3 + local_nodes : base + 4 + local_nodes, :LANES])

    def sum_rounds(number):
        gains = []
        for at in range(number):
            rows = slice(at * local_leaves, (at + 1) * local_leaves)
            live = info_ref[rounds + at : rounds + at + 1, :]
            strat = jnp.dot(picks[0], own_ref[rows, :], preferred_element_type=jnp.float32)
            for pick, pack in zip(picks[1:], came):
                strat = strat + jnp.dot(pick, pack[rows, :], preferred_element_type=jnp.float32)
            reach_all[at, :, :hands] = (lookup * strat * live[:, :hands]).astype(jnp.bfloat16)
        for at in range(number):
            live = info_ref[rounds + at : rounds + at + 1, :]
            shown = jnp.dot(reach_all[at], payoff_ref[at], preferred_element_type=jnp.float32)
            value = shown * pot_sorted
            best = value[:nodes]
            for row in range(nodes, leaves, nodes):
                best = jnp.maximum(best, value[row : row + nodes])
            gains.append(best * (live * info_ref[base : base + 1, :]))
        total[...] = sum(gains[1:], gains[0])

    total[...] = jnp.zeros_like(total)
    for number in range(1, rounds - 1):
        pl.when(live_rounds == number)(functools.partial(sum_rounds, number))
    if rounds > 1:
        pl.when(live_rounds >= rounds - 1)(functools.partial(sum_rounds, rounds - 1))


def tail_kernel(rounds, seq_count, nodes, *refs):
    payoff_ref, info_ref, own_ref = refs[:3]
    came = refs[3 : 2 + seq_count]
    before_ref, picks_ref, pot_ref, lookup_ref = refs[2 + seq_count : 6 + seq_count]
    outs, (total, reach_all) = refs[6 + seq_count : -2], refs[-2:]
    hands = own_ref.shape[-1]
    padded = payoff_ref.shape[-1]
    leaves = lookup_ref.shape[0]
    local_leaves, local_nodes = leaves // seq_count, nodes // seq_count
    base = 2 * rounds
    last = rounds - 1
    live_rounds = jnp.max(info_ref[base + 3 + local_nodes : base + 4 + local_nodes, :LANES])
    total[...] = before_ref[...]

    @pl.when(live_rounds > last)
    def _():
        reach_all[...] = jnp.zeros_like(reach_all)
        live = info_ref[rounds + last : rounds + last + 1, :]
        own = own_ref[last * local_leaves : rounds * local_leaves, :]
        strat = jnp.dot(picks_ref[0, :, :local_leaves], own, preferred_element_type=jnp.float32)
        for at, block in enumerate(came, 1):
            pick = picks_ref[at, :, :local_leaves]
            strat = strat + jnp.dot(pick, block[...], preferred_element_type=jnp.float32)
        reach_all[:, :hands] = (lookup_ref[...] * strat * live[:, :hands]).astype(jnp.bfloat16)
        shown = jnp.dot(reach_all[...], payoff_ref[last], preferred_element_type=jnp.float32)
        value = shown * pot_ref[:, :1]
        best = value[:nodes]
        for row in range(nodes, leaves, nodes):
            best = jnp.maximum(best, value[row : row + nodes])
        total[...] += best * (live * info_ref[base : base + 1, :])

    short = round_up(local_nodes, 8) - local_nodes
    for step in range(seq_count):
        rows = total[step * local_nodes : (step + 1) * local_nodes, :]
        if short:
            rows = jnp.concatenate([rows, jnp.zeros((short, padded), jnp.float32)], axis=0)
        for at, tile in enumerate(pack_tiles(rows, local_nodes, hands)):
            outs[step][at] = tile


def share_kernel(rows, hands, tiles_ref, out_ref, tmp, sem):
    tiles = [tiles_ref[at] for at in range(tile_count(rows, hands))]
    for at, group in enumerate(unpack_tiles(tiles, rows, hands)):
        for row in range(8 * at, min(8 * at + 8, rows)):
            tmp[row] = group[row - 8 * at : row - 8 * at + 1]
    copy = pltpu.make_async_copy(tmp, out_ref, sem)
    copy.start()
    copy.wait()


def root_kernel(rows, hands, mine_ref, other_ref, out_ref, tmp, sem):
    first = lax.rem(lax.axis_index("board"), 2) == 0
    lower = jnp.where(first, mine_ref[...], other_ref[...])
    upper = jnp.where(first, other_ref[...], mine_ref[...])
    half = mine_ref.shape[0]
    count = tile_count(rows, hands)
    tiles = [lower[at] for at in range(half)] + [upper[at] for at in range(count - half)]
    for at, group in enumerate(unpack_tiles(tiles, rows, hands)):
        height = min(8, rows - 8 * at)
        tmp[8 * at : 8 * at + height, :] = group[:height]
    copy = pltpu.make_async_copy(tmp, out_ref, sem)
    copy.start()
    copy.wait()


def body(
    board_cards, hand_ranks, river_count, reach_in, strategy, parent_node, pot_size, flop_weight
):
    seq_count = lax.axis_size("seq")
    seq_here = lax.axis_index("seq")
    board_count = lax.axis_size("board")
    rivers, local_leaves, hands = strategy.shape[1:]
    local_nodes = reach_in.shape[1]
    nodes, leaves = local_nodes * seq_count, local_leaves * seq_count
    rounds = -(-rivers // seq_count)
    padded = round_up(hands, LANES)
    anywhere = pl.BlockSpec(memory_space=pltpu.HBM)
    vmem = pl.BlockSpec(memory_space=pltpu.VMEM)
    params = pltpu.CompilerParams(vmem_limit_bytes=16 * MIB)

    def shift(array, step):
        return lax.ppermute(
            array, "seq", [(at, (at + step) % seq_count) for at in range(seq_count)]
        )

    def strategy_for(step):
        owner = (seq_here + step) % seq_count
        if rivers % seq_count == 0:
            split = strategy.reshape(rounds, seq_count, local_leaves, hands)
            rows = lax.dynamic_slice_in_dim(split, owner, 1, axis=1)
        else:
            picked = [
                lax.dynamic_slice_in_dim(
                    strategy[0], jnp.minimum(at * seq_count + owner, rivers - 1), 1, axis=0
                )
                for at in range(rounds)
            ]
            rows = jnp.concatenate(picked, axis=0)
        return rows.reshape(rounds * local_leaves, hands)

    own = strategy_for(0)
    last = rounds - 1
    sent = [strategy_for(step) for step in range(1, seq_count)]
    own, *sent = lax.optimization_barrier((own, *sent))
    came_head = [shift(rows[: last * local_leaves], step) for step, rows in enumerate(sent, 1)]

    small_rows = round_up(local_nodes + 4, 16)
    info_rows = round_up(2 * rounds + 4 + local_nodes, 8)
    small, info = pl.pallas_call(
        functools.partial(pack_kernel, rounds, seq_count),
        out_shape=[
            jax.ShapeDtypeStruct((small_rows, hands), jnp.bfloat16),
            jax.ShapeDtypeStruct((info_rows, padded), jnp.float32),
        ],
        in_specs=[anywhere] * 6,
        out_specs=[anywhere] * 2,
        scratch_shapes=[
            pltpu.VMEM(reach_in.shape, jnp.bfloat16),
            pltpu.VMEM((1, local_leaves), jnp.int32),
            pltpu.VMEM((1, local_leaves), jnp.float32),
            pltpu.VMEM((rivers, 1, hands), jnp.int32),
            pltpu.SMEM((board_cards.shape[2], 1, rivers), jnp.int32),
            pltpu.SMEM((1,), jnp.int32),
            pltpu.VMEM((small_rows, hands), jnp.bfloat16),
            pltpu.VMEM((info_rows, padded), jnp.float32),
            pltpu.SemaphoreType.DMA((6,)),
            pltpu.SemaphoreType.DMA((2,)),
        ],
        compiler_params=pltpu.CompilerParams(vmem_limit_bytes=60 * MIB),
        name="pack",
    )(
        reach_in,
        parent_node[None],
        pot_size[None],
        hand_ranks.transpose(1, 0, 2),
        board_cards.transpose(2, 0, 1),
        river_count,
    )
    smalls = [shift(small, step) for step in range(1, seq_count)]
    *sent, info = lax.optimization_barrier((*sent, info))
    came_tail = [shift(rows[last * local_leaves :], step) for step, rows in enumerate(sent, 1)]

    payoff, info = pl.pallas_call(
        functools.partial(build_kernel, rounds),
        out_shape=[
            jax.ShapeDtypeStruct((rounds, padded, padded), jnp.bfloat16),
            jax.ShapeDtypeStruct((info_rows, padded), jnp.float32),
        ],
        in_specs=[vmem],
        out_specs=[vmem] * 2,
        scratch_shapes=[
            pltpu.VMEM((rounds, 16, padded), jnp.bfloat16),
            pltpu.VMEM((rounds, 16, padded), jnp.bfloat16),
            pltpu.VMEM((round_up(DECK + 1, 16), padded), jnp.bfloat16),
            pltpu.VMEM((round_up(DECK + 1, 16), padded), jnp.bfloat16),
        ],
        compiler_params=pltpu.CompilerParams(vmem_limit_bytes=30 * MIB),
        cost_estimate=pl.CostEstimate(
            flops=10 * rounds * padded * padded, bytes_accessed=4 * padded * padded, transcendentals=0
        ),
        name="build",
    )(info)

    count = tile_count(local_nodes, hands)
    total, *labels = pl.pallas_call(
        functools.partial(head_kernel, rounds, seq_count, nodes, leaves),
        out_shape=[
            jax.ShapeDtypeStruct((nodes, padded), jnp.float32),
            jax.ShapeDtypeStruct((seq_count, leaves, LANES), jnp.bfloat16),
            jax.ShapeDtypeStruct((leaves, LANES), jnp.float32),
            jax.ShapeDtypeStruct((leaves, hands), jnp.float32),
        ],
        in_specs=[vmem] * (1 + 2 * seq_count),
        out_specs=[vmem] * 4,
        scratch_shapes=[pltpu.VMEM((max(last, 1), leaves, padded), jnp.bfloat16)],
        compiler_params=params,
        cost_estimate=pl.CostEstimate(
            flops=2 * rounds * leaves * padded * padded, bytes_accessed=2 * rounds * padded * padded, transcendentals=0
        ),
        name="head",
    )(payoff, info, own, *came_head, *smalls)
    shares = pl.pallas_call(
        functools.partial(tail_kernel, rounds, seq_count, nodes),
        out_shape=[jax.ShapeDtypeStruct((count, 8, LANES), jnp.float32)] * seq_count,
        in_specs=[vmem] * (6 + seq_count),
        out_specs=[vmem] * seq_count,
        scratch_shapes=[
            pltpu.VMEM((nodes, padded), jnp.float32),
            pltpu.VMEM((leaves, padded), jnp.bfloat16),
        ],
        compiler_params=params,
        name="tail",
    )(payoff, info, own, *came_tail, total, *labels)

    share = shares[0]
    for step in range(1, seq_count):
        share = share + shift(shares[step], -step)
    def swap(array, step):
        return lax.ppermute(array, "board", [(at, at ^ step) for at in range(board_count)])

    half = -(-count // 2)
    parity = lax.axis_index("board") % 2
    root = share * (flop_weight[0] / board_count)
    if count % 2:
        root = jnp.concatenate([root, jnp.zeros((1, 8, LANES), jnp.float32)], axis=0)
    root = root.reshape(2, half, 8, LANES)
    mine = lax.dynamic_index_in_dim(root, parity, 0, keepdims=False)
    mine = mine + swap(lax.dynamic_index_in_dim(root, 1 - parity, 0, keepdims=False), 1)
    step = 2
    while step < board_count:
        if step == 2 and board_count >= 8:
            near, far, across = [swap(mine, at) for at in (2, 4, 6)]
            mine = (mine + near) + (far + across)
            step *= 4
        else:
            mine = mine + swap(mine, step)
            step *= 2
    other = swap(mine, 1)

    turn_value = pl.pallas_call(
        functools.partial(share_kernel, local_nodes, hands),
        out_shape=jax.ShapeDtypeStruct((local_nodes, 1, hands), jnp.float32),
        in_specs=[vmem],
        out_specs=anywhere,
        scratch_shapes=[
            pltpu.VMEM((local_nodes, 1, hands), jnp.float32),
            pltpu.SemaphoreType.DMA,
        ],
        compiler_params=params,
        name="share",
    )(share)
    root_value = pl.pallas_call(
        functools.partial(root_kernel, local_nodes, hands),
        out_shape=jax.ShapeDtypeStruct((local_nodes, hands), jnp.float32),
        in_specs=[vmem] * 2,
        out_specs=anywhere,
        scratch_shapes=[pltpu.VMEM((local_nodes, hands), jnp.float32), pltpu.SemaphoreType.DMA],
        compiler_params=params,
        name="root",
    )(mine, other)
    return (turn_value.transpose(1, 0, 2), root_value)


def solution(mesh):
    return jax.shard_map(
        body,
        mesh=mesh,
        in_specs=(
            P("board", None, None),
            P("board", None, None),
            P("board"),
            P("board", "seq", None),
            P("board", None, "seq", None),
            P("seq"),
            P("seq"),
            P("board"),
        ),
        out_specs=(P("board", "seq", None), P("seq", None)),
        check_vma=False,
    )
```

```python
import functools

import jax
import jax.numpy as jnp
from jax import lax
from jax.experimental import pallas as pl
from jax.experimental.pallas import tpu as pltpu
from jax.sharding import PartitionSpec as P

DECK = 52
LANES = 128
MIB = 1024 * 1024


def round_up(value, step):
    return -(-value // step) * step


def hand_cards(padded):
    hand = lax.broadcasted_iota(jnp.int32, (1, padded), 1)
    low = jnp.zeros((1, padded), jnp.int32)
    start = jnp.zeros((1, padded), jnp.int32)
    first = 0
    for card in range(DECK - 1):
        if card:
            low = jnp.where(hand >= first, card, low)
            start = jnp.where(hand >= first, first, start)
        first += DECK - 1 - card
    high = hand - start + low + 1
    real = hand < first
    return jnp.where(real, low, -1), jnp.where(real, high, -1)


def pad_rows(rows):
    return 1 << max(rows - 1, 0).bit_length()


def tile_count(rows, hands):
    full, rest = divmod(rows, 8)
    whole, tail = divmod(hands, LANES)
    count = full * whole
    if rest:
        count += -(-whole // (8 // pad_rows(rest)))
    groups = full + (rest > 0)
    if tail:
        count += -(-groups // 2) if tail <= LANES // 2 else groups
    return count


def pack_tiles(value, rows, hands):
    full, rest = divmod(rows, 8)
    whole, tail = divmod(hands, LANES)
    tiles = [
        value[8 * group : 8 * group + 8, LANES * at : LANES * (at + 1)]
        for group in range(full)
        for at in range(whole)
    ]
    if rest:
        part = pad_rows(rest)
        each = 8 // part
        for start in range(0, whole, each):
            pieces = [
                value[8 * full : 8 * full + part, LANES * at : LANES * (at + 1)]
                for at in range(start, min(start + each, whole))
            ]
            if len(pieces) < each:
                pieces.append(jnp.zeros((8 - part * len(pieces), LANES), value.dtype))
            tiles.append(jnp.concatenate(pieces, axis=0) if len(pieces) > 1 else pieces[0])
    if tail:
        groups = full + (rest > 0)
        tails = [value[8 * group : 8 * group + 8, LANES * whole :] for group in range(groups)]
        if tail <= LANES // 2:
            for at in range(0, groups, 2):
                tile = tails[at]
                if at + 1 < groups:
                    tile = tile + pltpu.roll(tails[at + 1], LANES // 2, 1)
                tiles.append(tile)
        else:
            tiles.extend(tails)
    return tiles


def unpack_tiles(tiles, rows, hands):
    full, rest = divmod(rows, 8)
    whole, tail = divmod(hands, LANES)
    groups = [[tiles[group * whole + at] for at in range(whole)] for group in range(full)]
    used = full * whole
    if rest:
        part = pad_rows(rest)
        each = 8 // part
        last = []
        for at in range(whole):
            tile = tiles[used + at // each]
            begin = part * (at % each)
            last.append(pltpu.roll(tile, (8 - begin) % 8, 0) if begin else tile)
        used += -(-whole // each)
        groups.append(last)
    if tail:
        for at, group in enumerate(groups):
            if tail <= LANES // 2:
                tile = tiles[used + at // 2]
                if at % 2:
                    tile = pltpu.roll(tile, LANES // 2, 1)
            else:
                tile = tiles[used + at]
            group.append(tile[:, :tail])
    return [jnp.concatenate(group, axis=1) for group in groups]


def copy_all(pairs, sems):
    copies = [
        pltpu.make_async_copy(source, target, sems.at[at])
        for at, (source, target) in enumerate(pairs)
    ]
    for copy in copies:
        copy.start()
    return copies


def pack_kernel(
    rounds,
    seq_count,
    reach_ref,
    parent_ref,
    pot_ref,
    rank_ref,
    board_ref,
    count_ref,
    small_ref,
    info_ref,
    reach_tmp,
    parent_tmp,
    pot_tmp,
    rank_tmp,
    board_tmp,
    count_tmp,
    small,
    info,
    sems,
    out_sems,
):
    hands, padded = small.shape[-1], info.shape[-1]
    nodes, leaves = reach_tmp.shape[1], parent_tmp.shape[-1]
    rivers = rank_tmp.shape[0]
    here = lax.axis_index("seq")
    loads = copy_all(
        [
            (reach_ref, reach_tmp),
            (parent_ref, parent_tmp),
            (pot_ref, pot_tmp),
            (rank_ref, rank_tmp),
            (board_ref, board_tmp),
            (count_ref, count_tmp),
        ],
        sems,
    )
    low, high = hand_cards(padded)
    info[...] = jnp.zeros_like(info)
    for copy in loads[:3]:
        copy.wait()
    pot = pot_tmp[...]
    parent = parent_tmp[...].astype(jnp.float32)
    reach = reach_tmp[0].astype(jnp.float32)
    top = pot.astype(jnp.bfloat16).astype(jnp.float32)
    middle = (pot - top).astype(jnp.bfloat16).astype(jnp.float32)
    labels = jnp.concatenate([parent, top, middle, pot - top - middle], axis=0)
    rows = [reach, jnp.concatenate([labels, jnp.zeros((4, hands - leaves), jnp.float32)], axis=1)]
    extra = small.shape[0]
    if extra > nodes + 4:
        rows.append(jnp.zeros((extra - nodes - 4, hands), jnp.float32))
    small[...] = jnp.concatenate(rows, axis=0).astype(jnp.bfloat16)
    sent = pltpu.make_async_copy(small, small_ref, out_sems.at[0])
    sent.start()

    for copy in loads[3:]:
        copy.wait()
    live_count = count_tmp[0]
    base = 2 * rounds
    for at in range(rounds):
        river = jnp.minimum(at * seq_count + here, rivers - 1)
        info[at : at + 1, :hands] = rank_tmp[river].astype(jnp.float32)
        alive = jnp.where(at * seq_count + here < live_count, 1.0, 0.0)
        live = jnp.where(low >= 0, alive, 0.0)
        for slot in range(board_tmp.shape[0]):
            card = board_tmp[slot, 0, river]
            live = jnp.where((low == card) | (high == card), 0.0, live)
        info[rounds + at : rounds + at + 1, :] = live
    info[base : base + 1, :] = 1.0 / (hands * jnp.full((1, padded), live_count.astype(jnp.float32)))
    live_rounds = lax.div(live_count - here + seq_count - 1, seq_count)
    info[base + 3 + nodes : base + 4 + nodes, :] = jnp.full(
        (1, padded), live_rounds.astype(jnp.float32)
    )
    info[base + 1 : base + 2, :leaves] = parent
    info[base + 2 : base + 3, :leaves] = pot
    info[base + 3 : base + 3 + nodes, :hands] = reach
    kept = pltpu.make_async_copy(info, info_ref, out_sems.at[1])
    kept.start()
    sent.wait()
    kept.wait()


def build_kernel(rounds, info_ref, payoff_ref, kept_ref, ranks, gaps, holds, lacks):
    padded = payoff_ref.shape[-1]
    kept_ref[...] = info_ref[...]

    low, high = hand_cards(padded)
    card = lax.broadcasted_iota(jnp.int32, (holds.shape[0], padded), 0)
    held = jnp.where((card == low) | (card == high), 1.0, 0.0)
    holds[...] = jnp.where(card == DECK, 1.0, held).astype(jnp.bfloat16)
    lacks[...] = jnp.where(card == DECK, 1.0, -held).astype(jnp.bfloat16)
    row = lax.broadcasted_iota(jnp.int32, (ranks.shape[1], padded), 0)
    for at in range(rounds):
        rank = info_ref[at : at + 1, :]
        top = jnp.floor(rank * (1.0 / LANES)) * LANES
        rest = rank - top
        sides = jnp.where(row % 2 == 0, top, rest)
        ones = jnp.where(row < 4, 1.0, 0.0)
        ranks[at] = jnp.where(row < 2, -sides, ones).astype(jnp.bfloat16)
        gaps[at] = jnp.where(row < 2, ones, jnp.where(row < 4, sides, 0.0)).astype(jnp.bfloat16)

    def product(left, right):
        return lax.dot_general(
            left, right, (((0,), (0,)), ((), ())), preferred_element_type=jnp.float32
        ).astype(jnp.bfloat16)

    for start in range(0, padded, LANES):
        rows = slice(start, start + LANES)
        columns = [
            jnp.broadcast_to(info_ref[at : at + 1, rows], (LANES, LANES)).T
            for at in range(1, rounds)
        ]
        for lane in range(0, padded, 2 * LANES):
            here = slice(lane, min(lane + 2 * LANES, padded))
            mask = product(holds[:, rows], lacks[:, here])
            if here.start <= start < here.stop:
                mask = jnp.maximum(mask, 0.0)
            for at in range(rounds):
                if at == 0:
                    gap = product(ranks[at, :, rows], gaps[at, :, here])
                else:
                    pieces = [
                        (info_ref[at : at + 1, left : left + LANES] - columns[at - 1]).astype(
                            jnp.bfloat16
                        )
                        for left in range(here.start, here.stop, LANES)
                    ]
                    gap = jnp.concatenate(pieces, axis=1)
                payoff_ref[at, rows, here] = jnp.maximum(jnp.minimum(gap, mask), -mask)


def head_kernel(rounds, seq_count, nodes, leaves, *refs):
    payoff_ref, info_ref, own_ref = refs[:3]
    came = refs[3 : 2 + seq_count]
    smalls = refs[2 + seq_count : 1 + 2 * seq_count]
    total, picks_ref, pot_ref, lookup_ref, reach_all = refs[1 + 2 * seq_count :]
    hands = own_ref.shape[-1]
    padded = payoff_ref.shape[-1]
    local_leaves, local_nodes = leaves // seq_count, nodes // seq_count
    here = lax.axis_index("seq")
    base = 2 * rounds

    reach, places, pots = [], [], []
    for at in range(seq_count):
        if at == 0:
            reach.append(info_ref[base + 3 : base + 3 + local_nodes, :hands])
            parent = info_ref[base + 1 : base + 2, :LANES]
            pots.append(info_ref[base + 2 : base + 3, :LANES])
        else:
            small = smalls[at - 1][...].astype(jnp.float32)
            reach.append(small[:local_nodes])
            labels = small[local_nodes : local_nodes + 4, :LANES]
            parent = labels[0:1]
            pots.append(labels[1:2] + labels[2:3] + labels[3:4])
        place = parent
        for owner in range(seq_count):
            inside = (parent >= owner * local_nodes) & (parent < (owner + 1) * local_nodes)
            move = (lax.rem(here - owner + seq_count, seq_count) - owner) * local_nodes
            place = jnp.where(inside, parent + move.astype(jnp.float32), place)
        lane = lax.broadcasted_iota(jnp.int32, (1, LANES), 1)
        places.append(jnp.where(lane < local_leaves, place, -1.0))

    sub = lax.broadcasted_iota(jnp.int32, (LANES, LANES), 0)
    lane = lax.broadcasted_iota(jnp.int32, (LANES, LANES), 1)
    columns = [jnp.broadcast_to(place, (LANES, LANES)).T for place in places]
    picks = []
    pot_sorted = jnp.zeros((leaves, 1), jnp.float32)
    target = lax.broadcasted_iota(jnp.int32, (leaves, LANES), 0).astype(jnp.float32)
    for at in range(seq_count):
        nth = jnp.sum(
            jnp.where((columns[at] == places[at]) & (sub < lane), 1.0, 0.0), axis=0, keepdims=True
        )
        for before in range(at):
            nth = nth + jnp.sum(
                jnp.where(columns[before] == places[at], 1.0, 0.0), axis=0, keepdims=True
            )
        slot = jnp.where(places[at] >= 0.0, nth * nodes + places[at], -1.0)
        pick = jnp.where(target == slot, 1.0, 0.0)
        pot_sorted = pot_sorted + jnp.sum(pick * pots[at], axis=1, keepdims=True)
        picks_ref[at] = pick.astype(jnp.bfloat16)
        picks.append(picks_ref[at, :, :local_leaves])
    lookup = jnp.concatenate(reach * (leaves // nodes), axis=0)
    lookup_ref[...] = lookup
    pot_ref[...] = jnp.broadcast_to(pot_sorted, pot_ref.shape)

    reach_all[...] = jnp.zeros_like(reach_all)
    live_rounds = jnp.max(info_ref[base + 3 + local_nodes : base + 4 + local_nodes, :LANES])

    def sum_rounds(number):
        gains = []
        for at in range(number):
            rows = slice(at * local_leaves, (at + 1) * local_leaves)
            live = info_ref[rounds + at : rounds + at + 1, :]
            strat = jnp.dot(picks[0], own_ref[rows, :], preferred_element_type=jnp.float32)
            for pick, pack in zip(picks[1:], came):
                strat = strat + jnp.dot(pick, pack[rows, :], preferred_element_type=jnp.float32)
            reach_all[at, :, :hands] = (lookup * strat * live[:, :hands]).astype(jnp.bfloat16)
        for at in range(number):
            live = info_ref[rounds + at : rounds + at + 1, :]
            shown = jnp.dot(reach_all[at], payoff_ref[at], preferred_element_type=jnp.float32)
            value = shown * pot_sorted
            best = value[:nodes]
            for row in range(nodes, leaves, nodes):
                best = jnp.maximum(best, value[row : row + nodes])
            gains.append(best * (live * info_ref[base : base + 1, :]))
        total[...] = sum(gains[1:], gains[0])

    total[...] = jnp.zeros_like(total)
    for number in range(1, rounds - 1):
        pl.when(live_rounds == number)(functools.partial(sum_rounds, number))
    if rounds > 1:
        pl.when(live_rounds >= rounds - 1)(functools.partial(sum_rounds, rounds - 1))


def tail_kernel(rounds, seq_count, nodes, *refs):
    payoff_ref, info_ref, own_ref = refs[:3]
    came = refs[3 : 2 + seq_count]
    before_ref, picks_ref, pot_ref, lookup_ref = refs[2 + seq_count : 6 + seq_count]
    outs, (total, reach_all) = refs[6 + seq_count : -2], refs[-2:]
    hands = own_ref.shape[-1]
    padded = payoff_ref.shape[-1]
    leaves = lookup_ref.shape[0]
    local_leaves, local_nodes = leaves // seq_count, nodes // seq_count
    base = 2 * rounds
    last = rounds - 1
    live_rounds = jnp.max(info_ref[base + 3 + local_nodes : base + 4 + local_nodes, :LANES])
    total[...] = before_ref[...]

    @pl.when(live_rounds > last)
    def _():
        reach_all[...] = jnp.zeros_like(reach_all)
        live = info_ref[rounds + last : rounds + last + 1, :]
        own = own_ref[last * local_leaves : rounds * local_leaves, :]
        strat = jnp.dot(picks_ref[0, :, :local_leaves], own, preferred_element_type=jnp.float32)
        for at, block in enumerate(came, 1):
            pick = picks_ref[at, :, :local_leaves]
            strat = strat + jnp.dot(pick, block[...], preferred_element_type=jnp.float32)
        reach_all[:, :hands] = (lookup_ref[...] * strat * live[:, :hands]).astype(jnp.bfloat16)
        shown = jnp.dot(reach_all[...], payoff_ref[last], preferred_element_type=jnp.float32)
        value = shown * pot_ref[:, :1]
        best = value[:nodes]
        for row in range(nodes, leaves, nodes):
            best = jnp.maximum(best, value[row : row + nodes])
        total[...] += best * (live * info_ref[base : base + 1, :])

    short = round_up(local_nodes, 8) - local_nodes
    for step in range(seq_count):
        rows = total[step * local_nodes : (step + 1) * local_nodes, :]
        if short:
            rows = jnp.concatenate([rows, jnp.zeros((short, padded), jnp.float32)], axis=0)
        for at, tile in enumerate(pack_tiles(rows, local_nodes, hands)):
            outs[step][at] = tile


def share_kernel(rows, hands, tiles_ref, out_ref, tmp, sem):
    tiles = [tiles_ref[at] for at in range(tile_count(rows, hands))]
    for at, group in enumerate(unpack_tiles(tiles, rows, hands)):
        for row in range(8 * at, min(8 * at + 8, rows)):
            tmp[row] = group[row - 8 * at : row - 8 * at + 1]
    copy = pltpu.make_async_copy(tmp, out_ref, sem)
    copy.start()
    copy.wait()


def root_kernel(rows, hands, mine_ref, other_ref, out_ref, tmp, sem):
    first = lax.rem(lax.axis_index("board"), 2) == 0
    lower = jnp.where(first, mine_ref[...], other_ref[...])
    upper = jnp.where(first, other_ref[...], mine_ref[...])
    half = mine_ref.shape[0]
    count = tile_count(rows, hands)
    tiles = [lower[at] for at in range(half)] + [upper[at] for at in range(count - half)]
    for at, group in enumerate(unpack_tiles(tiles, rows, hands)):
        height = min(8, rows - 8 * at)
        tmp[8 * at : 8 * at + height, :] = group[:height]
    copy = pltpu.make_async_copy(tmp, out_ref, sem)
    copy.start()
    copy.wait()


def body(
    board_cards, hand_ranks, river_count, reach_in, strategy, parent_node, pot_size, flop_weight
):
    seq_count = lax.axis_size("seq")
    seq_here = lax.axis_index("seq")
    board_count = lax.axis_size("board")
    rivers, local_leaves, hands = strategy.shape[1:]
    local_nodes = reach_in.shape[1]
    nodes, leaves = local_nodes * seq_count, local_leaves * seq_count
    rounds = -(-rivers // seq_count)
    padded = round_up(hands, LANES)
    anywhere = pl.BlockSpec(memory_space=pltpu.HBM)
    vmem = pl.BlockSpec(memory_space=pltpu.VMEM)
    params = pltpu.CompilerParams(vmem_limit_bytes=16 * MIB)

    def shift(array, step):
        return lax.ppermute(
            array, "seq", [(at, (at + step) % seq_count) for at in range(seq_count)]
        )

    def strategy_for(step):
        owner = (seq_here + step) % seq_count
        if rivers % seq_count == 0:
            split = strategy.reshape(rounds, seq_count, local_leaves, hands)
            rows = lax.dynamic_slice_in_dim(split, owner, 1, axis=1)
        else:
            picked = [
                lax.dynamic_slice_in_dim(
                    strategy[0], jnp.minimum(at * seq_count + owner, rivers - 1), 1, axis=0
                )
                for at in range(rounds)
            ]
            rows = jnp.concatenate(picked, axis=0)
        return rows.reshape(rounds * local_leaves, hands)

    own = strategy_for(0)
    last = rounds - 1
    sent = [strategy_for(step) for step in range(1, seq_count)]
    own, *sent = lax.optimization_barrier((own, *sent))
    came_head = [shift(rows[: last * local_leaves], step) for step, rows in enumerate(sent, 1)]

    small_rows = round_up(local_nodes + 4, 16)
    info_rows = round_up(2 * rounds + 4 + local_nodes, 8)
    small, info = pl.pallas_call(
        functools.partial(pack_kernel, rounds, seq_count),
        out_shape=[
            jax.ShapeDtypeStruct((small_rows, hands), jnp.bfloat16),
            jax.ShapeDtypeStruct((info_rows, padded), jnp.float32),
        ],
        in_specs=[anywhere] * 6,
        out_specs=[anywhere] * 2,
        scratch_shapes=[
            pltpu.VMEM(reach_in.shape, jnp.bfloat16),
            pltpu.VMEM((1, local_leaves), jnp.int32),
            pltpu.VMEM((1, local_leaves), jnp.float32),
            pltpu.VMEM((rivers, 1, hands), jnp.int32),
            pltpu.SMEM((board_cards.shape[2], 1, rivers), jnp.int32),
            pltpu.SMEM((1,), jnp.int32),
            pltpu.VMEM((small_rows, hands), jnp.bfloat16),
            pltpu.VMEM((info_rows, padded), jnp.float32),
            pltpu.SemaphoreType.DMA((6,)),
            pltpu.SemaphoreType.DMA((2,)),
        ],
        compiler_params=pltpu.CompilerParams(vmem_limit_bytes=60 * MIB),
        name="pack",
    )(
        reach_in,
        parent_node[None],
        pot_size[None],
        hand_ranks.transpose(1, 0, 2),
        board_cards.transpose(2, 0, 1),
        river_count,
    )
    smalls = [shift(small, step) for step in range(1, seq_count)]
    *sent, info = lax.optimization_barrier((*sent, info))
    came_tail = [shift(rows[last * local_leaves :], step) for step, rows in enumerate(sent, 1)]

    payoff, info = pl.pallas_call(
        functools.partial(build_kernel, rounds),
        out_shape=[
            jax.ShapeDtypeStruct((rounds, padded, padded), jnp.bfloat16),
            jax.ShapeDtypeStruct((info_rows, padded), jnp.float32),
        ],
        in_specs=[vmem],
        out_specs=[vmem] * 2,
        scratch_shapes=[
            pltpu.VMEM((rounds, 16, padded), jnp.bfloat16),
            pltpu.VMEM((rounds, 16, padded), jnp.bfloat16),
            pltpu.VMEM((round_up(DECK + 1, 16), padded), jnp.bfloat16),
            pltpu.VMEM((round_up(DECK + 1, 16), padded), jnp.bfloat16),
        ],
        compiler_params=pltpu.CompilerParams(vmem_limit_bytes=30 * MIB),
        cost_estimate=pl.CostEstimate(
            flops=10 * rounds * padded * padded, bytes_accessed=4 * padded * padded, transcendentals=0
        ),
        name="build",
    )(info)

    count = tile_count(local_nodes, hands)
    total, *labels = pl.pallas_call(
        functools.partial(head_kernel, rounds, seq_count, nodes, leaves),
        out_shape=[
            jax.ShapeDtypeStruct((nodes, padded), jnp.float32),
            jax.ShapeDtypeStruct((seq_count, leaves, LANES), jnp.bfloat16),
            jax.ShapeDtypeStruct((leaves, LANES), jnp.float32),
            jax.ShapeDtypeStruct((leaves, hands), jnp.float32),
        ],
        in_specs=[vmem] * (1 + 2 * seq_count),
        out_specs=[vmem] * 4,
        scratch_shapes=[pltpu.VMEM((max(last, 1), leaves, padded), jnp.bfloat16)],
        compiler_params=params,
        cost_estimate=pl.CostEstimate(
            flops=2 * rounds * leaves * padded * padded, bytes_accessed=2 * rounds * padded * padded, transcendentals=0
        ),
        name="head",
    )(payoff, info, own, *came_head, *smalls)
    shares = pl.pallas_call(
        functools.partial(tail_kernel, rounds, seq_count, nodes),
        out_shape=[jax.ShapeDtypeStruct((count, 8, LANES), jnp.float32)] * seq_count,
        in_specs=[vmem] * (6 + seq_count),
        out_specs=[vmem] * seq_count,
        scratch_shapes=[
            pltpu.VMEM((nodes, padded), jnp.float32),
            pltpu.VMEM((leaves, padded), jnp.bfloat16),
        ],
        compiler_params=params,
        name="tail",
    )(payoff, info, own, *came_tail, total, *labels)

    share = shares[0]
    for step in range(1, seq_count):
        share = share + shift(shares[step], -step)
    def swap(array, step):
        return lax.ppermute(array, "board", [(at, at ^ step) for at in range(board_count)])

    half = -(-count // 2)
    parity = lax.axis_index("board") % 2
    root = share * (flop_weight[0] / board_count)
    if count % 2:
        root = jnp.concatenate([root, jnp.zeros((1, 8, LANES), jnp.float32)], axis=0)
    root = root.reshape(2, half, 8, LANES)
    mine = lax.dynamic_index_in_dim(root, parity, 0, keepdims=False)
    mine = mine + swap(lax.dynamic_index_in_dim(root, 1 - parity, 0, keepdims=False), 1)
    step = 2
    while step < board_count:
        if step == 2 and board_count >= 8:
            near, far, across = [swap(mine, at) for at in (2, 4, 6)]
            mine = (mine + near) + (far + across)
            step *= 4
        else:
            mine = mine + swap(mine, step)
            step *= 2
    other = swap(mine, 1)

    turn_value = pl.pallas_call(
        functools.partial(share_kernel, local_nodes, hands),
        out_shape=jax.ShapeDtypeStruct((local_nodes, 1, hands), jnp.float32),
        in_specs=[vmem],
        out_specs=anywhere,
        scratch_shapes=[
            pltpu.VMEM((local_nodes, 1, hands), jnp.float32),
            pltpu.SemaphoreType.DMA,
        ],
        compiler_params=params,
        name="share",
    )(share)
    root_value = pl.pallas_call(
        functools.partial(root_kernel, local_nodes, hands),
        out_shape=jax.ShapeDtypeStruct((local_nodes, hands), jnp.float32),
        in_specs=[vmem] * 2,
        out_specs=anywhere,
        scratch_shapes=[pltpu.VMEM((local_nodes, hands), jnp.float32), pltpu.SemaphoreType.DMA],
        compiler_params=params,
        name="root",
    )(mine, other)
    return (turn_value.transpose(1, 0, 2), root_value)


def solution(mesh):
    return jax.shard_map(
        body,
        mesh=mesh,
        in_specs=(
            P("board", None, None),
            P("board", None, None),
            P("board"),
            P("board", "seq", None),
            P("board", None, "seq", None),
            P("seq"),
            P("seq"),
            P("board"),
        ),
        out_specs=(P("board", "seq", None), P("seq", None)),
        check_vma=False,
    )
```

```python
import functools

import jax
import jax.numpy as jnp
from jax import lax
from jax.experimental import pallas as pl
from jax.experimental.pallas import tpu as pltpu
from jax.sharding import PartitionSpec as P

DECK = 52
LANES = 128
MIB = 1024 * 1024


def round_up(value, step):
    return -(-value // step) * step


def hand_cards(padded):
    hand = lax.broadcasted_iota(jnp.int32, (1, padded), 1)
    low = jnp.zeros((1, padded), jnp.int32)
    start = jnp.zeros((1, padded), jnp.int32)
    first = 0
    for card in range(DECK - 1):
        if card:
            low = jnp.where(hand >= first, card, low)
            start = jnp.where(hand >= first, first, start)
        first += DECK - 1 - card
    high = hand - start + low + 1
    real = hand < first
    return jnp.where(real, low, -1), jnp.where(real, high, -1)


def pad_rows(rows):
    return 1 << max(rows - 1, 0).bit_length()


def tile_count(rows, hands):
    full, rest = divmod(rows, 8)
    whole, tail = divmod(hands, LANES)
    count = full * whole
    if rest:
        count += -(-whole // (8 // pad_rows(rest)))
    groups = full + (rest > 0)
    if tail:
        count += -(-groups // 2) if tail <= LANES // 2 else groups
    return count


def pack_tiles(value, rows, hands):
    full, rest = divmod(rows, 8)
    whole, tail = divmod(hands, LANES)
    tiles = [
        value[8 * group : 8 * group + 8, LANES * at : LANES * (at + 1)]
        for group in range(full)
        for at in range(whole)
    ]
    if rest:
        part = pad_rows(rest)
        each = 8 // part
        for start in range(0, whole, each):
            pieces = [
                value[8 * full : 8 * full + part, LANES * at : LANES * (at + 1)]
                for at in range(start, min(start + each, whole))
            ]
            if len(pieces) < each:
                pieces.append(jnp.zeros((8 - part * len(pieces), LANES), value.dtype))
            tiles.append(jnp.concatenate(pieces, axis=0) if len(pieces) > 1 else pieces[0])
    if tail:
        groups = full + (rest > 0)
        tails = [value[8 * group : 8 * group + 8, LANES * whole :] for group in range(groups)]
        if tail <= LANES // 2:
            for at in range(0, groups, 2):
                tile = tails[at]
                if at + 1 < groups:
                    tile = tile + pltpu.roll(tails[at + 1], LANES // 2, 1)
                tiles.append(tile)
        else:
            tiles.extend(tails)
    return tiles


def unpack_tiles(tiles, rows, hands):
    full, rest = divmod(rows, 8)
    whole, tail = divmod(hands, LANES)
    groups = [[tiles[group * whole + at] for at in range(whole)] for group in range(full)]
    used = full * whole
    if rest:
        part = pad_rows(rest)
        each = 8 // part
        last = []
        for at in range(whole):
            tile = tiles[used + at // each]
            begin = part * (at % each)
            last.append(pltpu.roll(tile, (8 - begin) % 8, 0) if begin else tile)
        used += -(-whole // each)
        groups.append(last)
    if tail:
        for at, group in enumerate(groups):
            if tail <= LANES // 2:
                tile = tiles[used + at // 2]
                if at % 2:
                    tile = pltpu.roll(tile, LANES // 2, 1)
            else:
                tile = tiles[used + at]
            group.append(tile[:, :tail])
    return [jnp.concatenate(group, axis=1) for group in groups]


def copy_all(pairs, sems):
    copies = [
        pltpu.make_async_copy(source, target, sems.at[at])
        for at, (source, target) in enumerate(pairs)
    ]
    for copy in copies:
        copy.start()
    return copies


def pack_kernel(
    rounds,
    seq_count,
    reach_ref,
    parent_ref,
    pot_ref,
    rank_ref,
    board_ref,
    count_ref,
    small_ref,
    info_ref,
    reach_tmp,
    parent_tmp,
    pot_tmp,
    rank_tmp,
    board_tmp,
    count_tmp,
    small,
    info,
    sems,
    out_sems,
):
    hands, padded = small.shape[-1], info.shape[-1]
    nodes, leaves = reach_tmp.shape[1], parent_tmp.shape[-1]
    rivers = rank_tmp.shape[0]
    here = lax.axis_index("seq")
    loads = copy_all(
        [
            (reach_ref, reach_tmp),
            (parent_ref, parent_tmp),
            (pot_ref, pot_tmp),
            (rank_ref, rank_tmp),
            (board_ref, board_tmp),
            (count_ref, count_tmp),
        ],
        sems,
    )
    low, high = hand_cards(padded)
    info[...] = jnp.zeros_like(info)
    for copy in loads[:3]:
        copy.wait()
    pot = pot_tmp[...]
    parent = parent_tmp[...].astype(jnp.float32)
    reach = reach_tmp[0].astype(jnp.float32)
    top = pot.astype(jnp.bfloat16).astype(jnp.float32)
    middle = (pot - top).astype(jnp.bfloat16).astype(jnp.float32)
    labels = jnp.concatenate([parent, top, middle, pot - top - middle], axis=0)
    rows = [reach, jnp.concatenate([labels, jnp.zeros((4, hands - leaves), jnp.float32)], axis=1)]
    extra = small.shape[0]
    if extra > nodes + 4:
        rows.append(jnp.zeros((extra - nodes - 4, hands), jnp.float32))
    small[...] = jnp.concatenate(rows, axis=0).astype(jnp.bfloat16)
    sent = pltpu.make_async_copy(small, small_ref, out_sems.at[0])
    sent.start()

    for copy in loads[3:]:
        copy.wait()
    live_count = count_tmp[0]
    base = 2 * rounds
    for at in range(rounds):
        river = jnp.minimum(at * seq_count + here, rivers - 1)
        info[at : at + 1, :hands] = rank_tmp[river].astype(jnp.float32)
        alive = jnp.where(at * seq_count + here < live_count, 1.0, 0.0)
        live = jnp.where(low >= 0, alive, 0.0)
        for slot in range(board_tmp.shape[0]):
            card = board_tmp[slot, 0, river]
            live = jnp.where((low == card) | (high == card), 0.0, live)
        info[rounds + at : rounds + at + 1, :] = live
    info[base : base + 1, :] = 1.0 / (hands * jnp.full((1, padded), live_count.astype(jnp.float32)))
    live_rounds = lax.div(live_count - here + seq_count - 1, seq_count)
    info[base + 3 + nodes : base + 4 + nodes, :] = jnp.full(
        (1, padded), live_rounds.astype(jnp.float32)
    )
    info[base + 1 : base + 2, :leaves] = parent
    info[base + 2 : base + 3, :leaves] = pot
    info[base + 3 : base + 3 + nodes, :hands] = reach
    kept = pltpu.make_async_copy(info, info_ref, out_sems.at[1])
    kept.start()
    sent.wait()
    kept.wait()


def build_kernel(rounds, info_ref, payoff_ref, kept_ref, holds, lacks):
    padded = payoff_ref.shape[-1]
    kept_ref[...] = info_ref[...]

    low, high = hand_cards(padded)
    card = lax.broadcasted_iota(jnp.int32, (holds.shape[0], padded), 0)
    held = jnp.where((card == low) | (card == high), 1.0, 0.0)
    holds[...] = jnp.where(card == DECK, 1.0, held).astype(jnp.bfloat16)
    lacks[...] = jnp.where(card == DECK, 1.0, -held).astype(jnp.bfloat16)
    def product(left, right):
        return lax.dot_general(
            left, right, (((0,), (0,)), ((), ())), preferred_element_type=jnp.float32
        ).astype(jnp.bfloat16)

    for start in range(0, padded, LANES):
        rows = slice(start, start + LANES)
        columns = [
            jnp.broadcast_to(info_ref[at : at + 1, rows], (LANES, LANES)).T
            for at in range(rounds)
        ]
        for lane in range(0, padded, 2 * LANES):
            here = slice(lane, min(lane + 2 * LANES, padded))
            mask = product(holds[:, rows], lacks[:, here])
            if here.start <= start < here.stop:
                mask = jnp.maximum(mask, 0.0)
            for at in range(rounds):
                pieces = [
                    (info_ref[at : at + 1, left : left + LANES] - columns[at]).astype(jnp.bfloat16)
                    for left in range(here.start, here.stop, LANES)
                ]
                gap = jnp.concatenate(pieces, axis=1)
                payoff_ref[at, rows, here] = jnp.maximum(jnp.minimum(gap, mask), -mask)


def head_kernel(rounds, seq_count, nodes, leaves, *refs):
    payoff_ref, info_ref, own_ref = refs[:3]
    came = refs[3 : 2 + seq_count]
    smalls = refs[2 + seq_count : 1 + 2 * seq_count]
    total, picks_ref, pot_ref, lookup_ref, reach_all = refs[1 + 2 * seq_count :]
    hands = own_ref.shape[-1]
    padded = payoff_ref.shape[-1]
    local_leaves, local_nodes = leaves // seq_count, nodes // seq_count
    here = lax.axis_index("seq")
    base = 2 * rounds

    reach, places, pots = [], [], []
    for at in range(seq_count):
        if at == 0:
            reach.append(info_ref[base + 3 : base + 3 + local_nodes, :hands])
            parent = info_ref[base + 1 : base + 2, :LANES]
            pots.append(info_ref[base + 2 : base + 3, :LANES])
        else:
            small = smalls[at - 1][...].astype(jnp.float32)
            reach.append(small[:local_nodes])
            labels = small[local_nodes : local_nodes + 4, :LANES]
            parent = labels[0:1]
            pots.append(labels[1:2] + labels[2:3] + labels[3:4])
        place = parent
        for owner in range(seq_count):
            inside = (parent >= owner * local_nodes) & (parent < (owner + 1) * local_nodes)
            move = (lax.rem(here - owner + seq_count, seq_count) - owner) * local_nodes
            place = jnp.where(inside, parent + move.astype(jnp.float32), place)
        lane = lax.broadcasted_iota(jnp.int32, (1, LANES), 1)
        places.append(jnp.where(lane < local_leaves, place, -1.0))

    sub = lax.broadcasted_iota(jnp.int32, (LANES, LANES), 0)
    lane = lax.broadcasted_iota(jnp.int32, (LANES, LANES), 1)
    columns = [jnp.broadcast_to(place, (LANES, LANES)).T for place in places]
    picks = []
    pot_sorted = jnp.zeros((leaves, 1), jnp.float32)
    target = lax.broadcasted_iota(jnp.int32, (leaves, LANES), 0).astype(jnp.float32)
    for at in range(seq_count):
        nth = jnp.sum(
            jnp.where((columns[at] == places[at]) & (sub < lane), 1.0, 0.0), axis=0, keepdims=True
        )
        for before in range(at):
            nth = nth + jnp.sum(
                jnp.where(columns[before] == places[at], 1.0, 0.0), axis=0, keepdims=True
            )
        slot = jnp.where(places[at] >= 0.0, nth * nodes + places[at], -1.0)
        pick = jnp.where(target == slot, 1.0, 0.0)
        pot_sorted = pot_sorted + jnp.sum(pick * pots[at], axis=1, keepdims=True)
        picks_ref[at] = pick.astype(jnp.bfloat16)
        picks.append(picks_ref[at, :, :local_leaves])
    lookup = jnp.concatenate(reach * (leaves // nodes), axis=0)
    lookup_ref[...] = lookup
    pot_ref[...] = jnp.broadcast_to(pot_sorted, pot_ref.shape)

    reach_all[...] = jnp.zeros_like(reach_all)
    live_rounds = jnp.max(info_ref[base + 3 + local_nodes : base + 4 + local_nodes, :LANES])

    def sum_rounds(number):
        gains = []
        for at in range(number):
            rows = slice(at * local_leaves, (at + 1) * local_leaves)
            live = info_ref[rounds + at : rounds + at + 1, :]
            strat = jnp.dot(picks[0], own_ref[rows, :], preferred_element_type=jnp.float32)
            for pick, pack in zip(picks[1:], came):
                strat = strat + jnp.dot(pick, pack[rows, :], preferred_element_type=jnp.float32)
            reach_all[at, :, :hands] = (lookup * strat * live[:, :hands]).astype(jnp.bfloat16)
        for at in range(number):
            live = info_ref[rounds + at : rounds + at + 1, :]
            shown = jnp.dot(reach_all[at], payoff_ref[at], preferred_element_type=jnp.float32)
            value = shown * pot_sorted
            best = value[:nodes]
            for row in range(nodes, leaves, nodes):
                best = jnp.maximum(best, value[row : row + nodes])
            gains.append(best * (live * info_ref[base : base + 1, :]))
        total[...] = sum(gains[1:], gains[0])

    total[...] = jnp.zeros_like(total)
    for number in range(1, rounds - 1):
        pl.when(live_rounds == number)(functools.partial(sum_rounds, number))
    if rounds > 1:
        pl.when(live_rounds >= rounds - 1)(functools.partial(sum_rounds, rounds - 1))


def tail_kernel(rounds, seq_count, nodes, *refs):
    payoff_ref, info_ref, own_ref = refs[:3]
    came = refs[3 : 2 + seq_count]
    before_ref, picks_ref, pot_ref, lookup_ref = refs[2 + seq_count : 6 + seq_count]
    outs, (total, reach_all) = refs[6 + seq_count : -2], refs[-2:]
    hands = own_ref.shape[-1]
    padded = payoff_ref.shape[-1]
    leaves = lookup_ref.shape[0]
    local_leaves, local_nodes = leaves // seq_count, nodes // seq_count
    base = 2 * rounds
    last = rounds - 1
    live_rounds = jnp.max(info_ref[base + 3 + local_nodes : base + 4 + local_nodes, :LANES])
    total[...] = before_ref[...]

    @pl.when(live_rounds > last)
    def _():
        reach_all[...] = jnp.zeros_like(reach_all)
        live = info_ref[rounds + last : rounds + last + 1, :]
        own = own_ref[last * local_leaves : rounds * local_leaves, :]
        strat = jnp.dot(picks_ref[0, :, :local_leaves], own, preferred_element_type=jnp.float32)
        for at, block in enumerate(came, 1):
            pick = picks_ref[at, :, :local_leaves]
            strat = strat + jnp.dot(pick, block[...], preferred_element_type=jnp.float32)
        reach_all[:, :hands] = (lookup_ref[...] * strat * live[:, :hands]).astype(jnp.bfloat16)
        shown = jnp.dot(reach_all[...], payoff_ref[last], preferred_element_type=jnp.float32)
        value = shown * pot_ref[:, :1]
        best = value[:nodes]
        for row in range(nodes, leaves, nodes):
            best = jnp.maximum(best, value[row : row + nodes])
        total[...] += best * (live * info_ref[base : base + 1, :])

    short = round_up(local_nodes, 8) - local_nodes
    for step in range(seq_count):
        rows = total[step * local_nodes : (step + 1) * local_nodes, :]
        if short:
            rows = jnp.concatenate([rows, jnp.zeros((short, padded), jnp.float32)], axis=0)
        for at, tile in enumerate(pack_tiles(rows, local_nodes, hands)):
            outs[step][at] = tile


def share_kernel(rows, hands, tiles_ref, out_ref, tmp, sem):
    tiles = [tiles_ref[at] for at in range(tile_count(rows, hands))]
    for at, group in enumerate(unpack_tiles(tiles, rows, hands)):
        for row in range(8 * at, min(8 * at + 8, rows)):
            tmp[row] = group[row - 8 * at : row - 8 * at + 1]
    copy = pltpu.make_async_copy(tmp, out_ref, sem)
    copy.start()
    copy.wait()


def root_kernel(rows, hands, mine_ref, other_ref, out_ref, tmp, sem):
    first = lax.rem(lax.axis_index("board"), 2) == 0
    lower = jnp.where(first, mine_ref[...], other_ref[...])
    upper = jnp.where(first, other_ref[...], mine_ref[...])
    half = mine_ref.shape[0]
    count = tile_count(rows, hands)
    tiles = [lower[at] for at in range(half)] + [upper[at] for at in range(count - half)]
    for at, group in enumerate(unpack_tiles(tiles, rows, hands)):
        height = min(8, rows - 8 * at)
        tmp[8 * at : 8 * at + height, :] = group[:height]
    copy = pltpu.make_async_copy(tmp, out_ref, sem)
    copy.start()
    copy.wait()


def body(
    board_cards, hand_ranks, river_count, reach_in, strategy, parent_node, pot_size, flop_weight
):
    seq_count = lax.axis_size("seq")
    seq_here = lax.axis_index("seq")
    board_count = lax.axis_size("board")
    rivers, local_leaves, hands = strategy.shape[1:]
    local_nodes = reach_in.shape[1]
    nodes, leaves = local_nodes * seq_count, local_leaves * seq_count
    rounds = -(-rivers // seq_count)
    padded = round_up(hands, LANES)
    anywhere = pl.BlockSpec(memory_space=pltpu.HBM)
    vmem = pl.BlockSpec(memory_space=pltpu.VMEM)
    params = pltpu.CompilerParams(vmem_limit_bytes=16 * MIB)

    def shift(array, step):
        return lax.ppermute(
            array, "seq", [(at, (at + step) % seq_count) for at in range(seq_count)]
        )

    def strategy_for(step):
        owner = (seq_here + step) % seq_count
        if rivers % seq_count == 0:
            split = strategy.reshape(rounds, seq_count, local_leaves, hands)
            rows = lax.dynamic_slice_in_dim(split, owner, 1, axis=1)
        else:
            picked = [
                lax.dynamic_slice_in_dim(
                    strategy[0], jnp.minimum(at * seq_count + owner, rivers - 1), 1, axis=0
                )
                for at in range(rounds)
            ]
            rows = jnp.concatenate(picked, axis=0)
        return rows.reshape(rounds * local_leaves, hands)

    own = strategy_for(0)
    last = rounds - 1
    sent = [strategy_for(step) for step in range(1, seq_count)]
    own, *sent = lax.optimization_barrier((own, *sent))
    came_head = [shift(rows[: last * local_leaves], step) for step, rows in enumerate(sent, 1)]

    small_rows = round_up(local_nodes + 4, 16)
    info_rows = round_up(2 * rounds + 4 + local_nodes, 8)
    small, info = pl.pallas_call(
        functools.partial(pack_kernel, rounds, seq_count),
        out_shape=[
            jax.ShapeDtypeStruct((small_rows, hands), jnp.bfloat16),
            jax.ShapeDtypeStruct((info_rows, padded), jnp.float32),
        ],
        in_specs=[anywhere] * 6,
        out_specs=[anywhere] * 2,
        scratch_shapes=[
            pltpu.VMEM(reach_in.shape, jnp.bfloat16),
            pltpu.VMEM((1, local_leaves), jnp.int32),
            pltpu.VMEM((1, local_leaves), jnp.float32),
            pltpu.VMEM((rivers, 1, hands), jnp.int32),
            pltpu.SMEM((board_cards.shape[2], 1, rivers), jnp.int32),
            pltpu.SMEM((1,), jnp.int32),
            pltpu.VMEM((small_rows, hands), jnp.bfloat16),
            pltpu.VMEM((info_rows, padded), jnp.float32),
            pltpu.SemaphoreType.DMA((6,)),
            pltpu.SemaphoreType.DMA((2,)),
        ],
        compiler_params=pltpu.CompilerParams(vmem_limit_bytes=60 * MIB),
        name="pack",
    )(
        reach_in,
        parent_node[None],
        pot_size[None],
        hand_ranks.transpose(1, 0, 2),
        board_cards.transpose(2, 0, 1),
        river_count,
    )
    smalls = [shift(small, step) for step in range(1, seq_count)]
    *sent, info = lax.optimization_barrier((*sent, info))
    came_tail = [shift(rows[last * local_leaves :], step) for step, rows in enumerate(sent, 1)]

    payoff, info = pl.pallas_call(
        functools.partial(build_kernel, rounds),
        out_shape=[
            jax.ShapeDtypeStruct((rounds, padded, padded), jnp.bfloat16),
            jax.ShapeDtypeStruct((info_rows, padded), jnp.float32),
        ],
        in_specs=[vmem],
        out_specs=[vmem] * 2,
        scratch_shapes=[
            pltpu.VMEM((round_up(DECK + 1, 16), padded), jnp.bfloat16),
            pltpu.VMEM((round_up(DECK + 1, 16), padded), jnp.bfloat16),
        ],
        compiler_params=pltpu.CompilerParams(vmem_limit_bytes=30 * MIB),
        cost_estimate=pl.CostEstimate(
            flops=10 * rounds * padded * padded, bytes_accessed=4 * padded * padded, transcendentals=0
        ),
        name="build",
    )(info)

    count = tile_count(local_nodes, hands)
    total, *labels = pl.pallas_call(
        functools.partial(head_kernel, rounds, seq_count, nodes, leaves),
        out_shape=[
            jax.ShapeDtypeStruct((nodes, padded), jnp.float32),
            jax.ShapeDtypeStruct((seq_count, leaves, LANES), jnp.bfloat16),
            jax.ShapeDtypeStruct((leaves, LANES), jnp.float32),
            jax.ShapeDtypeStruct((leaves, hands), jnp.float32),
        ],
        in_specs=[vmem] * (1 + 2 * seq_count),
        out_specs=[vmem] * 4,
        scratch_shapes=[pltpu.VMEM((max(last, 1), leaves, padded), jnp.bfloat16)],
        compiler_params=params,
        cost_estimate=pl.CostEstimate(
            flops=2 * rounds * leaves * padded * padded, bytes_accessed=2 * rounds * padded * padded, transcendentals=0
        ),
        name="head",
    )(payoff, info, own, *came_head, *smalls)
    shares = pl.pallas_call(
        functools.partial(tail_kernel, rounds, seq_count, nodes),
        out_shape=[jax.ShapeDtypeStruct((count, 8, LANES), jnp.float32)] * seq_count,
        in_specs=[vmem] * (6 + seq_count),
        out_specs=[vmem] * seq_count,
        scratch_shapes=[
            pltpu.VMEM((nodes, padded), jnp.float32),
            pltpu.VMEM((leaves, padded), jnp.bfloat16),
        ],
        compiler_params=params,
        name="tail",
    )(payoff, info, own, *came_tail, total, *labels)

    share = shares[0]
    for step in range(1, seq_count):
        share = share + shift(shares[step], -step)
    def swap(array, step):
        return lax.ppermute(array, "board", [(at, at ^ step) for at in range(board_count)])

    half = -(-count // 2)
    parity = lax.axis_index("board") % 2
    root = share * (flop_weight[0] / board_count)
    if count % 2:
        root = jnp.concatenate([root, jnp.zeros((1, 8, LANES), jnp.float32)], axis=0)
    root = root.reshape(2, half, 8, LANES)
    mine = lax.dynamic_index_in_dim(root, parity, 0, keepdims=False)
    mine = mine + swap(lax.dynamic_index_in_dim(root, 1 - parity, 0, keepdims=False), 1)
    step = 2
    while step < board_count:
        if step == 2 and board_count >= 8:
            near, far, across = [swap(mine, at) for at in (2, 4, 6)]
            mine = (mine + near) + (far + across)
            step *= 4
        else:
            mine = mine + swap(mine, step)
            step *= 2
    other = swap(mine, 1)

    turn_value = pl.pallas_call(
        functools.partial(share_kernel, local_nodes, hands),
        out_shape=jax.ShapeDtypeStruct((local_nodes, 1, hands), jnp.float32),
        in_specs=[vmem],
        out_specs=anywhere,
        scratch_shapes=[
            pltpu.VMEM((local_nodes, 1, hands), jnp.float32),
            pltpu.SemaphoreType.DMA,
        ],
        compiler_params=params,
        name="share",
    )(share)
    root_value = pl.pallas_call(
        functools.partial(root_kernel, local_nodes, hands),
        out_shape=jax.ShapeDtypeStruct((local_nodes, hands), jnp.float32),
        in_specs=[vmem] * 2,
        out_specs=anywhere,
        scratch_shapes=[pltpu.VMEM((local_nodes, hands), jnp.float32), pltpu.SemaphoreType.DMA],
        compiler_params=params,
        name="root",
    )(mine, other)
    return (turn_value.transpose(1, 0, 2), root_value)


def solution(mesh):
    return jax.shard_map(
        body,
        mesh=mesh,
        in_specs=(
            P("board", None, None),
            P("board", None, None),
            P("board"),
            P("board", "seq", None),
            P("board", None, "seq", None),
            P("seq"),
            P("seq"),
            P("board"),
        ),
        out_specs=(P("board", "seq", None), P("seq", None)),
        check_vma=False,
    )
```

```python
import functools

import jax
import jax.numpy as jnp
from jax import lax
from jax.experimental import pallas as pl
from jax.experimental.pallas import tpu as pltpu
from jax.sharding import PartitionSpec as P

DECK = 52
LANES = 128
MIB = 1024 * 1024


def round_up(value, step):
    return -(-value // step) * step


def hand_cards(padded):
    hand = lax.broadcasted_iota(jnp.int32, (1, padded), 1)
    low = jnp.zeros((1, padded), jnp.int32)
    start = jnp.zeros((1, padded), jnp.int32)
    first = 0
    for card in range(DECK - 1):
        if card:
            low = jnp.where(hand >= first, card, low)
            start = jnp.where(hand >= first, first, start)
        first += DECK - 1 - card
    high = hand - start + low + 1
    real = hand < first
    return jnp.where(real, low, -1), jnp.where(real, high, -1)


def pad_rows(rows):
    return 1 << max(rows - 1, 0).bit_length()


def tile_count(rows, hands):
    full, rest = divmod(rows, 8)
    whole, tail = divmod(hands, LANES)
    count = full * whole
    if rest:
        count += -(-whole // (8 // pad_rows(rest)))
    groups = full + (rest > 0)
    if tail:
        count += -(-groups // 2) if tail <= LANES // 2 else groups
    return count


def pack_tiles(value, rows, hands):
    full, rest = divmod(rows, 8)
    whole, tail = divmod(hands, LANES)
    tiles = [
        value[8 * group : 8 * group + 8, LANES * at : LANES * (at + 1)]
        for group in range(full)
        for at in range(whole)
    ]
    if rest:
        part = pad_rows(rest)
        each = 8 // part
        for start in range(0, whole, each):
            pieces = [
                value[8 * full : 8 * full + part, LANES * at : LANES * (at + 1)]
                for at in range(start, min(start + each, whole))
            ]
            if len(pieces) < each:
                pieces.append(jnp.zeros((8 - part * len(pieces), LANES), value.dtype))
            tiles.append(jnp.concatenate(pieces, axis=0) if len(pieces) > 1 else pieces[0])
    if tail:
        groups = full + (rest > 0)
        tails = [value[8 * group : 8 * group + 8, LANES * whole :] for group in range(groups)]
        if tail <= LANES // 2:
            for at in range(0, groups, 2):
                tile = tails[at]
                if at + 1 < groups:
                    tile = tile + pltpu.roll(tails[at + 1], LANES // 2, 1)
                tiles.append(tile)
        else:
            tiles.extend(tails)
    return tiles


def unpack_tiles(tiles, rows, hands):
    full, rest = divmod(rows, 8)
    whole, tail = divmod(hands, LANES)
    groups = [[tiles[group * whole + at] for at in range(whole)] for group in range(full)]
    used = full * whole
    if rest:
        part = pad_rows(rest)
        each = 8 // part
        last = []
        for at in range(whole):
            tile = tiles[used + at // each]
            begin = part * (at % each)
            last.append(pltpu.roll(tile, (8 - begin) % 8, 0) if begin else tile)
        used += -(-whole // each)
        groups.append(last)
    if tail:
        for at, group in enumerate(groups):
            if tail <= LANES // 2:
                tile = tiles[used + at // 2]
                if at % 2:
                    tile = pltpu.roll(tile, LANES // 2, 1)
            else:
                tile = tiles[used + at]
            group.append(tile[:, :tail])
    return [jnp.concatenate(group, axis=1) for group in groups]


def copy_all(pairs, sems):
    copies = [
        pltpu.make_async_copy(source, target, sems.at[at])
        for at, (source, target) in enumerate(pairs)
    ]
    for copy in copies:
        copy.start()
    return copies


def pack_kernel(
    rounds,
    seq_count,
    reach_ref,
    parent_ref,
    pot_ref,
    rank_ref,
    board_ref,
    count_ref,
    small_ref,
    info_ref,
    reach_tmp,
    parent_tmp,
    pot_tmp,
    rank_tmp,
    board_tmp,
    count_tmp,
    small,
    info,
    sems,
    out_sems,
):
    hands, padded = small.shape[-1], info.shape[-1]
    nodes, leaves = reach_tmp.shape[1], parent_tmp.shape[-1]
    rivers = rank_tmp.shape[0]
    here = lax.axis_index("seq")
    loads = copy_all(
        [
            (reach_ref, reach_tmp),
            (parent_ref, parent_tmp),
            (pot_ref, pot_tmp),
            (rank_ref, rank_tmp),
            (board_ref, board_tmp),
            (count_ref, count_tmp),
        ],
        sems,
    )
    low, high = hand_cards(padded)
    info[...] = jnp.zeros_like(info)
    for copy in loads[:3]:
        copy.wait()
    pot = pot_tmp[...]
    parent = parent_tmp[...].astype(jnp.float32)
    reach = reach_tmp[0].astype(jnp.float32)
    top = pot.astype(jnp.bfloat16).astype(jnp.float32)
    middle = (pot - top).astype(jnp.bfloat16).astype(jnp.float32)
    labels = jnp.concatenate([parent, top, middle, pot - top - middle], axis=0)
    rows = [reach, jnp.concatenate([labels, jnp.zeros((4, hands - leaves), jnp.float32)], axis=1)]
    extra = small.shape[0]
    if extra > nodes + 4:
        rows.append(jnp.zeros((extra - nodes - 4, hands), jnp.float32))
    small[...] = jnp.concatenate(rows, axis=0).astype(jnp.bfloat16)
    sent = pltpu.make_async_copy(small, small_ref, out_sems.at[0])
    sent.start()

    for copy in loads[3:]:
        copy.wait()
    live_count = count_tmp[0]
    base = 2 * rounds
    for at in range(rounds):
        river = jnp.minimum(at * seq_count + here, rivers - 1)
        info[at : at + 1, :hands] = rank_tmp[river].astype(jnp.float32)
        alive = jnp.where(at * seq_count + here < live_count, 1.0, 0.0)
        live = jnp.where(low >= 0, alive, 0.0)
        for slot in range(board_tmp.shape[0]):
            card = board_tmp[slot, 0, river]
            live = jnp.where((low == card) | (high == card), 0.0, live)
        info[rounds + at : rounds + at + 1, :] = live
    info[base : base + 1, :] = 1.0 / (hands * jnp.full((1, padded), live_count.astype(jnp.float32)))
    live_rounds = lax.div(live_count - here + seq_count - 1, seq_count)
    info[base + 3 + nodes : base + 4 + nodes, :] = jnp.full(
        (1, padded), live_rounds.astype(jnp.float32)
    )
    info[base + 4 + nodes : base + 5 + nodes, :] = low.astype(jnp.float32)
    info[base + 5 + nodes : base + 6 + nodes, :] = high.astype(jnp.float32)
    info[base + 1 : base + 2, :leaves] = parent
    info[base + 2 : base + 3, :leaves] = pot
    info[base + 3 : base + 3 + nodes, :hands] = reach
    kept = pltpu.make_async_copy(info, info_ref, out_sems.at[1])
    kept.start()
    sent.wait()
    kept.wait()


def build_kernel(rounds, nodes, info_ref, payoff_ref, kept_ref, holds, lacks):
    padded = payoff_ref.shape[-1]
    kept_ref[...] = info_ref[...]

    at = 2 * rounds + 4 + nodes
    low, high = info_ref[at : at + 1, :], info_ref[at + 1 : at + 2, :]
    card = lax.broadcasted_iota(jnp.int32, (holds.shape[0], padded), 0).astype(jnp.float32)
    held = jnp.where((card == low) | (card == high), 1.0, 0.0)
    holds[...] = jnp.where(card == DECK, 1.0, held).astype(jnp.bfloat16)
    lacks[...] = jnp.where(card == DECK, 1.0, -held).astype(jnp.bfloat16)
    def product(left, right):
        return lax.dot_general(
            left, right, (((0,), (0,)), ((), ())), preferred_element_type=jnp.float32
        ).astype(jnp.bfloat16)

    for start in range(0, padded, LANES):
        rows = slice(start, start + LANES)
        columns = [
            jnp.broadcast_to(info_ref[at : at + 1, rows], (LANES, LANES)).T
            for at in range(rounds)
        ]
        for lane in range(0, padded, 2 * LANES):
            here = slice(lane, min(lane + 2 * LANES, padded))
            mask = product(holds[:, rows], lacks[:, here])
            if here.start <= start < here.stop:
                mask = jnp.maximum(mask, 0.0)
            for at in range(rounds):
                pieces = [
                    (info_ref[at : at + 1, left : left + LANES] - columns[at]).astype(jnp.bfloat16)
                    for left in range(here.start, here.stop, LANES)
                ]
                gap = jnp.concatenate(pieces, axis=1)
                payoff_ref[at, rows, here] = jnp.maximum(jnp.minimum(gap, mask), -mask)


def head_kernel(rounds, seq_count, nodes, leaves, *refs):
    payoff_ref, info_ref, own_ref = refs[:3]
    came = refs[3 : 2 + seq_count]
    smalls = refs[2 + seq_count : 1 + 2 * seq_count]
    total, picks_ref, pot_ref, lookup_ref, reach_all = refs[1 + 2 * seq_count :]
    hands = own_ref.shape[-1]
    padded = payoff_ref.shape[-1]
    local_leaves, local_nodes = leaves // seq_count, nodes // seq_count
    here = lax.axis_index("seq")
    base = 2 * rounds

    reach, places, pots = [], [], []
    for at in range(seq_count):
        if at == 0:
            reach.append(info_ref[base + 3 : base + 3 + local_nodes, :hands])
            parent = info_ref[base + 1 : base + 2, :LANES]
            pots.append(info_ref[base + 2 : base + 3, :LANES])
        else:
            small = smalls[at - 1][...].astype(jnp.float32)
            reach.append(small[:local_nodes])
            labels = small[local_nodes : local_nodes + 4, :LANES]
            parent = labels[0:1]
            pots.append(labels[1:2] + labels[2:3] + labels[3:4])
        place = parent
        for owner in range(seq_count):
            inside = (parent >= owner * local_nodes) & (parent < (owner + 1) * local_nodes)
            move = (lax.rem(here - owner + seq_count, seq_count) - owner) * local_nodes
            place = jnp.where(inside, parent + move.astype(jnp.float32), place)
        lane = lax.broadcasted_iota(jnp.int32, (1, LANES), 1)
        places.append(jnp.where(lane < local_leaves, place, -1.0))

    sub = lax.broadcasted_iota(jnp.int32, (LANES, LANES), 0)
    lane = lax.broadcasted_iota(jnp.int32, (LANES, LANES), 1)
    columns = [jnp.broadcast_to(place, (LANES, LANES)).T for place in places]
    picks = []
    pot_sorted = jnp.zeros((leaves, 1), jnp.float32)
    target = lax.broadcasted_iota(jnp.int32, (leaves, LANES), 0).astype(jnp.float32)
    for at in range(seq_count):
        nth = jnp.sum(
            jnp.where((columns[at] == places[at]) & (sub < lane), 1.0, 0.0), axis=0, keepdims=True
        )
        for before in range(at):
            nth = nth + jnp.sum(
                jnp.where(columns[before] == places[at], 1.0, 0.0), axis=0, keepdims=True
            )
        slot = jnp.where(places[at] >= 0.0, nth * nodes + places[at], -1.0)
        pick = jnp.where(target == slot, 1.0, 0.0)
        pot_sorted = pot_sorted + jnp.sum(pick * pots[at], axis=1, keepdims=True)
        picks_ref[at] = pick.astype(jnp.bfloat16)
        picks.append(picks_ref[at, :, :local_leaves])
    lookup = jnp.concatenate(reach * (leaves // nodes), axis=0)
    lookup_ref[...] = lookup
    pot_ref[...] = jnp.broadcast_to(pot_sorted, pot_ref.shape)

    reach_all[...] = jnp.zeros_like(reach_all)
    live_rounds = jnp.max(info_ref[base + 3 + local_nodes : base + 4 + local_nodes, :LANES])

    def sum_rounds(number):
        gains = []
        for at in range(number):
            rows = slice(at * local_leaves, (at + 1) * local_leaves)
            live = info_ref[rounds + at : rounds + at + 1, :]
            strat = jnp.dot(picks[0], own_ref[rows, :], preferred_element_type=jnp.float32)
            for pick, pack in zip(picks[1:], came):
                strat = strat + jnp.dot(pick, pack[rows, :], preferred_element_type=jnp.float32)
            reach_all[at, :, :hands] = (lookup * strat * live[:, :hands]).astype(jnp.bfloat16)
        for at in range(number):
            live = info_ref[rounds + at : rounds + at + 1, :]
            shown = jnp.dot(reach_all[at], payoff_ref[at], preferred_element_type=jnp.float32)
            value = shown * pot_sorted
            best = value[:nodes]
            for row in range(nodes, leaves, nodes):
                best = jnp.maximum(best, value[row : row + nodes])
            gains.append(best * (live * info_ref[base : base + 1, :]))
        total[...] = sum(gains[1:], gains[0])

    total[...] = jnp.zeros_like(total)
    for number in range(1, rounds - 1):
        pl.when(live_rounds == number)(functools.partial(sum_rounds, number))
    if rounds > 1:
        pl.when(live_rounds >= rounds - 1)(functools.partial(sum_rounds, rounds - 1))


def tail_kernel(rounds, seq_count, nodes, *refs):
    payoff_ref, info_ref, own_ref = refs[:3]
    came = refs[3 : 2 + seq_count]
    before_ref, picks_ref, pot_ref, lookup_ref = refs[2 + seq_count : 6 + seq_count]
    outs, (total, reach_all) = refs[6 + seq_count : -2], refs[-2:]
    hands = own_ref.shape[-1]
    padded = payoff_ref.shape[-1]
    leaves = lookup_ref.shape[0]
    local_leaves, local_nodes = leaves // seq_count, nodes // seq_count
    base = 2 * rounds
    last = rounds - 1
    live_rounds = jnp.max(info_ref[base + 3 + local_nodes : base + 4 + local_nodes, :LANES])
    total[...] = before_ref[...]

    @pl.when(live_rounds > last)
    def _():
        reach_all[...] = jnp.zeros_like(reach_all)
        live = info_ref[rounds + last : rounds + last + 1, :]
        own = own_ref[last * local_leaves : rounds * local_leaves, :]
        strat = jnp.dot(picks_ref[0, :, :local_leaves], own, preferred_element_type=jnp.float32)
        for at, block in enumerate(came, 1):
            pick = picks_ref[at, :, :local_leaves]
            strat = strat + jnp.dot(pick, block[...], preferred_element_type=jnp.float32)
        reach_all[:, :hands] = (lookup_ref[...] * strat * live[:, :hands]).astype(jnp.bfloat16)
        shown = jnp.dot(reach_all[...], payoff_ref[last], preferred_element_type=jnp.float32)
        value = shown * pot_ref[:, :1]
        best = value[:nodes]
        for row in range(nodes, leaves, nodes):
            best = jnp.maximum(best, value[row : row + nodes])
        total[...] += best * (live * info_ref[base : base + 1, :])

    short = round_up(local_nodes, 8) - local_nodes
    for step in range(seq_count):
        rows = total[step * local_nodes : (step + 1) * local_nodes, :]
        if short:
            rows = jnp.concatenate([rows, jnp.zeros((short, padded), jnp.float32)], axis=0)
        for at, tile in enumerate(pack_tiles(rows, local_nodes, hands)):
            outs[step][at] = tile


def share_kernel(rows, hands, tiles_ref, out_ref, tmp, sem):
    tiles = [tiles_ref[at] for at in range(tile_count(rows, hands))]
    for at, group in enumerate(unpack_tiles(tiles, rows, hands)):
        for row in range(8 * at, min(8 * at + 8, rows)):
            tmp[row] = group[row - 8 * at : row - 8 * at + 1]
    copy = pltpu.make_async_copy(tmp, out_ref, sem)
    copy.start()
    copy.wait()


def root_kernel(rows, hands, mine_ref, other_ref, out_ref, tmp, sem):
    first = lax.rem(lax.axis_index("board"), 2) == 0
    lower = jnp.where(first, mine_ref[...], other_ref[...])
    upper = jnp.where(first, other_ref[...], mine_ref[...])
    half = mine_ref.shape[0]
    count = tile_count(rows, hands)
    tiles = [lower[at] for at in range(half)] + [upper[at] for at in range(count - half)]
    for at, group in enumerate(unpack_tiles(tiles, rows, hands)):
        height = min(8, rows - 8 * at)
        tmp[8 * at : 8 * at + height, :] = group[:height]
    copy = pltpu.make_async_copy(tmp, out_ref, sem)
    copy.start()
    copy.wait()


def body(
    board_cards, hand_ranks, river_count, reach_in, strategy, parent_node, pot_size, flop_weight
):
    seq_count = lax.axis_size("seq")
    seq_here = lax.axis_index("seq")
    board_count = lax.axis_size("board")
    rivers, local_leaves, hands = strategy.shape[1:]
    local_nodes = reach_in.shape[1]
    nodes, leaves = local_nodes * seq_count, local_leaves * seq_count
    rounds = -(-rivers // seq_count)
    padded = round_up(hands, LANES)
    anywhere = pl.BlockSpec(memory_space=pltpu.HBM)
    vmem = pl.BlockSpec(memory_space=pltpu.VMEM)
    params = pltpu.CompilerParams(vmem_limit_bytes=16 * MIB)

    def shift(array, step):
        return lax.ppermute(
            array, "seq", [(at, (at + step) % seq_count) for at in range(seq_count)]
        )

    def strategy_for(step):
        owner = (seq_here + step) % seq_count
        if rivers % seq_count == 0:
            split = strategy.reshape(rounds, seq_count, local_leaves, hands)
            rows = lax.dynamic_slice_in_dim(split, owner, 1, axis=1)
        else:
            picked = [
                lax.dynamic_slice_in_dim(
                    strategy[0], jnp.minimum(at * seq_count + owner, rivers - 1), 1, axis=0
                )
                for at in range(rounds)
            ]
            rows = jnp.concatenate(picked, axis=0)
        return rows.reshape(rounds * local_leaves, hands)

    own = strategy_for(0)
    last = rounds - 1
    sent = [strategy_for(step) for step in range(1, seq_count)]
    own, *sent = lax.optimization_barrier((own, *sent))
    came_head = [shift(rows[: last * local_leaves], step) for step, rows in enumerate(sent, 1)]

    small_rows = round_up(local_nodes + 4, 16)
    info_rows = round_up(2 * rounds + 6 + local_nodes, 8)
    small, info = pl.pallas_call(
        functools.partial(pack_kernel, rounds, seq_count),
        out_shape=[
            jax.ShapeDtypeStruct((small_rows, hands), jnp.bfloat16),
            jax.ShapeDtypeStruct((info_rows, padded), jnp.float32),
        ],
        in_specs=[anywhere] * 6,
        out_specs=[anywhere] * 2,
        scratch_shapes=[
            pltpu.VMEM(reach_in.shape, jnp.bfloat16),
            pltpu.VMEM((1, local_leaves), jnp.int32),
            pltpu.VMEM((1, local_leaves), jnp.float32),
            pltpu.VMEM((rivers, 1, hands), jnp.int32),
            pltpu.SMEM((board_cards.shape[2], 1, rivers), jnp.int32),
            pltpu.SMEM((1,), jnp.int32),
            pltpu.VMEM((small_rows, hands), jnp.bfloat16),
            pltpu.VMEM((info_rows, padded), jnp.float32),
            pltpu.SemaphoreType.DMA((6,)),
            pltpu.SemaphoreType.DMA((2,)),
        ],
        compiler_params=pltpu.CompilerParams(vmem_limit_bytes=60 * MIB),
        name="pack",
    )(
        reach_in,
        parent_node[None],
        pot_size[None],
        hand_ranks.transpose(1, 0, 2),
        board_cards.transpose(2, 0, 1),
        river_count,
    )
    smalls = [shift(small, step) for step in range(1, seq_count)]
    *sent, info = lax.optimization_barrier((*sent, info))
    came_tail = [shift(rows[last * local_leaves :], step) for step, rows in enumerate(sent, 1)]

    payoff, info = pl.pallas_call(
        functools.partial(build_kernel, rounds, local_nodes),
        out_shape=[
            jax.ShapeDtypeStruct((rounds, padded, padded), jnp.bfloat16),
            jax.ShapeDtypeStruct((info_rows, padded), jnp.float32),
        ],
        in_specs=[vmem],
        out_specs=[vmem] * 2,
        scratch_shapes=[
            pltpu.VMEM((round_up(DECK + 1, 16), padded), jnp.bfloat16),
            pltpu.VMEM((round_up(DECK + 1, 16), padded), jnp.bfloat16),
        ],
        compiler_params=pltpu.CompilerParams(vmem_limit_bytes=30 * MIB),
        cost_estimate=pl.CostEstimate(
            flops=10 * rounds * padded * padded, bytes_accessed=4 * padded * padded, transcendentals=0
        ),
        name="build",
    )(info)

    count = tile_count(local_nodes, hands)
    total, *labels = pl.pallas_call(
        functools.partial(head_kernel, rounds, seq_count, nodes, leaves),
        out_shape=[
            jax.ShapeDtypeStruct((nodes, padded), jnp.float32),
            jax.ShapeDtypeStruct((seq_count, leaves, LANES), jnp.bfloat16),
            jax.ShapeDtypeStruct((leaves, LANES), jnp.float32),
            jax.ShapeDtypeStruct((leaves, hands), jnp.float32),
        ],
        in_specs=[vmem] * (1 + 2 * seq_count),
        out_specs=[vmem] * 4,
        scratch_shapes=[pltpu.VMEM((max(last, 1), leaves, padded), jnp.bfloat16)],
        compiler_params=params,
        cost_estimate=pl.CostEstimate(
            flops=2 * rounds * leaves * padded * padded, bytes_accessed=2 * rounds * padded * padded, transcendentals=0
        ),
        name="head",
    )(payoff, info, own, *came_head, *smalls)
    shares = pl.pallas_call(
        functools.partial(tail_kernel, rounds, seq_count, nodes),
        out_shape=[jax.ShapeDtypeStruct((count, 8, LANES), jnp.float32)] * seq_count,
        in_specs=[vmem] * (6 + seq_count),
        out_specs=[vmem] * seq_count,
        scratch_shapes=[
            pltpu.VMEM((nodes, padded), jnp.float32),
            pltpu.VMEM((leaves, padded), jnp.bfloat16),
        ],
        compiler_params=params,
        name="tail",
    )(payoff, info, own, *came_tail, total, *labels)

    share = shares[0]
    for step in range(1, seq_count):
        share = share + shift(shares[step], -step)
    def swap(array, step):
        return lax.ppermute(array, "board", [(at, at ^ step) for at in range(board_count)])

    half = -(-count // 2)
    parity = lax.axis_index("board") % 2
    root = share * (flop_weight[0] / board_count)
    if count % 2:
        root = jnp.concatenate([root, jnp.zeros((1, 8, LANES), jnp.float32)], axis=0)
    root = root.reshape(2, half, 8, LANES)
    mine = lax.dynamic_index_in_dim(root, parity, 0, keepdims=False)
    mine = mine + swap(lax.dynamic_index_in_dim(root, 1 - parity, 0, keepdims=False), 1)
    step = 2
    while step < board_count:
        if step == 2 and board_count >= 8:
            near, far, across = [swap(mine, at) for at in (2, 4, 6)]
            mine = (mine + near) + (far + across)
            step *= 4
        else:
            mine = mine + swap(mine, step)
            step *= 2
    other = swap(mine, 1)

    turn_value = pl.pallas_call(
        functools.partial(share_kernel, local_nodes, hands),
        out_shape=jax.ShapeDtypeStruct((local_nodes, 1, hands), jnp.float32),
        in_specs=[vmem],
        out_specs=anywhere,
        scratch_shapes=[
            pltpu.VMEM((local_nodes, 1, hands), jnp.float32),
            pltpu.SemaphoreType.DMA,
        ],
        compiler_params=params,
        name="share",
    )(share)
    root_value = pl.pallas_call(
        functools.partial(root_kernel, local_nodes, hands),
        out_shape=jax.ShapeDtypeStruct((local_nodes, hands), jnp.float32),
        in_specs=[vmem] * 2,
        out_specs=anywhere,
        scratch_shapes=[pltpu.VMEM((local_nodes, hands), jnp.float32), pltpu.SemaphoreType.DMA],
        compiler_params=params,
        name="root",
    )(mine, other)
    return (turn_value.transpose(1, 0, 2), root_value)


def solution(mesh):
    return jax.shard_map(
        body,
        mesh=mesh,
        in_specs=(
            P("board", None, None),
            P("board", None, None),
            P("board"),
            P("board", "seq", None),
            P("board", None, "seq", None),
            P("seq"),
            P("seq"),
            P("board"),
        ),
        out_specs=(P("board", "seq", None), P("seq", None)),
        check_vma=False,
    )
```

```python
import functools

import jax
import jax.numpy as jnp
from jax import lax
from jax.experimental import pallas as pl
from jax.experimental.pallas import tpu as pltpu
from jax.sharding import PartitionSpec as P

DECK = 52
LANES = 128
MIB = 1024 * 1024


def round_up(value, step):
    return -(-value // step) * step


def hand_cards(padded):
    hand = lax.broadcasted_iota(jnp.int32, (1, padded), 1)
    low = jnp.zeros((1, padded), jnp.int32)
    start = jnp.zeros((1, padded), jnp.int32)
    first = 0
    for card in range(DECK - 1):
        if card:
            low = jnp.where(hand >= first, card, low)
            start = jnp.where(hand >= first, first, start)
        first += DECK - 1 - card
    high = hand - start + low + 1
    real = hand < first
    return jnp.where(real, low, -1), jnp.where(real, high, -1)


def pad_rows(rows):
    return 1 << max(rows - 1, 0).bit_length()


def tile_count(rows, hands):
    full, rest = divmod(rows, 8)
    whole, tail = divmod(hands, LANES)
    count = full * whole
    if rest:
        count += -(-whole // (8 // pad_rows(rest)))
    groups = full + (rest > 0)
    if tail:
        count += -(-groups // 2) if tail <= LANES // 2 else groups
    return count


def pack_tiles(value, rows, hands):
    full, rest = divmod(rows, 8)
    whole, tail = divmod(hands, LANES)
    tiles = [
        value[8 * group : 8 * group + 8, LANES * at : LANES * (at + 1)]
        for group in range(full)
        for at in range(whole)
    ]
    if rest:
        part = pad_rows(rest)
        each = 8 // part
        for start in range(0, whole, each):
            pieces = [
                value[8 * full : 8 * full + part, LANES * at : LANES * (at + 1)]
                for at in range(start, min(start + each, whole))
            ]
            if len(pieces) < each:
                pieces.append(jnp.zeros((8 - part * len(pieces), LANES), value.dtype))
            tiles.append(jnp.concatenate(pieces, axis=0) if len(pieces) > 1 else pieces[0])
    if tail:
        groups = full + (rest > 0)
        tails = [value[8 * group : 8 * group + 8, LANES * whole :] for group in range(groups)]
        if tail <= LANES // 2:
            for at in range(0, groups, 2):
                tile = tails[at]
                if at + 1 < groups:
                    tile = tile + pltpu.roll(tails[at + 1], LANES // 2, 1)
                tiles.append(tile)
        else:
            tiles.extend(tails)
    return tiles


def unpack_tiles(tiles, rows, hands):
    full, rest = divmod(rows, 8)
    whole, tail = divmod(hands, LANES)
    groups = [[tiles[group * whole + at] for at in range(whole)] for group in range(full)]
    used = full * whole
    if rest:
        part = pad_rows(rest)
        each = 8 // part
        last = []
        for at in range(whole):
            tile = tiles[used + at // each]
            begin = part * (at % each)
            last.append(pltpu.roll(tile, (8 - begin) % 8, 0) if begin else tile)
        used += -(-whole // each)
        groups.append(last)
    if tail:
        for at, group in enumerate(groups):
            if tail <= LANES // 2:
                tile = tiles[used + at // 2]
                if at % 2:
                    tile = pltpu.roll(tile, LANES // 2, 1)
            else:
                tile = tiles[used + at]
            group.append(tile[:, :tail])
    return [jnp.concatenate(group, axis=1) for group in groups]


def copy_all(pairs, sems):
    copies = [
        pltpu.make_async_copy(source, target, sems.at[at])
        for at, (source, target) in enumerate(pairs)
    ]
    for copy in copies:
        copy.start()
    return copies


def pack_kernel(
    rounds,
    seq_count,
    reach_ref,
    parent_ref,
    pot_ref,
    rank_ref,
    board_ref,
    count_ref,
    small_ref,
    info_ref,
    reach_tmp,
    parent_tmp,
    pot_tmp,
    rank_tmp,
    board_tmp,
    count_tmp,
    small,
    info,
    sems,
    out_sems,
):
    hands, padded = small.shape[-1], info.shape[-1]
    nodes, leaves = reach_tmp.shape[1], parent_tmp.shape[-1]
    rivers = rank_tmp.shape[0]
    here = lax.axis_index("seq")
    loads = copy_all(
        [
            (reach_ref, reach_tmp),
            (parent_ref, parent_tmp),
            (pot_ref, pot_tmp),
            (rank_ref, rank_tmp),
            (board_ref, board_tmp),
            (count_ref, count_tmp),
        ],
        sems,
    )
    low, high = hand_cards(padded)
    info[...] = jnp.zeros_like(info)
    for copy in loads[:3]:
        copy.wait()
    pot = pot_tmp[...]
    parent = parent_tmp[...].astype(jnp.float32)
    reach = reach_tmp[0].astype(jnp.float32)
    top = pot.astype(jnp.bfloat16).astype(jnp.float32)
    middle = (pot - top).astype(jnp.bfloat16).astype(jnp.float32)
    labels = jnp.concatenate([parent, top, middle, pot - top - middle], axis=0)
    rows = [reach, jnp.concatenate([labels, jnp.zeros((4, hands - leaves), jnp.float32)], axis=1)]
    extra = small.shape[0]
    if extra > nodes + 4:
        rows.append(jnp.zeros((extra - nodes - 4, hands), jnp.float32))
    small[...] = jnp.concatenate(rows, axis=0).astype(jnp.bfloat16)
    sent = pltpu.make_async_copy(small, small_ref, out_sems.at[0])
    sent.start()

    for copy in loads[3:]:
        copy.wait()
    live_count = count_tmp[0]
    base = 2 * rounds
    for at in range(rounds):
        river = jnp.minimum(at * seq_count + here, rivers - 1)
        info[at : at + 1, :hands] = rank_tmp[river].astype(jnp.float32)
        alive = jnp.where(at * seq_count + here < live_count, 1.0, 0.0)
        live = jnp.where(low >= 0, alive, 0.0)
        for slot in range(board_tmp.shape[0]):
            card = board_tmp[slot, 0, river]
            live = jnp.where((low == card) | (high == card), 0.0, live)
        info[rounds + at : rounds + at + 1, :] = live
    info[base : base + 1, :] = 1.0 / (hands * jnp.full((1, padded), live_count.astype(jnp.float32)))
    live_rounds = lax.div(live_count - here + seq_count - 1, seq_count)
    info[base + 3 + nodes : base + 4 + nodes, :] = jnp.full(
        (1, padded), live_rounds.astype(jnp.float32)
    )
    info[base + 4 + nodes : base + 5 + nodes, :] = low.astype(jnp.float32)
    info[base + 5 + nodes : base + 6 + nodes, :] = high.astype(jnp.float32)
    info[base + 1 : base + 2, :leaves] = parent
    info[base + 2 : base + 3, :leaves] = pot
    info[base + 3 : base + 3 + nodes, :hands] = reach
    kept = pltpu.make_async_copy(info, info_ref, out_sems.at[1])
    kept.start()
    sent.wait()
    kept.wait()


def build_kernel(rounds, nodes, info_ref, payoff_ref, kept_ref, holds, lacks):
    padded = payoff_ref.shape[-1]
    kept_ref[...] = info_ref[...]

    at = 2 * rounds + 4 + nodes
    low, high = info_ref[at : at + 1, :], info_ref[at + 1 : at + 2, :]
    card = lax.broadcasted_iota(jnp.int32, (holds.shape[0], padded), 0).astype(jnp.float32)
    held = jnp.where((card == low) | (card == high), 1.0, 0.0)
    holds[...] = jnp.where(card == DECK, 1.0, held).astype(jnp.bfloat16)
    lacks[...] = jnp.where(card == DECK, 1.0, -held).astype(jnp.bfloat16)
    def product(left, right):
        return lax.dot_general(
            left, right, (((0,), (0,)), ((), ())), preferred_element_type=jnp.float32
        ).astype(jnp.bfloat16)

    def build_rounds(number):
        for start in range(0, padded, LANES):
            rows = slice(start, start + LANES)
            columns = [
                jnp.broadcast_to(info_ref[at : at + 1, rows], (LANES, LANES)).T
                for at in range(number)
            ]
            for lane in range(0, padded, 2 * LANES):
                here = slice(lane, min(lane + 2 * LANES, padded))
                mask = product(holds[:, rows], lacks[:, here])
                if here.start <= start < here.stop:
                    mask = jnp.maximum(mask, 0.0)
                for at in range(number):
                    pieces = [
                        (info_ref[at : at + 1, left : left + LANES] - columns[at]).astype(jnp.bfloat16)
                        for left in range(here.start, here.stop, LANES)
                    ]
                    gap = jnp.concatenate(pieces, axis=1)
                    payoff_ref[at, rows, here] = jnp.maximum(jnp.minimum(gap, mask), -mask)

    live_rounds = jnp.max(info_ref[2 * rounds + 3 + nodes : 2 * rounds + 4 + nodes, :LANES])
    for number in range(1, rounds + 1):
        pl.when(live_rounds == number)(functools.partial(build_rounds, number))


def head_kernel(rounds, seq_count, nodes, leaves, *refs):
    payoff_ref, info_ref, own_ref = refs[:3]
    came = refs[3 : 2 + seq_count]
    smalls = refs[2 + seq_count : 1 + 2 * seq_count]
    total, picks_ref, pot_ref, lookup_ref, reach_all = refs[1 + 2 * seq_count :]
    hands = own_ref.shape[-1]
    padded = payoff_ref.shape[-1]
    local_leaves, local_nodes = leaves // seq_count, nodes // seq_count
    here = lax.axis_index("seq")
    base = 2 * rounds

    reach, places, pots = [], [], []
    for at in range(seq_count):
        if at == 0:
            reach.append(info_ref[base + 3 : base + 3 + local_nodes, :hands])
            parent = info_ref[base + 1 : base + 2, :LANES]
            pots.append(info_ref[base + 2 : base + 3, :LANES])
        else:
            small = smalls[at - 1][...].astype(jnp.float32)
            reach.append(small[:local_nodes])
            labels = small[local_nodes : local_nodes + 4, :LANES]
            parent = labels[0:1]
            pots.append(labels[1:2] + labels[2:3] + labels[3:4])
        place = parent
        for owner in range(seq_count):
            inside = (parent >= owner * local_nodes) & (parent < (owner + 1) * local_nodes)
            move = (lax.rem(here - owner + seq_count, seq_count) - owner) * local_nodes
            place = jnp.where(inside, parent + move.astype(jnp.float32), place)
        lane = lax.broadcasted_iota(jnp.int32, (1, LANES), 1)
        places.append(jnp.where(lane < local_leaves, place, -1.0))

    sub = lax.broadcasted_iota(jnp.int32, (LANES, LANES), 0)
    lane = lax.broadcasted_iota(jnp.int32, (LANES, LANES), 1)
    columns = [jnp.broadcast_to(place, (LANES, LANES)).T for place in places]
    picks = []
    pot_sorted = jnp.zeros((leaves, 1), jnp.float32)
    target = lax.broadcasted_iota(jnp.int32, (leaves, LANES), 0).astype(jnp.float32)
    for at in range(seq_count):
        nth = jnp.sum(
            jnp.where((columns[at] == places[at]) & (sub < lane), 1.0, 0.0), axis=0, keepdims=True
        )
        for before in range(at):
            nth = nth + jnp.sum(
                jnp.where(columns[before] == places[at], 1.0, 0.0), axis=0, keepdims=True
            )
        slot = jnp.where(places[at] >= 0.0, nth * nodes + places[at], -1.0)
        pick = jnp.where(target == slot, 1.0, 0.0)
        pot_sorted = pot_sorted + jnp.sum(pick * pots[at], axis=1, keepdims=True)
        picks_ref[at] = pick.astype(jnp.bfloat16)
        picks.append(picks_ref[at, :, :local_leaves])
    lookup = jnp.concatenate(reach * (leaves // nodes), axis=0)
    lookup_ref[...] = lookup
    pot_ref[...] = jnp.broadcast_to(pot_sorted, pot_ref.shape)

    reach_all[...] = jnp.zeros_like(reach_all)
    live_rounds = jnp.max(info_ref[base + 3 + local_nodes : base + 4 + local_nodes, :LANES])

    def sum_rounds(number):
        gains = []
        for at in range(number):
            rows = slice(at * local_leaves, (at + 1) * local_leaves)
            live = info_ref[rounds + at : rounds + at + 1, :]
            strat = jnp.dot(picks[0], own_ref[rows, :], preferred_element_type=jnp.float32)
            for pick, pack in zip(picks[1:], came):
                strat = strat + jnp.dot(pick, pack[rows, :], preferred_element_type=jnp.float32)
            reach_all[at, :, :hands] = (lookup * strat * live[:, :hands]).astype(jnp.bfloat16)
        for at in range(number):
            live = info_ref[rounds + at : rounds + at + 1, :]
            shown = jnp.dot(reach_all[at], payoff_ref[at], preferred_element_type=jnp.float32)
            value = shown * pot_sorted
            best = value[:nodes]
            for row in range(nodes, leaves, nodes):
                best = jnp.maximum(best, value[row : row + nodes])
            gains.append(best * (live * info_ref[base : base + 1, :]))
        total[...] = sum(gains[1:], gains[0])

    total[...] = jnp.zeros_like(total)
    for number in range(1, rounds - 1):
        pl.when(live_rounds == number)(functools.partial(sum_rounds, number))
    if rounds > 1:
        pl.when(live_rounds >= rounds - 1)(functools.partial(sum_rounds, rounds - 1))


def tail_kernel(rounds, seq_count, nodes, *refs):
    payoff_ref, info_ref, own_ref = refs[:3]
    came = refs[3 : 2 + seq_count]
    before_ref, picks_ref, pot_ref, lookup_ref = refs[2 + seq_count : 6 + seq_count]
    outs, (total, reach_all) = refs[6 + seq_count : -2], refs[-2:]
    hands = own_ref.shape[-1]
    padded = payoff_ref.shape[-1]
    leaves = lookup_ref.shape[0]
    local_leaves, local_nodes = leaves // seq_count, nodes // seq_count
    base = 2 * rounds
    last = rounds - 1
    live_rounds = jnp.max(info_ref[base + 3 + local_nodes : base + 4 + local_nodes, :LANES])
    total[...] = before_ref[...]

    @pl.when(live_rounds > last)
    def _():
        reach_all[...] = jnp.zeros_like(reach_all)
        live = info_ref[rounds + last : rounds + last + 1, :]
        own = own_ref[last * local_leaves : rounds * local_leaves, :]
        strat = jnp.dot(picks_ref[0, :, :local_leaves], own, preferred_element_type=jnp.float32)
        for at, block in enumerate(came, 1):
            pick = picks_ref[at, :, :local_leaves]
            strat = strat + jnp.dot(pick, block[...], preferred_element_type=jnp.float32)
        reach_all[:, :hands] = (lookup_ref[...] * strat * live[:, :hands]).astype(jnp.bfloat16)
        shown = jnp.dot(reach_all[...], payoff_ref[last], preferred_element_type=jnp.float32)
        value = shown * pot_ref[:, :1]
        best = value[:nodes]
        for row in range(nodes, leaves, nodes):
            best = jnp.maximum(best, value[row : row + nodes])
        total[...] += best * (live * info_ref[base : base + 1, :])

    short = round_up(local_nodes, 8) - local_nodes
    for step in range(seq_count):
        rows = total[step * local_nodes : (step + 1) * local_nodes, :]
        if short:
            rows = jnp.concatenate([rows, jnp.zeros((short, padded), jnp.float32)], axis=0)
        for at, tile in enumerate(pack_tiles(rows, local_nodes, hands)):
            outs[step][at] = tile


def share_kernel(rows, hands, tiles_ref, out_ref, tmp, sem):
    tiles = [tiles_ref[at] for at in range(tile_count(rows, hands))]
    for at, group in enumerate(unpack_tiles(tiles, rows, hands)):
        for row in range(8 * at, min(8 * at + 8, rows)):
            tmp[row] = group[row - 8 * at : row - 8 * at + 1]
    copy = pltpu.make_async_copy(tmp, out_ref, sem)
    copy.start()
    copy.wait()


def root_kernel(rows, hands, mine_ref, other_ref, out_ref, tmp, sem):
    first = lax.rem(lax.axis_index("board"), 2) == 0
    lower = jnp.where(first, mine_ref[...], other_ref[...])
    upper = jnp.where(first, other_ref[...], mine_ref[...])
    half = mine_ref.shape[0]
    count = tile_count(rows, hands)
    tiles = [lower[at] for at in range(half)] + [upper[at] for at in range(count - half)]
    for at, group in enumerate(unpack_tiles(tiles, rows, hands)):
        height = min(8, rows - 8 * at)
        tmp[8 * at : 8 * at + height, :] = group[:height]
    copy = pltpu.make_async_copy(tmp, out_ref, sem)
    copy.start()
    copy.wait()


def body(
    board_cards, hand_ranks, river_count, reach_in, strategy, parent_node, pot_size, flop_weight
):
    seq_count = lax.axis_size("seq")
    seq_here = lax.axis_index("seq")
    board_count = lax.axis_size("board")
    rivers, local_leaves, hands = strategy.shape[1:]
    local_nodes = reach_in.shape[1]
    nodes, leaves = local_nodes * seq_count, local_leaves * seq_count
    rounds = -(-rivers // seq_count)
    padded = round_up(hands, LANES)
    anywhere = pl.BlockSpec(memory_space=pltpu.HBM)
    vmem = pl.BlockSpec(memory_space=pltpu.VMEM)
    params = pltpu.CompilerParams(vmem_limit_bytes=16 * MIB)

    def shift(array, step):
        return lax.ppermute(
            array, "seq", [(at, (at + step) % seq_count) for at in range(seq_count)]
        )

    def strategy_for(step):
        owner = (seq_here + step) % seq_count
        if rivers % seq_count == 0:
            split = strategy.reshape(rounds, seq_count, local_leaves, hands)
            rows = lax.dynamic_slice_in_dim(split, owner, 1, axis=1)
        else:
            picked = [
                lax.dynamic_slice_in_dim(
                    strategy[0], jnp.minimum(at * seq_count + owner, rivers - 1), 1, axis=0
                )
                for at in range(rounds)
            ]
            rows = jnp.concatenate(picked, axis=0)
        return rows.reshape(rounds * local_leaves, hands)

    own = strategy_for(0)
    last = rounds - 1
    sent = [strategy_for(step) for step in range(1, seq_count)]
    own, *sent = lax.optimization_barrier((own, *sent))
    came_head = [shift(rows[: last * local_leaves], step) for step, rows in enumerate(sent, 1)]

    small_rows = round_up(local_nodes + 4, 16)
    info_rows = round_up(2 * rounds + 6 + local_nodes, 8)
    small, info = pl.pallas_call(
        functools.partial(pack_kernel, rounds, seq_count),
        out_shape=[
            jax.ShapeDtypeStruct((small_rows, hands), jnp.bfloat16),
            jax.ShapeDtypeStruct((info_rows, padded), jnp.float32),
        ],
        in_specs=[anywhere] * 6,
        out_specs=[anywhere] * 2,
        scratch_shapes=[
            pltpu.VMEM(reach_in.shape, jnp.bfloat16),
            pltpu.VMEM((1, local_leaves), jnp.int32),
            pltpu.VMEM((1, local_leaves), jnp.float32),
            pltpu.VMEM((rivers, 1, hands), jnp.int32),
            pltpu.SMEM((board_cards.shape[2], 1, rivers), jnp.int32),
            pltpu.SMEM((1,), jnp.int32),
            pltpu.VMEM((small_rows, hands), jnp.bfloat16),
            pltpu.VMEM((info_rows, padded), jnp.float32),
            pltpu.SemaphoreType.DMA((6,)),
            pltpu.SemaphoreType.DMA((2,)),
        ],
        compiler_params=pltpu.CompilerParams(vmem_limit_bytes=60 * MIB),
        name="pack",
    )(
        reach_in,
        parent_node[None],
        pot_size[None],
        hand_ranks.transpose(1, 0, 2),
        board_cards.transpose(2, 0, 1),
        river_count,
    )
    smalls = [shift(small, step) for step in range(1, seq_count)]
    *sent, info = lax.optimization_barrier((*sent, info))
    came_tail = [shift(rows[last * local_leaves :], step) for step, rows in enumerate(sent, 1)]

    payoff, info = pl.pallas_call(
        functools.partial(build_kernel, rounds, local_nodes),
        out_shape=[
            jax.ShapeDtypeStruct((rounds, padded, padded), jnp.bfloat16),
            jax.ShapeDtypeStruct((info_rows, padded), jnp.float32),
        ],
        in_specs=[vmem],
        out_specs=[vmem] * 2,
        scratch_shapes=[
            pltpu.VMEM((round_up(DECK + 1, 16), padded), jnp.bfloat16),
            pltpu.VMEM((round_up(DECK + 1, 16), padded), jnp.bfloat16),
        ],
        compiler_params=pltpu.CompilerParams(vmem_limit_bytes=30 * MIB),
        cost_estimate=pl.CostEstimate(
            flops=10 * rounds * padded * padded, bytes_accessed=4 * padded * padded, transcendentals=0
        ),
        name="build",
    )(info)

    count = tile_count(local_nodes, hands)
    total, *labels = pl.pallas_call(
        functools.partial(head_kernel, rounds, seq_count, nodes, leaves),
        out_shape=[
            jax.ShapeDtypeStruct((nodes, padded), jnp.float32),
            jax.ShapeDtypeStruct((seq_count, leaves, LANES), jnp.bfloat16),
            jax.ShapeDtypeStruct((leaves, LANES), jnp.float32),
            jax.ShapeDtypeStruct((leaves, hands), jnp.float32),
        ],
        in_specs=[vmem] * (1 + 2 * seq_count),
        out_specs=[vmem] * 4,
        scratch_shapes=[pltpu.VMEM((max(last, 1), leaves, padded), jnp.bfloat16)],
        compiler_params=params,
        cost_estimate=pl.CostEstimate(
            flops=2 * rounds * leaves * padded * padded, bytes_accessed=2 * rounds * padded * padded, transcendentals=0
        ),
        name="head",
    )(payoff, info, own, *came_head, *smalls)
    shares = pl.pallas_call(
        functools.partial(tail_kernel, rounds, seq_count, nodes),
        out_shape=[jax.ShapeDtypeStruct((count, 8, LANES), jnp.float32)] * seq_count,
        in_specs=[vmem] * (6 + seq_count),
        out_specs=[vmem] * seq_count,
        scratch_shapes=[
            pltpu.VMEM((nodes, padded), jnp.float32),
            pltpu.VMEM((leaves, padded), jnp.bfloat16),
        ],
        compiler_params=params,
        name="tail",
    )(payoff, info, own, *came_tail, total, *labels)

    share = shares[0]
    for step in range(1, seq_count):
        share = share + shift(shares[step], -step)
    def swap(array, step):
        return lax.ppermute(array, "board", [(at, at ^ step) for at in range(board_count)])

    half = -(-count // 2)
    parity = lax.axis_index("board") % 2
    root = share * (flop_weight[0] / board_count)
    if count % 2:
        root = jnp.concatenate([root, jnp.zeros((1, 8, LANES), jnp.float32)], axis=0)
    root = root.reshape(2, half, 8, LANES)
    mine = lax.dynamic_index_in_dim(root, parity, 0, keepdims=False)
    mine = mine + swap(lax.dynamic_index_in_dim(root, 1 - parity, 0, keepdims=False), 1)
    step = 2
    while step < board_count:
        if step == 2 and board_count >= 8:
            near, far, across = [swap(mine, at) for at in (2, 4, 6)]
            mine = (mine + near) + (far + across)
            step *= 4
        else:
            mine = mine + swap(mine, step)
            step *= 2
    other = swap(mine, 1)

    turn_value = pl.pallas_call(
        functools.partial(share_kernel, local_nodes, hands),
        out_shape=jax.ShapeDtypeStruct((local_nodes, 1, hands), jnp.float32),
        in_specs=[vmem],
        out_specs=anywhere,
        scratch_shapes=[
            pltpu.VMEM((local_nodes, 1, hands), jnp.float32),
            pltpu.SemaphoreType.DMA,
        ],
        compiler_params=params,
        name="share",
    )(share)
    root_value = pl.pallas_call(
        functools.partial(root_kernel, local_nodes, hands),
        out_shape=jax.ShapeDtypeStruct((local_nodes, hands), jnp.float32),
        in_specs=[vmem] * 2,
        out_specs=anywhere,
        scratch_shapes=[pltpu.VMEM((local_nodes, hands), jnp.float32), pltpu.SemaphoreType.DMA],
        compiler_params=params,
        name="root",
    )(mine, other)
    return (turn_value.transpose(1, 0, 2), root_value)


def solution(mesh):
    return jax.shard_map(
        body,
        mesh=mesh,
        in_specs=(
            P("board", None, None),
            P("board", None, None),
            P("board"),
            P("board", "seq", None),
            P("board", None, "seq", None),
            P("seq"),
            P("seq"),
            P("board"),
        ),
        out_specs=(P("board", "seq", None), P("seq", None)),
        check_vma=False,
    )
```
